32 devices in a mesh: tok: 8 (over y, x, core), bkt: 4 (over z).
Axes of the slice: x: 2, y: 2, z: 4, core: 2. Of those that a mesh axis runs over, the one named last changes fastest.
Arguments:
- block_in: bfloat16 [8192, 2048], P(('tok', 'bkt')), may hold values from -6 to 6
- cotangent: float32 [8192, 2048], P(('tok', 'bkt')), may hold values from -8 to 8
- buckets: int32 [8], P('tok'), may hold values from 0 to 3, as said below
- qkv_weight: float32 [3, 2048, 2048], P(None, 'tok', 'bkt'), may hold values from -0.125 to 0.125
- qkv_first: float32 [3, 2048, 2048], P(None, 'tok', 'bkt'), may hold values from -0.00024414062 to 0.00024414062
- qkv_second: float32 [3, 2048, 2048], P(None, 'tok', 'bkt'), may hold values from 1.0449831e-09 to 4.1719854e-09
- out_weight: float32 [2048, 2048], P('bkt', 'tok'), may hold values from -0.5 to 0.5
- out_first: float32 [2048, 2048], P('bkt', 'tok'), may hold values from -0.00024414062 to 0.00024414062
- out_second: float32 [2048, 2048], P('bkt', 'tok'), may hold values from 1.0449831e-09 to 4.1719854e-09
- up_weight: float32 [2048, 8192], P('tok', 'bkt'), may hold values from -0.125 to 0.125
- up_first: float32 [2048, 8192], P('tok', 'bkt'), may hold values from -0.00024414062 to 0.00024414062
- up_second: float32 [2048, 8192], P('tok', 'bkt'), may hold values from 1.0449831e-09 to 4.1719854e-09
- down_weight: float32 [8192, 2048], P('bkt', 'tok'), may hold values from -0.0625 to 0.0625
- down_first: float32 [8192, 2048], P('bkt', 'tok'), may hold values from -0.00024414062 to 0.00024414062
- down_second: float32 [8192, 2048], P('bkt', 'tok'), may hold values from 1.0449831e-09 to 4.1719854e-09
- norm_gains: float32 [2, 2048], P(None, 'tok'), may hold values from 0.25 to 1.75
- gains_first: float32 [2, 2048], P(None, 'tok'), may hold values from -0.0007324219 to 0.0007324219
- gains_second: float32 [2, 2048], P(None, 'tok'), may hold values from 9.337301e-09 to 3.7746535e-08
Outputs:
- block_out: float32 [8192, 2048], P(('tok', 'bkt'))
- block_in_grad: float32 [8192, 2048], P(('tok', 'bkt'))
- grad_norm: float32 [], replicated
- qkv_new: float32 [3, 2048, 2048], P(None, 'tok', 'bkt')
- qkv_copy: bfloat16 [3, 2048, 2048], P(None, 'tok', 'bkt')
- qkv_first_new: float32 [3, 2048, 2048], P(None, 'tok', 'bkt')
- qkv_second_new: float32 [3, 2048, 2048], P(None, 'tok', 'bkt')
- out_new: float32 [2048, 2048], P('bkt', 'tok')
- out_copy: bfloat16 [2048, 2048], P('bkt', 'tok')
- out_first_new: float32 [2048, 2048], P('bkt', 'tok')
- out_second_new: float32 [2048, 2048], P('bkt', 'tok')
- up_new: float32 [2048, 8192], P('tok', 'bkt')
- up_copy: bfloat16 [2048, 8192], P('tok', 'bkt')
- up_first_new: float32 [2048, 8192], P('tok', 'bkt')
- up_second_new: float32 [2048, 8192], P('tok', 'bkt')
- down_new: float32 [8192, 2048], P('bkt', 'tok')
- down_copy: bfloat16 [8192, 2048], P('bkt', 'tok')
- down_first_new: float32 [8192, 2048], P('bkt', 'tok')
- down_second_new: float32 [8192, 2048], P('bkt', 'tok')
- gains_new: float32 [2, 2048], P(None, 'tok')
- gains_copy: bfloat16 [2, 2048], P(None, 'tok')
- gains_first_new: float32 [2, 2048], P(None, 'tok')
- gains_second_new: float32 [2, 2048], P(None, 'tok')
The draws below stay inside these ranges and needn't reach their ends.
Inputs may be any that keep to these rules, and one draw needn't show every extreme that they name: `buckets`: each of the 4 widths is chosen by exactly 2 sequences.
All inputs are finite; a program needn't handle non-finite values.
Results may differ from the reference program's by a relative error of at most 0.019.
Values may be sent and summed in bfloat16 or wider, within the bound.
No kernel may reach another device: no remote copies, remote signals or barrier semaphores. Data moves between devices by JAX's collectives and lax.ppermute only.
A program may use at most 192 MiB of HBM per device.

```python
import math
import jax
import jax.numpy as jnp
from jax import lax

D = 2048
H = 16
HD = 128
FF = 8192
LEN = 1024
BUCKETS = 4
STEP = 10
SEQS = 8
TOKENS = 8192
PARAMS = 50335744


def draw_buckets(key, part):
    key = jax.random.fold_in(key, 11)
    order = jax.random.permutation(key, SEQS)
    return (order % BUCKETS).astype(jnp.int32)


def draw_cotangent(key, part):
    key = jax.random.fold_in(key, 12)
    columns = jnp.arange(D).astype(jnp.float32) / D
    ramp = 0.6 + 1.2 * columns
    noise = jnp.clip(jax.random.normal(key, (TOKENS, D), jnp.float32), -4.0, 4.0)
    return noise * ramp[None, :]


def draw_norm_gains(key, part):
    key = jax.random.fold_in(key, 13)
    columns = jnp.arange(D).astype(jnp.float32) / D
    wobble = jax.random.uniform(key, (2, D), jnp.float32, 0.85, 1.15)
    ramp = 0.5 + columns
    return ramp[None, :] * wobble


def block_scale(own_key, shape, cuts, smallest, top_value):
    level, own = 1.0, jax.random.fold_in(own_key, 6)
    for position, blocks in cuts:
        draws = jnp.exp(jax.random.uniform(jax.random.fold_in(own, position), (blocks,), jnp.float32, smallest / len(cuts), top_value / len(cuts)))
        level = level * jnp.repeat(draws, shape[position] // blocks).reshape([-1 if axis == position else 1 for axis in range(len(shape))])
    return level


def scatter_about(own_key, dims, width, bound, pieces=(), held_as=jnp.bfloat16):
    drawn = jax.random.normal(own_key, dims, jnp.float32) * width
    if len(pieces) > 0:
        drawn = block_scale(own_key, dims, pieces, -0.22, 0.18) * drawn
    return jnp.clip(drawn, min=-bound, max=bound).astype(held_as)


def setup_inputs(seed: int = 0) -> dict:
    arg_keys = jax.random.split(jax.random.key(seed), 19)
    block_in = scatter_about(arg_keys[0], (TOKENS, D), 1.0, 6.0, ((0, 32),))
    cotangent = draw_cotangent(jax.random.fold_in(arg_keys[18], 71), 0)
    buckets = draw_buckets(jax.random.fold_in(arg_keys[18], 71), 0)
    qkv_weight = scatter_about(arg_keys[3], (3, D, H * HD), D ** -0.5, 0.125, ((1, 8), (2, 4)), jnp.float32)
    qkv_first = scatter_about(arg_keys[4], (3, D, H * HD), (0.111 * PARAMS ** -0.5), 0.00024414062, ((1, 8), (2, 4)), jnp.float32)
    qkv_second = jnp.clip(jnp.exp(math.log(4.171985423795377e-09) - 1.3843913 * jax.random.uniform(arg_keys[5], (3, D, H * HD), jnp.float32) ** block_scale(arg_keys[5], (3, D, H * HD), ((1, 8), (2, 4)), -0.2, 0.2)), 1.044983100051411e-09, 4.171985423795377e-09)
    out_weight = scatter_about(arg_keys[6], (H * HD, D), (H * HD // 16) ** -0.5, 0.5, ((0, 4), (1, 8)), jnp.float32)
    out_first = scatter_about(arg_keys[7], (H * HD, D), (0.111 * PARAMS ** -0.5), 0.00024414062, ((0, 4), (1, 8)), jnp.float32)
    out_second = jnp.clip(jnp.exp(math.log(4.171985423795377e-09) - 1.3843913 * jax.random.uniform(arg_keys[8], (H * HD, D), jnp.float32) ** block_scale(arg_keys[8], (H * HD, D), ((0, 4), (1, 8)), -0.2, 0.2)), 1.044983100051411e-09, 4.171985423795377e-09)
    up_weight = scatter_about(arg_keys[9], (D, FF), D ** -0.5, 0.125, ((0, 8), (1, 4)), jnp.float32)
    up_first = scatter_about(arg_keys[10], (D, FF), (0.111 * PARAMS ** -0.5), 0.00024414062, ((0, 8), (1, 4)), jnp.float32)
    up_second = jnp.clip(jnp.exp(math.log(4.171985423795377e-09) - 1.3843913 * jax.random.uniform(arg_keys[11], (D, FF), jnp.float32) ** block_scale(arg_keys[11], (D, FF), ((0, 8), (1, 4)), -0.2, 0.2)), 1.044983100051411e-09, 4.171985423795377e-09)
    down_weight = scatter_about(arg_keys[12], (FF, D), FF ** -0.5, 0.0625, ((0, 4), (1, 8)), jnp.float32)
    down_first = scatter_about(arg_keys[13], (FF, D), (0.111 * PARAMS ** -0.5), 0.00024414062, ((0, 4), (1, 8)), jnp.float32)
    down_second = jnp.clip(jnp.exp(math.log(4.171985423795377e-09) - 1.3843913 * jax.random.uniform(arg_keys[14], (FF, D), jnp.float32) ** block_scale(arg_keys[14], (FF, D), ((0, 4), (1, 8)), -0.2, 0.2)), 1.044983100051411e-09, 4.171985423795377e-09)
    norm_gains = draw_norm_gains(jax.random.fold_in(arg_keys[18], 71), 0)
    gains_first = scatter_about(arg_keys[16], (2, D), (0.333 * PARAMS ** -0.5), 0.0007324219, ((1, 8),), jnp.float32)
    gains_second = jnp.clip(jnp.exp(math.log(3.7746534786720076e-08) - 1.3968765 * jax.random.uniform(arg_keys[17], (2, D), jnp.float32) ** block_scale(arg_keys[17], (2, D), ((1, 8),), -0.2, 0.2)), 9.337300710399177e-09, 3.7746534786720076e-08)
    return dict(block_in=block_in, cotangent=cotangent, buckets=buckets, qkv_weight=qkv_weight, qkv_first=qkv_first, qkv_second=qkv_second, out_weight=out_weight, out_first=out_first, out_second=out_second, up_weight=up_weight, up_first=up_first, up_second=up_second, down_weight=down_weight, down_first=down_first, down_second=down_second, norm_gains=norm_gains, gains_first=gains_first, gains_second=gains_second)


@jax.custom_vjp
def low(v):
    return lax.optimization_barrier(v.astype(jnp.bfloat16)).astype(jnp.float32)

@jax.custom_vjp
def low_back(v):
    return v

def low_keep(v):
    return (low(v), None)

def low_pass(kept, grad):
    return (grad,)

def back_keep(v):
    return (v, None)

def back_low(kept, grad):
    return (low(grad),)
low.defvjp(low_keep, low_pass)
low_back.defvjp(back_keep, back_low)
NORM_EPS = 1e-05
ADAM_EPS = 1e-08
CLIP_NORM = 1.0
BETA_ONE = 0.9
BETA_TWO = 0.95
DECAY_RATE = 0.1
GAIN_RATE = 0.3
ROPE_BASE = 10000.0
HIGH = lax.Precision.HIGHEST

def rms_scale(values, gain):
    return values * lax.rsqrt(lax.optimization_barrier(jnp.mean(values * values, axis=-1, keepdims=True)) + NORM_EPS) * gain

def rotary_tables(length):
    positions = jnp.arange(length).astype(jnp.float32)[:, None]
    freq_index = jnp.arange(HD // 2).astype(jnp.float32)
    angles = positions * (ROPE_BASE ** (-2.0 * freq_index / HD))[None, :]
    cosine = jnp.cos(angles)
    sine = jnp.sin(angles)
    return (jnp.concatenate([cosine, cosine], axis=-1), jnp.concatenate([sine, sine], axis=-1))

def rotate(values, cosine, sine):
    half = values.shape[-1] // 2
    turned = jnp.concatenate([-values[..., half:], values[..., :half]], axis=-1)
    return values * cosine[:, None, :] + turned * sine[:, None, :]

def sequence_layer(params, rows, bucket):
    gain_low, qkv_low, out_low, up_low, down_low = params
    length = rows.shape[0]
    normed_one = low(rms_scale(rows, gain_low[0]))
    project = jnp.einsum('td,cdh->cth', normed_one, qkv_low, precision=HIGH)
    query = low_back(project[0]).reshape(length, H, HD)
    keys = low_back(project[1]).reshape(length, H, HD)
    values = low(low_back(project[2])).reshape(length, H, HD)
    cosine, sine = rotary_tables(length)
    query_turn = low(rotate(query, cosine, sine))
    key_turn = low(rotate(keys, cosine, sine))
    scores = low_back(jnp.einsum('qhe,khe->hqk', query_turn, key_turn, precision=HIGH) * HD ** (-0.5))
    causal = jnp.arange(length)[:, None] >= jnp.arange(length)[None, :]
    scores = jnp.where(causal[None], scores, -1e+30)
    probs = low(jax.nn.softmax(scores, axis=-1))
    mixed = jnp.einsum('hqk,khe->qhe', probs, values, precision=HIGH).reshape(length, H * HD)
    mixed = low(low_back(mixed))
    attended = low_back(jnp.dot(mixed, out_low, precision=HIGH))
    middle = rows + attended
    normed_two = low(rms_scale(middle, gain_low[1]))
    inner = low_back(jnp.dot(normed_two, up_low, precision=HIGH))
    used = (jnp.arange(FF) < (bucket + 1) * (FF // BUCKETS)).astype(jnp.float32)
    hidden = low(jnp.square(jax.nn.relu(inner)) * used[None, :])
    return middle + low_back(jnp.dot(hidden, down_low, precision=HIGH))

def forward(block_rows, norm_gains, qkv_weight, out_weight, up_weight, down_weight, buckets):
    params = (low(norm_gains), low(qkv_weight), low(out_weight), low(up_weight), low(down_weight))
    layer = jax.checkpoint(sequence_layer)

    def visit(carry, item):
        return (carry, layer(params, item[0], item[1]))
    _, outputs = lax.scan(visit, 0, (block_rows.reshape(SEQS, LEN, D), buckets))
    return outputs.reshape(SEQS * LEN, D)

def adam_step(weight, grad, first, second, factor, rate, decay):
    clipped = grad * factor
    first_new = BETA_ONE * first + (1.0 - BETA_ONE) * clipped
    second_new = BETA_TWO * second + (1.0 - BETA_TWO) * clipped * clipped
    first_hat = first_new / (1.0 - BETA_ONE ** STEP)
    second_hat = second_new / (1.0 - BETA_TWO ** STEP)
    weight_new = weight - rate * (first_hat / (jnp.sqrt(second_hat) + ADAM_EPS) + decay * weight)
    return (weight_new, weight_new.astype(jnp.bfloat16), first_new, second_new)

def reference(block_in, cotangent, buckets, qkv_weight, qkv_first, qkv_second, out_weight, out_first, out_second, up_weight, up_first, up_second, down_weight, down_first, down_second, norm_gains, gains_first, gains_second):

    def wrapped(rows, gains, qkv_part, out_part, up_part, down_part):
        return forward(rows, gains, qkv_part, out_part, up_part, down_part, buckets)
    block_out, pull = jax.vjp(wrapped, block_in.astype(jnp.float32), norm_gains, qkv_weight, out_weight, up_weight, down_weight)
    in_grad, gain_grad, qkv_grad, out_grad, up_grad, down_grad = pull(cotangent)
    total = jnp.sum(qkv_grad * qkv_grad) + jnp.sum(out_grad * out_grad) + jnp.sum(up_grad * up_grad)
    total = total + jnp.sum(down_grad * down_grad) + jnp.sum(gain_grad * gain_grad)
    grad_norm = jnp.sqrt(total)
    factor = jnp.minimum(1.0, CLIP_NORM / grad_norm)
    qkv_out = adam_step(qkv_weight, qkv_grad, qkv_first, qkv_second, factor, D ** (-0.5), DECAY_RATE)
    out_out = adam_step(out_weight, out_grad, out_first, out_second, factor, (H * HD // 16) ** (-0.5), DECAY_RATE)
    up_out = adam_step(up_weight, up_grad, up_first, up_second, factor, D ** (-0.5), DECAY_RATE)
    down_out = adam_step(down_weight, down_grad, down_first, down_second, factor, FF ** (-0.5), DECAY_RATE)
    gain_out = adam_step(norm_gains, gain_grad, gains_first, gains_second, factor, GAIN_RATE, 0.0)
    return (block_out, in_grad, grad_norm, qkv_out[0], qkv_out[1], qkv_out[2], qkv_out[3], out_out[0], out_out[1], out_out[2], out_out[3], up_out[0], up_out[1], up_out[2], up_out[3], down_out[0], down_out[1], down_out[2], down_out[3], gain_out[0], gain_out[1], gain_out[2], gain_out[3])
```

```python
import functools
import jax
import jax.numpy as jnp
from jax import lax
from jax.experimental import pallas as pl
from jax.experimental.pallas import tpu as pltpu
from jax.sharding import PartitionSpec as P

D = 2048
H = 16
HD = 128
FF = 8192
STEP = 10

NORM_EPS = 1e-05
ADAM_EPS = 1e-08
CLIP_NORM = 1.0
BETA_ONE = 0.9
BETA_TWO = 0.95
DECAY_RATE = 0.1
GAIN_RATE = 0.3
ROPE_BASE = 10000.0

LOW = jnp.bfloat16
FULL = jnp.float32
SCALE = HD ** (-0.5)
VMEM_BYTES = 48 * 1024 * 1024
NT = (((1,), (1,)), ((), ()))
TN = (((0,), (0,)), ((), ()))


def rotary_tables(length):
    positions = jnp.arange(length).astype(FULL)[:, None]
    freq_index = jnp.arange(HD // 2).astype(FULL)
    angles = positions * (ROPE_BASE ** (-2.0 * freq_index / HD))[None, :]
    cosine = jnp.cos(angles)
    sine = jnp.sin(angles)
    return (jnp.concatenate([cosine, cosine], axis=-1), jnp.concatenate([-sine, sine], axis=-1))


def params(vmem=VMEM_BYTES):
    return pltpu.CompilerParams(vmem_limit_bytes=vmem)


def project_body(place_ref, x_ref, gain_ref, w_ref, cos_ref, sin_ref, *rest):
    normed_ref, out_ref, seq_ref = rest[-3:]
    part = pl.program_id(0)

    @pl.when(part == 0)
    def _():
        low = x_ref[...]
        seq_ref[...] = low
        values = low.astype(FULL)
        inverse = lax.rsqrt(jnp.mean(values * values, axis=-1, keepdims=True) + NORM_EPS)
        normed_ref[...] = (values * inverse * gain_ref[...]).astype(LOW)

    product = jnp.dot(normed_ref[...], w_ref[0], preferred_element_type=FULL)

    @pl.when(part < 2)
    def _():
        for head in range(product.shape[1] // HD):
            one = product[:, head * HD : (head + 1) * HD]
            turned = one * cos_ref[...] + pltpu.roll(one, HD // 2, 1) * sin_ref[...]
            out_ref[0, :, head * HD : (head + 1) * HD] = turned.astype(LOW)

    @pl.when(part == 2)
    def _():
        out_ref[0] = product.astype(LOW)


def project(place, x, gain, weight, cosine, sine, carried):
    rows, width = x.shape
    length = cosine.shape[0]
    cols = weight.shape[2]
    shapes = [
        jax.ShapeDtypeStruct((length, width), LOW),
        jax.ShapeDtypeStruct((3, length, cols), LOW),
        jax.ShapeDtypeStruct((length, width), LOW),
    ]
    in_specs = [
        pl.BlockSpec((rows, width), lambda c, p: (0, 0)),
        pl.BlockSpec((1, width), lambda c, p: (0, 0)),
        pl.BlockSpec((1, width, cols), lambda c, p: (c, 0, 0)),
        pl.BlockSpec((rows, HD), lambda c, p: (p[0], 0)),
        pl.BlockSpec((rows, HD), lambda c, p: (p[0], 0)),
    ]
    aliases = {}
    if carried is not None:
        in_specs += [pl.BlockSpec(memory_space=pl.ANY)] * 3
        aliases = {6: 0, 7: 1, 8: 2}
    return pl.pallas_call(
        project_body,
        grid_spec=pltpu.PrefetchScalarGridSpec(
            num_scalar_prefetch=1,
            grid=(3,),
            in_specs=in_specs,
            out_specs=[
                pl.BlockSpec((rows, width), lambda c, p: (p[0], 0)),
                pl.BlockSpec((1, rows, cols), lambda c, p: (c, p[0], 0)),
                pl.BlockSpec((rows, width), lambda c, p: (p[0], 0)),
            ],
        ),
        out_shape=shapes,
        input_output_aliases=aliases,
        compiler_params=params(),
        cost_estimate=pl.CostEstimate(
            flops=2 * rows * width * cols * 3, bytes_accessed=3 * width * cols * 2, transcendentals=0
        ),
    )(place, x, gain, weight, cosine, sine, *(carried or ()))


def attend_body(half, blocks, q_ref, k_ref, v_ref, mixed_ref, log_ref):
    length = q_ref.shape[1]
    block = length // blocks
    rows = block // 2
    for index in range(blocks):
        first = index * block + half * rows
        last = first + rows
        query = q_ref[0, first:last]
        scores = (
            lax.dot_general(query, k_ref[0, :last], NT, preferred_element_type=FULL) * SCALE
        )
        row = lax.broadcasted_iota(jnp.int32, scores.shape, 0) + first
        col = lax.broadcasted_iota(jnp.int32, scores.shape, 1)
        scores = jnp.where(row >= col, scores, -1e30)
        peak = jnp.max(scores, axis=-1, keepdims=True)
        expo = jnp.exp(scores - peak)
        total = jnp.sum(expo, axis=-1, keepdims=True)
        probs = (expo / total).astype(LOW)
        mixed = jnp.dot(probs, v_ref[0, :last], preferred_element_type=FULL)
        mixed_ref[index * rows : (index + 1) * rows] = mixed.astype(LOW)
        log_ref[index * rows : (index + 1) * rows] = jnp.broadcast_to(
            peak + jnp.log(total), (rows, HD)
        )


def attend(half, blocks, qkv):
    _, length, cols = qkv.shape
    heads = cols // HD
    return pl.pallas_call(
        functools.partial(attend_body, half, blocks),
        grid=(heads,),
        in_specs=[
            pl.BlockSpec((1, length, HD), lambda h: (0, 0, h)),
            pl.BlockSpec((1, length, HD), lambda h: (1, 0, h)),
            pl.BlockSpec((1, length, HD), lambda h: (2, 0, h)),
        ],
        out_specs=[
            pl.BlockSpec((length // 2, HD), lambda h: (0, h)),
            pl.BlockSpec((length // 2, HD), lambda h: (0, h)),
        ],
        out_shape=[
            jax.ShapeDtypeStruct((length // 2, cols), LOW),
            jax.ShapeDtypeStruct((length // 2, cols), FULL),
        ],
        compiler_params=params(),
        cost_estimate=pl.CostEstimate(
            flops=2 * length * length * cols, bytes_accessed=8 * length * cols, transcendentals=length * length * 2
        ),
    )(qkv, qkv, qkv)


def attend_back_body(
    blocks, q_ref, k_ref, v_ref, back_ref, log_a_ref, log_b_ref, cos_ref, sin_ref, out_ref, key_acc, value_acc
):
    length = q_ref.shape[1]
    block = length // blocks
    rows = block // 2

    def turn_back(one, cosine, sine):
        return one * cosine - pltpu.roll(one, HD // 2, 1) * sine

    for index in range(blocks):
        first, last = index * block, (index + 1) * block
        query = q_ref[0, first:last]
        back = back_ref[first:last]
        keys = k_ref[0, :last]
        log_total = jnp.concatenate(
            [
                log_a_ref[index * rows : (index + 1) * rows, :1],
                log_b_ref[index * rows : (index + 1) * rows, :1],
            ],
            axis=0,
        )
        scores = lax.dot_general(query, keys, NT, preferred_element_type=FULL) * SCALE
        row = lax.broadcasted_iota(jnp.int32, scores.shape, 0) + first
        col = lax.broadcasted_iota(jnp.int32, scores.shape, 1)
        probs = jnp.exp(jnp.where(row >= col, scores, -1e30) - log_total)
        back_probs = lax.dot_general(back, v_ref[0, :last], NT, preferred_element_type=FULL)
        centre = jnp.sum(probs * back_probs, axis=-1, keepdims=True)
        back_scores = (probs * (back_probs - centre)).astype(LOW)
        query_grad = jnp.dot(back_scores, keys, preferred_element_type=FULL) * SCALE
        out_ref[0, first:last] = turn_back(query_grad, cos_ref[first:last], sin_ref[first:last]).astype(LOW)
        key_part = lax.dot_general(back_scores, query, TN, preferred_element_type=FULL)
        value_part = lax.dot_general(probs.astype(LOW), back, TN, preferred_element_type=FULL)
        if index > 0:
            key_acc[:first] += key_part[:first]
            value_acc[:first] += value_part[:first]
        key_acc[first:last] = key_part[first:]
        value_acc[first:last] = value_part[first:]
    out_ref[1] = turn_back(key_acc[...] * SCALE, cos_ref[...], sin_ref[...]).astype(LOW)
    out_ref[2] = value_acc[...].astype(LOW)


def attend_back(blocks, qkv, back, log_a, log_b, cosine, sine):
    _, length, cols = qkv.shape
    heads = cols // HD
    column = lambda h: (0, h)
    return pl.pallas_call(
        functools.partial(attend_back_body, blocks),
        grid=(heads,),
        in_specs=[
            pl.BlockSpec((1, length, HD), lambda h: (0, 0, h)),
            pl.BlockSpec((1, length, HD), lambda h: (1, 0, h)),
            pl.BlockSpec((1, length, HD), lambda h: (2, 0, h)),
            pl.BlockSpec((length, HD), column),
            pl.BlockSpec((length // 2, HD), column),
            pl.BlockSpec((length // 2, HD), column),
            pl.BlockSpec((length, HD), lambda h: (0, 0)),
            pl.BlockSpec((length, HD), lambda h: (0, 0)),
        ],
        out_specs=pl.BlockSpec((3, length, HD), lambda h: (0, 0, h)),
        out_shape=jax.ShapeDtypeStruct((3, length, cols), LOW),
        scratch_shapes=[pltpu.VMEM((length, HD), FULL), pltpu.VMEM((length, HD), FULL)],
        compiler_params=params(),
        cost_estimate=pl.CostEstimate(
            flops=5 * length * length * cols, bytes_accessed=14 * length * cols, transcendentals=length * length * 4
        ),
    )(qkv, qkv, qkv, back, log_a, log_b, cosine, sine)


def adam_step(weight, grad, first, second, factor, rate, decay):
    clipped = grad * factor
    first_new = BETA_ONE * first + (1.0 - BETA_ONE) * clipped
    second_new = BETA_TWO * second + (1.0 - BETA_TWO) * clipped * clipped
    first_hat = first_new / (1.0 - BETA_ONE**STEP)
    second_hat = second_new / (1.0 - BETA_TWO**STEP)
    weight_new = weight - rate * (first_hat / (jnp.sqrt(second_hat) + ADAM_EPS) + decay * weight)
    return (weight_new, weight_new.astype(LOW), first_new, second_new)


def per_device(
    toks,
    bkts,
    block_in,
    cotangent,
    buckets,
    qkv_weight,
    qkv_first,
    qkv_second,
    out_weight,
    out_first,
    out_second,
    up_weight,
    up_first,
    up_second,
    down_weight,
    down_first,
    down_second,
    norm_gains,
    gains_first,
    gains_second,
):
    group = lax.axis_index("bkt")
    rows, width = block_in.shape
    half = rows // 2
    length = rows * bkts
    ring = [(i, (i + 1) % bkts) for i in range(bkts)]

    def pass_on(value):
        return lax.ppermute(value, "bkt", ring)

    def owner(step):
        return lax.rem(group - step + bkts, bkts)

    def ring_gather(value):
        held = [value]
        for _ in range(bkts - 1):
            held.append(pass_on(held[-1]))
        return held

    def ring_sum(part_of):
        total = part_of(owner(1)).astype(LOW)
        for step in range(1, bkts):
            total = pass_on(total).astype(FULL) + part_of(owner(step + 1)).astype(FULL)
            if step < bkts - 1:
                total = total.astype(LOW)
        return total

    qkv_full = lax.all_gather(qkv_weight.astype(LOW), "tok", axis=1, tiled=True)
    gain_float = lax.all_gather(norm_gains.astype(LOW), "tok", axis=1, tiled=True).astype(FULL)
    x_held = ring_gather(block_in)
    out_held = ring_gather(out_weight.astype(LOW))
    out_depth, out_width = out_weight.shape
    out_line = jnp.zeros((bkts, out_depth, out_width), LOW)
    for step in range(bkts):
        out_line = lax.dynamic_update_slice(out_line, out_held[step][None], (owner(step), 0, 0))
    out_full = lax.all_gather(out_line.reshape(bkts * out_depth, out_width), "tok", axis=1, tiled=True)
    up_full = lax.all_gather(up_weight.astype(LOW), "tok", axis=0, tiled=True)
    down_full = lax.all_gather(down_weight.astype(LOW), "tok", axis=1, tiled=True)
    cosine, sine = rotary_tables(length)

    carried = None
    for step in range(bkts):
        carried = project(
            owner(step).reshape(1), x_held[step], gain_float[0:1], qkv_full, cosine, sine, carried
        )
    normed_one, qkv, seq_in = carried
    cols = qkv.shape[2]

    back_held = ring_gather(cotangent.astype(LOW))
    seq_back = jnp.zeros((bkts, rows, width), LOW)
    for step in range(bkts):
        seq_back = lax.dynamic_update_slice(seq_back, back_held[step][None], (owner(step), 0, 0))
    seq_in = seq_in.reshape(bkts, rows, width)

    live = (buckets[0] >= group).astype(FULL)
    mixed_own, logs, own_middle, own_two = [], [], [], []
    normed_two, hidden, back_inner, back_half = [], [], [], []
    mixed_halves, middles, back_twos = [], [], []
    for part in range(2):
        mixed, log_total = attend(part, bkts, qkv)
        logs.append(log_total)
        mixed_held = ring_gather(mixed)
        acc = seq_in[:, part * half : (part + 1) * half].reshape(bkts * half, width).astype(FULL)
        own_cols = []
        for step in range(bkts):
            weight = lax.dynamic_slice_in_dim(out_full, owner(step) * cols, cols, 0)
            acc = acc + jnp.dot(mixed_held[step], weight, preferred_element_type=FULL)
            own_cols.append(lax.dynamic_slice_in_dim(mixed_held[step], group * half, half, 0))
        mixed_rows = jnp.zeros((half, bkts * cols), LOW)
        for step in range(bkts):
            mixed_rows = lax.dynamic_update_slice(mixed_rows, own_cols[step], (0, owner(step) * cols))
        mixed_halves.append(mixed_rows)
        middles.append(lax.dynamic_slice_in_dim(acc, group * half, half, 0))
        inverse = lax.rsqrt(jnp.mean(acc * acc, axis=-1, keepdims=True) + NORM_EPS)
        normed = (acc * inverse * gain_float[1]).astype(LOW)
        normed_two.append(normed)
        inner = jax.nn.relu(jnp.dot(normed, up_full, preferred_element_type=FULL))
        hidden.append((inner * inner * live).astype(LOW))
        back_low = seq_back[:, part * half : (part + 1) * half].reshape(bkts * half, width)
        back_half.append(back_low)
        back_hidden = lax.dot_general(back_low, down_full, NT, preferred_element_type=FULL)
        back_inner.append((back_hidden * 2.0 * inner * live).astype(LOW))
        back_two_part = lax.dot_general(back_inner[-1], up_full, NT, preferred_element_type=FULL).astype(LOW)
        back_twos.append(
            ring_sum(lambda place: lax.dynamic_slice_in_dim(back_two_part, place * half, half, 0))
        )
    middle = jnp.concatenate(middles)
    back_two = jnp.concatenate(back_twos)
    mixed_rows = jnp.concatenate(mixed_halves)
    normed_two = jnp.concatenate(normed_two)
    back_inner = jnp.concatenate(back_inner)
    hidden = jnp.concatenate(hidden)
    back_half = jnp.concatenate(back_half)

    inverse = lax.rsqrt(jnp.mean(middle * middle, axis=-1, keepdims=True) + NORM_EPS)
    normal = middle * inverse
    scaled = gain_float[1] * back_two
    middle_grad = cotangent + inverse * (
        scaled - normal * jnp.mean(normal * scaled, axis=-1, keepdims=True)
    )
    gain_grad_two = jnp.sum(back_two * normal, axis=0)
    middle_low = middle_grad.astype(LOW)
    back_mixed = lax.dot_general(middle_low, out_full, NT, preferred_element_type=FULL).astype(LOW)
    back_seq = jnp.zeros((bkts, rows, cols), LOW)
    for step in range(bkts):
        piece = lax.dynamic_slice_in_dim(back_mixed, lax.rem(group + step, bkts) * cols, cols, 1)
        if step > 0:
            piece = lax.ppermute(piece, "bkt", [(i, (i + step) % bkts) for i in range(bkts)])
        back_seq = lax.dynamic_update_slice(back_seq, piece[None], (owner(step), 0, 0))

    up_grad = lax.dot_general(normed_two, back_inner, TN, preferred_element_type=FULL).astype(LOW)
    up_part = lax.psum_scatter(up_grad, "tok", scatter_dimension=0, tiled=True).astype(FULL)
    down_grad = lax.dot_general(hidden, back_half, TN, preferred_element_type=FULL).astype(LOW)
    down_part = lax.psum_scatter(down_grad, "tok", scatter_dimension=1, tiled=True).astype(FULL)
    out_grad = lax.dot_general(mixed_rows, middle_low, TN, preferred_element_type=FULL).astype(LOW)
    out_sum = lax.psum_scatter(out_grad, "tok", scatter_dimension=1, tiled=True)
    out_part = ring_sum(lambda place: lax.dynamic_slice_in_dim(out_sum, place * out_depth, out_depth, 0))

    down_prod = jnp.dot(hidden, down_full, preferred_element_type=FULL).astype(LOW)
    down_prod = down_prod.reshape(2, bkts, half, width)
    ffn_part = ring_sum(lambda place: lax.dynamic_slice_in_dim(down_prod, place, 1, 1)[:, 0])
    block_out = middle + ffn_part.reshape(rows, width)

    back_project = attend_back(
        bkts, qkv, back_seq.reshape(length, cols), logs[0], logs[1], cosine, sine
    )

    def back_one_part(place):
        piece = lax.dynamic_slice_in_dim(back_project, place * rows, rows, 1)
        return jnp.einsum("cth,cdh->td", piece, qkv_full, preferred_element_type=FULL)

    back_one = ring_sum(back_one_part)
    qkv_grad = jnp.einsum("td,cth->cdh", normed_one, back_project, preferred_element_type=FULL)
    qkv_part = lax.psum_scatter(
        qkv_grad.astype(LOW), "tok", scatter_dimension=1, tiled=True
    ).astype(FULL)
    residual_in = block_in.astype(FULL)
    inverse = lax.rsqrt(jnp.mean(residual_in * residual_in, axis=-1, keepdims=True) + NORM_EPS)
    normal = residual_in * inverse
    scaled = gain_float[0] * back_one
    block_in_grad = middle_grad + inverse * (
        scaled - normal * jnp.mean(normal * scaled, axis=-1, keepdims=True)
    )
    gain_grad_one = jnp.sum(back_one * normal, axis=0)

    weight_squares = jnp.sum(qkv_part * qkv_part) + jnp.sum(out_part * out_part)
    weight_squares = weight_squares + jnp.sum(up_part * up_part) + jnp.sum(down_part * down_part)
    packed = jnp.concatenate(
        [gain_grad_one, gain_grad_two, jnp.broadcast_to(weight_squares, (HD,))]
    )
    for axis, size in (("tok", toks), ("bkt", bkts)):
        if size & (size - 1):
            packed = lax.psum(packed, axis)
        else:
            step = 1
            while step < size:
                packed = packed + lax.ppermute(packed, axis, [(i, i ^ step) for i in range(size)])
                step *= 2
    gain_total = packed[: 2 * width].reshape(2, width)
    grad_norm = jnp.sqrt(packed[2 * width] + jnp.sum(gain_total * gain_total))
    factor = jnp.minimum(1.0, CLIP_NORM / grad_norm)
    gain_width = norm_gains.shape[1]
    gain_part = lax.dynamic_slice_in_dim(
        gain_total, lax.axis_index("tok") * gain_width, gain_width, 1
    )
    qkv_out = adam_step(
        qkv_weight, qkv_part, qkv_first, qkv_second, factor, D ** (-0.5), DECAY_RATE
    )
    out_out = adam_step(
        out_weight, out_part, out_first, out_second, factor, (H * HD // 16) ** (-0.5), DECAY_RATE
    )
    up_out = adam_step(up_weight, up_part, up_first, up_second, factor, D ** (-0.5), DECAY_RATE)
    down_out = adam_step(
        down_weight, down_part, down_first, down_second, factor, FF ** (-0.5), DECAY_RATE
    )
    gain_out = adam_step(norm_gains, gain_part, gains_first, gains_second, factor, GAIN_RATE, 0.0)
    return (block_out, block_in_grad, grad_norm, *qkv_out, *out_out, *up_out, *down_out, *gain_out)


def solution(mesh):
    rows = P(("tok", "bkt"), None)
    qkv = P(None, "tok", "bkt")
    tall = P("bkt", "tok")
    wide = P("tok", "bkt")
    gains = P(None, "tok")
    return jax.shard_map(
        functools.partial(per_device, mesh.shape["tok"], mesh.shape["bkt"]),
        mesh=mesh,
        in_specs=(rows, rows, P("tok"), *[qkv] * 3, *[tall] * 3, *[wide] * 3, *[tall] * 3, *[gains] * 3),
        out_specs=(rows, rows, P(), *[qkv] * 4, *[tall] * 4, *[wide] * 4, *[tall] * 4, *[gains] * 4),
        check_vma=False,
    )
```

```python
import functools
import jax
import jax.numpy as jnp
from jax import lax
from jax.experimental import pallas as pl
from jax.experimental.pallas import tpu as pltpu
from jax.sharding import Mesh, PartitionSpec as P

D = 2048
H = 16
HD = 128
FF = 8192
STEP = 10

NORM_EPS = 1e-05
ADAM_EPS = 1e-08
CLIP_NORM = 1.0
BETA_ONE = 0.9
BETA_TWO = 0.95
DECAY_RATE = 0.1
GAIN_RATE = 0.3
ROPE_BASE = 10000.0

LOW = jnp.bfloat16
FULL = jnp.float32
SCALE = HD ** (-0.5)
VMEM_BYTES = 48 * 1024 * 1024
NN = (((1,), (0,)), ((), ()))
NT = (((1,), (1,)), ((), ()))
TN = (((0,), (0,)), ((), ()))


def rotary_tables(length):
    positions = jnp.arange(length).astype(FULL)[:, None]
    freq_index = jnp.arange(HD // 2).astype(FULL)
    angles = positions * (ROPE_BASE ** (-2.0 * freq_index / HD))[None, :]
    cosine = jnp.cos(angles)
    sine = jnp.sin(angles)
    return (jnp.concatenate([cosine, cosine], axis=-1), jnp.concatenate([-sine, sine], axis=-1))


LIGHT = pl.CostEstimate(flops=1, bytes_accessed=1, transcendentals=0)


def params(vmem=VMEM_BYTES):
    return pltpu.CompilerParams(vmem_limit_bytes=vmem)


def project_body(place_ref, x_ref, gain_ref, w_ref, cos_ref, sin_ref, *rest):
    normed_ref, out_ref, seq_ref = rest[-3:]
    part = pl.program_id(0)

    @pl.when(part == 0)
    def _():
        low = x_ref[...]
        seq_ref[...] = low
        values = low.astype(FULL)
        inverse = lax.rsqrt(jnp.mean(values * values, axis=-1, keepdims=True) + NORM_EPS)
        normed_ref[...] = (values * inverse * gain_ref[...]).astype(LOW)

    product = jnp.dot(normed_ref[...], w_ref[0], preferred_element_type=FULL)

    @pl.when(part < 2)
    def _():
        for head in range(product.shape[1] // HD):
            one = product[:, head * HD : (head + 1) * HD]
            turned = one * cos_ref[...] + pltpu.roll(one, HD // 2, 1) * sin_ref[...]
            out_ref[0, :, head * HD : (head + 1) * HD] = turned.astype(LOW)

    @pl.when(part == 2)
    def _():
        out_ref[0] = product.astype(LOW)


def project(place, x, gain, weight, cosine, sine, carried):
    rows, width = x.shape
    length = cosine.shape[0]
    cols = weight.shape[2]
    shapes = [
        jax.ShapeDtypeStruct((length, width), LOW),
        jax.ShapeDtypeStruct((3, length, cols), LOW),
        jax.ShapeDtypeStruct((length, width), LOW),
    ]
    in_specs = [
        pl.BlockSpec((rows, width), lambda c, p: (0, 0)),
        pl.BlockSpec((1, width), lambda c, p: (0, 0)),
        pl.BlockSpec((1, width, cols), lambda c, p: (c, 0, 0)),
        pl.BlockSpec((rows, HD), lambda c, p: (p[0], 0)),
        pl.BlockSpec((rows, HD), lambda c, p: (p[0], 0)),
    ]
    aliases = {}
    if carried is not None:
        in_specs += [pl.BlockSpec(memory_space=pl.ANY)] * 3
        aliases = {6: 0, 7: 1, 8: 2}
    return pl.pallas_call(
        project_body,
        grid_spec=pltpu.PrefetchScalarGridSpec(
            num_scalar_prefetch=1,
            grid=(3,),
            in_specs=in_specs,
            out_specs=[
                pl.BlockSpec((rows, width), lambda c, p: (p[0], 0)),
                pl.BlockSpec((1, rows, cols), lambda c, p: (c, p[0], 0)),
                pl.BlockSpec((rows, width), lambda c, p: (p[0], 0)),
            ],
        ),
        out_shape=shapes,
        input_output_aliases=aliases,
        compiler_params=params(),
        cost_estimate=LIGHT,
    )(place, x, gain, weight, cosine, sine, *(carried or ()))


def attend_body(half, blocks, count, q_ref, k_ref, v_ref, *rest):
    cotangents, (ring_ref, log_ref) = rest[:count], rest[count:]
    length = q_ref.shape[1]
    block = length // blocks
    rows = block // 2
    for index in range(count):
        first = length // 2 + index * rows
        ring_ref[first : first + rows] = cotangents[index][...].astype(LOW)
    for index in range(blocks):
        first = index * block + half * rows
        last = first + rows
        query = q_ref[0, first:last]
        scores = (
            lax.dot_general(query, k_ref[0, :last], NT, preferred_element_type=FULL) * SCALE
        )
        row = lax.broadcasted_iota(jnp.int32, scores.shape, 0) + first
        col = lax.broadcasted_iota(jnp.int32, scores.shape, 1)
        scores = jnp.where(row >= col, scores, -1e30)
        peak = jnp.max(scores, axis=-1, keepdims=True)
        expo = jnp.exp(scores - peak)
        total = jnp.sum(expo, axis=-1, keepdims=True)
        probs = (expo / total).astype(LOW)
        mixed = jnp.dot(probs, v_ref[0, :last], preferred_element_type=FULL)
        ring_ref[index * rows : (index + 1) * rows] = mixed.astype(LOW)
        log_ref[index * rows : (index + 1) * rows] = jnp.broadcast_to(
            peak + jnp.log(total), (rows, HD)
        )


def attend(half, blocks, qkv, cotangent):
    _, length, cols = qkv.shape
    heads = cols // HD
    rows, width = cotangent.shape
    count = width // cols

    def cotangent_spec(index):
        return pl.BlockSpec((rows // 2, HD), lambda h: (half, index * heads + h))

    return pl.pallas_call(
        functools.partial(attend_body, half, blocks, count),
        grid=(heads,),
        in_specs=[
            pl.BlockSpec((1, length, HD), lambda h: (0, 0, h)),
            pl.BlockSpec((1, length, HD), lambda h: (1, 0, h)),
            pl.BlockSpec((1, length, HD), lambda h: (2, 0, h)),
        ]
        + [cotangent_spec(index) for index in range(count)],
        out_specs=[
            pl.BlockSpec((length // 2 + count * rows // 2, HD), lambda h: (0, h)),
            pl.BlockSpec((length // 2, HD), lambda h: (0, h)),
        ],
        out_shape=[
            jax.ShapeDtypeStruct((length // 2 + count * rows // 2, cols), LOW),
            jax.ShapeDtypeStruct((length // 2, cols), FULL),
        ],
        compiler_params=params(),
        cost_estimate=LIGHT,
    )(qkv, qkv, qkv, *[cotangent] * count)


def attend_back_body(blocks, place_ref, q_ref, k_ref, v_ref, log_a_ref, log_b_ref, cos_ref, sin_ref, *rest):
    pieces = rest[: 2 * blocks]
    out_ref, key_acc, value_acc, back_ref = rest[2 * blocks :]
    length = q_ref.shape[1]
    block = length // blocks
    rows = block // 2
    for half in range(2):
        for step in range(blocks):
            first = pl.multiple_of(place_ref[step] * block + half * rows, rows)
            back_ref[pl.ds(first, rows), :] = pieces[half * blocks + step][...]

    def turn_back(one, cosine, sine):
        return one * cosine - pltpu.roll(one, HD // 2, 1) * sine

    for index in range(blocks):
        first, last = index * block, (index + 1) * block
        query = q_ref[0, first:last]
        back = back_ref[first:last]
        keys = k_ref[0, :last]
        log_total = jnp.concatenate(
            [
                log_a_ref[index * rows : (index + 1) * rows, :1],
                log_b_ref[index * rows : (index + 1) * rows, :1],
            ],
            axis=0,
        )
        scores = lax.dot_general(query, keys, NT, preferred_element_type=FULL) * SCALE
        row = lax.broadcasted_iota(jnp.int32, scores.shape, 0) + first
        col = lax.broadcasted_iota(jnp.int32, scores.shape, 1)
        probs = jnp.exp(jnp.where(row >= col, scores, -1e30) - log_total)
        back_probs = lax.dot_general(back, v_ref[0, :last], NT, preferred_element_type=FULL)
        centre = jnp.sum(probs * back_probs, axis=-1, keepdims=True)
        back_scores = (probs * (back_probs - centre)).astype(LOW)
        query_grad = jnp.dot(back_scores, keys, preferred_element_type=FULL) * SCALE
        out_ref[0, first:last] = turn_back(query_grad, cos_ref[first:last], sin_ref[first:last]).astype(LOW)
        key_part = lax.dot_general(back_scores, query, TN, preferred_element_type=FULL)
        value_part = lax.dot_general(probs.astype(LOW), back, TN, preferred_element_type=FULL)
        if index > 0:
            key_acc[:first] += key_part[:first]
            value_acc[:first] += value_part[:first]
        key_acc[first:last] = key_part[first:]
        value_acc[first:last] = value_part[first:]
    out_ref[1] = turn_back(key_acc[...] * SCALE, cos_ref[...], sin_ref[...]).astype(LOW)
    out_ref[2] = value_acc[...].astype(LOW)


def attend_back(places, qkv, pieces, logs, cosine, sine):
    _, length, cols = qkv.shape
    heads = cols // HD
    blocks = len(pieces) // 2
    column = lambda h, p: (0, h)
    return pl.pallas_call(
        functools.partial(attend_back_body, blocks),
        grid_spec=pltpu.PrefetchScalarGridSpec(
            num_scalar_prefetch=1,
            grid=(heads,),
            in_specs=[
                pl.BlockSpec((1, length, HD), lambda h, p: (0, 0, h)),
                pl.BlockSpec((1, length, HD), lambda h, p: (1, 0, h)),
                pl.BlockSpec((1, length, HD), lambda h, p: (2, 0, h)),
                pl.BlockSpec((length // 2, HD), column),
                pl.BlockSpec((length // 2, HD), column),
                pl.BlockSpec((length, HD), lambda h, p: (0, 0)),
                pl.BlockSpec((length, HD), lambda h, p: (0, 0)),
            ]
            + [pl.BlockSpec((length // blocks // 2, HD), column)] * (2 * blocks),
            out_specs=pl.BlockSpec((3, length, HD), lambda h, p: (0, 0, h)),
            scratch_shapes=[
                pltpu.VMEM((length, HD), FULL),
                pltpu.VMEM((length, HD), FULL),
                pltpu.VMEM((length, HD), LOW),
            ],
        ),
        out_shape=jax.ShapeDtypeStruct((3, length, cols), LOW),
        compiler_params=params(),
        cost_estimate=LIGHT,
    )(places, qkv, qkv, qkv, logs[0], logs[1], cosine, sine, *pieces)


def mix_first_body(count, place_ref, seq_ref, *rest):
    slabs, weights, acc_ref = rest[:count], rest[count : 2 * count], rest[2 * count]
    blocks, rows, width = seq_ref.shape
    shards, _, _, shard = weights[0].shape
    for index in range(shards):
        span = slice(index * shard, (index + 1) * shard)
        total = seq_ref[:, :, span].reshape(blocks * rows, shard).astype(FULL)
        for slab, weight in zip(slabs, weights):
            total = total + jnp.dot(slab[...], weight[index, 0], preferred_element_type=FULL)
        acc_ref[:, span] = total


def mix_first(part, places, seq_in, slabs, weight):
    blocks, block, width = seq_in.shape
    half = block // 2
    shards, _, cols, shard = weight.shape
    tile = max(1, 512 // shard)
    count = len(slabs)

    def weight_spec(step):
        return pl.BlockSpec((tile, 1, cols, shard), lambda i, p: (i, p[step], 0, 0))

    return pl.pallas_call(
        functools.partial(mix_first_body, count),
        grid_spec=pltpu.PrefetchScalarGridSpec(
            num_scalar_prefetch=1,
            grid=(shards // tile,),
            in_specs=[pl.BlockSpec((blocks, half, tile * shard), lambda i, p: (0, part, i))]
            + [pl.BlockSpec((blocks * half, cols), lambda i, p: (0, 0))] * count
            + [weight_spec(step) for step in range(count)],
            out_specs=pl.BlockSpec((blocks * half, tile * shard), lambda i, p: (0, i)),
        ),
        out_shape=jax.ShapeDtypeStruct((blocks * half, width), FULL),
        compiler_params=params(),
        cost_estimate=LIGHT,
    )(places, seq_in, *slabs, *[weight] * count)


def mix_last_body(count, place_ref, acc_ref, gain_ref, weight_ref, *rest):
    slabs = rest[:count]
    normed_ref, middle_ref, mixed_ref = rest[count:]
    cols = slabs[0].shape[1]
    slab = slabs[-1][...]
    parts = [
        jnp.dot(slab, weight_ref[index, 0], preferred_element_type=FULL)
        for index in range(weight_ref.shape[0])
    ]
    middle = acc_ref[...] + jnp.concatenate(parts, axis=1)
    inverse = lax.rsqrt(jnp.mean(middle * middle, axis=-1, keepdims=True) + NORM_EPS)
    normed_ref[...] = (middle * inverse * gain_ref[...]).astype(LOW)

    @pl.when(pl.program_id(0) == place_ref[0])
    def _():
        middle_ref[...] = middle
        for step in range(count):
            first = pl.multiple_of(place_ref[step] * cols, cols)
            mixed_ref[:, pl.ds(first, cols)] = slabs[step][...]


def mix_last(places, acc, gain, slabs, weight):
    length, width = acc.shape
    shards, count, cols, shard = weight.shape
    rows = length // count
    return pl.pallas_call(
        functools.partial(mix_last_body, count),
        grid_spec=pltpu.PrefetchScalarGridSpec(
            num_scalar_prefetch=1,
            grid=(count,),
            in_specs=[
                pl.BlockSpec((rows, width), lambda i, p: (i, 0)),
                pl.BlockSpec((1, width), lambda i, p: (0, 0)),
                pl.BlockSpec((shards, 1, cols, shard), lambda i, p: (0, p[count - 1], 0, 0)),
            ]
            + [pl.BlockSpec((rows, cols), lambda i, p: (i, 0))] * count,
            out_specs=[
                pl.BlockSpec((rows, width), lambda i, p: (i, 0)),
                pl.BlockSpec((rows, width), lambda i, p: (0, 0)),
                pl.BlockSpec((rows, count * cols), lambda i, p: (0, 0)),
            ],
        ),
        out_shape=[
            jax.ShapeDtypeStruct((length, width), LOW),
            jax.ShapeDtypeStruct((rows, width), FULL),
            jax.ShapeDtypeStruct((rows, count * cols), LOW),
        ],
        compiler_params=params(),
        cost_estimate=LIGHT,
    )(places, acc, gain, weight, *slabs)


def hidden_body(count, place_ref, live_ref, normed_ref, up_ref, down_ref, *rest):
    pieces = rest[:count]
    hidden_ref, inner_ref, back_ref = rest[count:]
    cols = pieces[0].shape[1]
    rows = pieces[0].shape[0] * cols // back_ref.shape[1]

    @pl.when(pl.program_id(0) == 0)
    def _():
        for step in range(count):
            first = pl.multiple_of(place_ref[step] * rows, rows)
            for index in range(pieces[0].shape[0] // rows):
                span = slice(index * rows, (index + 1) * rows)
                back_ref[pl.ds(first, rows), index * cols : (index + 1) * cols] = pieces[step][span]

    inner = jnp.dot(normed_ref[...], up_ref[...], preferred_element_type=FULL)
    inner = jnp.maximum(inner, 0.0) * live_ref[0]
    hidden_ref[...] = (inner * inner).astype(LOW)
    back = lax.dot_general(back_ref[...], down_ref[...], NT, preferred_element_type=FULL)
    inner_ref[...] = (back * 2.0 * inner).astype(LOW)


def hidden_units(places, live, normed, up, down, pieces):
    length, width = normed.shape
    units = up.shape[1]
    tile = min(512, units)
    count = len(pieces)
    cols = pieces[0].shape[1]
    below = pieces[0].shape[0] - length
    whole = lambda i, p, l: (0, 0)
    column = lambda i, p, l: (0, i)
    return pl.pallas_call(
        functools.partial(hidden_body, count),
        grid_spec=pltpu.PrefetchScalarGridSpec(
            num_scalar_prefetch=2,
            grid=(units // tile,),
            in_specs=[
                pl.BlockSpec((length, width), whole),
                pl.BlockSpec((width, tile), column),
                pl.BlockSpec((tile, width), lambda i, p, l: (i, 0)),
            ]
            + [pl.BlockSpec((below, cols), lambda i, p, l: (length // below, 0))] * count,
            out_specs=[
                pl.BlockSpec((length, tile), column),
                pl.BlockSpec((length, tile), column),
                pl.BlockSpec((length, width), whole),
            ],
        ),
        out_shape=[
            jax.ShapeDtypeStruct((length, units), LOW),
            jax.ShapeDtypeStruct((length, units), LOW),
            jax.ShapeDtypeStruct((length, width), LOW),
        ],
        compiler_params=params(),
        cost_estimate=LIGHT,
    )(places, live, normed, up, down, *pieces)


def product_body(dims, left_ref, right_ref, out_ref):
    out_ref[...] = lax.dot_general(
        left_ref[...], right_ref[...], dims, preferred_element_type=FULL
    ).astype(LOW)


def product(left, right, turned):
    length, depth = left.shape
    width = right.shape[0] if turned else right.shape[1]
    tile = min(512, width)
    if turned:
        spec = pl.BlockSpec((tile, depth), lambda i: (i, 0))
    else:
        spec = pl.BlockSpec((depth, tile), lambda i: (0, i))
    return pl.pallas_call(
        functools.partial(product_body, NT if turned else NN),
        grid=(width // tile,),
        in_specs=[pl.BlockSpec((length, depth), lambda i: (0, 0)), spec],
        out_specs=pl.BlockSpec((length, tile), lambda i: (0, i)),
        out_shape=jax.ShapeDtypeStruct((length, width), LOW),
        compiler_params=params(),
        cost_estimate=LIGHT,
    )(left, right)


def split_shards(core, total, axis, first, kept_ref, sent_refs):
    shard = kept_ref.shape[1 + axis]
    count = total.shape[axis] // (2 * shard)

    def cut(index):
        span = slice(index * shard, (index + 1) * shard)
        return total[span] if axis == 0 else total[:, span]

    for index in range(count):
        even, odd = cut(2 * index), cut(2 * index + 1)
        kept_ref[index] = jnp.where(core == 0, even, odd).astype(LOW)
        sent = jnp.where(core == 0, odd, even).astype(LOW)
        if axis == 1:
            sent_refs[index][...] = sent
        else:
            for chip in range(index, len(sent_refs), count):

                @pl.when(first + index == chip)
                def _():
                    sent_refs[chip][...] = sent


def grad_body(count, axis, core_ref, *refs):
    total = None
    for index in range(count):
        product = lax.dot_general(
            refs[index][...], refs[count + index][...], TN, preferred_element_type=FULL
        )
        total = product if total is None else total + product
    kept_ref, sent_refs = refs[2 * count], refs[2 * count + 1 :]
    first = pl.program_id(0) * kept_ref.shape[0] if axis == 0 else 0
    split_shards(core_ref[0], total, axis, first, kept_ref, sent_refs)


def weight_grad(core, lefts, rights, chips, axis):
    depth = lefts[0].shape[1]
    width = rights[0].shape[1]
    tile = min(512, depth)
    shards = 2 * chips
    if axis == 1:
        shape = (depth, width // shards)
        spec = pl.BlockSpec((chips, tile, width // shards), lambda i, c: (0, i, 0))
        sent = pl.BlockSpec((tile, width // shards), lambda i, c: (i, 0))
    else:
        shape = (depth // shards, width)
        spec = pl.BlockSpec((tile * chips // depth, depth // shards, width), lambda i, c: (i, 0, 0))
        sent = pl.BlockSpec(shape, lambda i, c: (0, 0))
    out = pl.pallas_call(
        functools.partial(grad_body, len(lefts), axis),
        grid_spec=pltpu.PrefetchScalarGridSpec(
            num_scalar_prefetch=1,
            grid=(depth // tile,),
            in_specs=[pl.BlockSpec((left.shape[0], tile), lambda i, c: (0, i)) for left in lefts]
            + [pl.BlockSpec(right.shape, lambda i, c: (0, 0)) for right in rights],
            out_specs=[spec] + [sent] * chips,
        ),
        out_shape=[jax.ShapeDtypeStruct((chips, *shape), LOW)] + [jax.ShapeDtypeStruct(shape, LOW)] * chips,
        compiler_params=params(),
        cost_estimate=LIGHT,
    )(core, *lefts, *rights)
    return out[0], out[1:]


def project_grad_body(core_ref, left_ref, right_ref, kept_ref, *sent_refs):
    products = [
        lax.dot_general(left_ref[...], right_ref[part], TN, preferred_element_type=FULL)
        for part in range(3)
    ]
    first = pl.program_id(0) * kept_ref.shape[0]
    split_shards(core_ref[0], jnp.concatenate(products, axis=1), 0, first, kept_ref, sent_refs)


def project_grad(core, left, right, chips):
    length, depth = left.shape
    cols = right.shape[2]
    tile = min(512, depth)
    shards = 2 * chips
    shape = (depth // shards, 3 * cols)
    out = pl.pallas_call(
        project_grad_body,
        grid_spec=pltpu.PrefetchScalarGridSpec(
            num_scalar_prefetch=1,
            grid=(depth // tile,),
            in_specs=[
                pl.BlockSpec((length, tile), lambda i, c: (0, i)),
                pl.BlockSpec(right.shape, lambda i, c: (0, 0, 0)),
            ],
            out_specs=[pl.BlockSpec((tile * chips // depth, *shape), lambda i, c: (i, 0, 0))]
            + [pl.BlockSpec(shape, lambda i, c: (0, 0))] * chips,
        ),
        out_shape=[jax.ShapeDtypeStruct((chips, *shape), LOW)] + [jax.ShapeDtypeStruct(shape, LOW)] * chips,
        compiler_params=params(),
        cost_estimate=LIGHT,
    )(core, left, right)
    return out[0], out[1:]


def core_add_body(kept_ref, *refs):
    for index, arrived in enumerate(refs[:-1]):
        refs[-1][index] = (kept_ref[index].astype(FULL) + arrived[...].astype(FULL)).astype(LOW)


def core_add_kernel(kept, arrived):
    chips, rows, width = kept.shape
    tile = min(rows, max(16, rows // 4))
    spec = pl.BlockSpec((chips, tile, width), lambda i: (0, i, 0))
    return pl.pallas_call(
        core_add_body,
        grid=(rows // tile,),
        in_specs=[spec] + [pl.BlockSpec((tile, width), lambda i: (i, 0))] * chips,
        out_specs=spec,
        out_shape=jax.ShapeDtypeStruct(kept.shape, LOW),
        compiler_params=params(),
        cost_estimate=LIGHT,
    )(kept, *arrived)


def core_add_apart_body(count, chip_ref, kept_ref, *refs):
    for index in range(count):
        total = (kept_ref[index].astype(FULL) + refs[index][...].astype(FULL)).astype(LOW)
        for mask in range(count):

            @pl.when((chip_ref[0] ^ index) == mask)
            def _():
                refs[count + mask][...] = total


def core_add_apart(chip, kept, arrived):
    chips, rows, width = kept.shape
    tile = min(rows, max(16, rows // 4))
    spec = pl.BlockSpec((tile, width), lambda i, c: (i, 0))
    return pl.pallas_call(
        functools.partial(core_add_apart_body, chips),
        grid_spec=pltpu.PrefetchScalarGridSpec(
            num_scalar_prefetch=1,
            grid=(rows // tile,),
            in_specs=[pl.BlockSpec((chips, tile, width), lambda i, c: (0, i, 0))] + [spec] * chips,
            out_specs=[spec] * chips,
        ),
        out_shape=[jax.ShapeDtypeStruct((rows, width), LOW)] * chips,
        compiler_params=params(),
        cost_estimate=LIGHT,
    )(chip.reshape(1).astype(jnp.int32), kept, *arrived)


def add_many_body(*refs):
    total = refs[0][...].astype(FULL)
    for ref in refs[1:-1]:
        total = total + ref[...].astype(FULL)
    refs[-1][...] = total.astype(LOW)


def add_many(values):
    rows, width = values[0].shape
    tile = max(16, rows // 4)
    spec = pl.BlockSpec((tile, width), lambda i: (i, 0))
    return pl.pallas_call(
        add_many_body,
        grid=(rows // tile,),
        in_specs=[spec] * len(values),
        out_specs=spec,
        out_shape=jax.ShapeDtypeStruct((rows, width), LOW),
        compiler_params=params(),
        cost_estimate=LIGHT,
    )(*values)


def ring_add_body(place_ref, arrived_ref, part_ref, out_ref):
    out_ref[...] = (arrived_ref[...].astype(FULL) + part_ref[...].astype(FULL)).astype(out_ref.dtype)


def ring_add(place, arrived, part, kind):
    rows, width = arrived.shape
    return pl.pallas_call(
        ring_add_body,
        grid_spec=pltpu.PrefetchScalarGridSpec(
            num_scalar_prefetch=1,
            grid=(1,),
            in_specs=[
                pl.BlockSpec((rows, width), lambda i, p: (0, 0)),
                pl.BlockSpec((rows, width), lambda i, p: (p[0], 0)),
            ],
            out_specs=pl.BlockSpec((rows, width), lambda i, p: (0, 0)),
        ),
        out_shape=jax.ShapeDtypeStruct((rows, width), kind),
        compiler_params=params(),
        cost_estimate=LIGHT,
    )(place.reshape(1).astype(jnp.int32), arrived, part)


def pair_add_body(count, place_ref, *refs):
    out_ref = refs[-1]
    rows = refs[0].shape[0]
    for half in range(2):
        span = slice(half * rows, (half + 1) * rows)
        total = refs[half][...].astype(FULL)
        if count > 2:
            total = total + refs[2][span].astype(FULL)
        if count > 3:
            total = total + refs[3 + half][...]
        out_ref[span] = total.astype(out_ref.dtype)


def pair_add(place, block_rows, parts, arrived, bases, kind):
    rows, width = 2 * block_rows, parts[0].shape[1]
    block = pl.BlockSpec((rows // 2, width), lambda i, p: (p[0], 0))
    whole = pl.BlockSpec((rows, width), lambda i, p: (0, 0))
    half = pl.BlockSpec((rows // 2, width), lambda i, p: (0, 0))
    operands, in_specs = list(parts), [block, block]
    if arrived is not None:
        operands.append(arrived)
        in_specs.append(whole)
    if bases is not None:
        operands += bases
        in_specs += [half, half]
    return pl.pallas_call(
        functools.partial(pair_add_body, len(operands)),
        grid_spec=pltpu.PrefetchScalarGridSpec(
            num_scalar_prefetch=1, grid=(1,), in_specs=in_specs, out_specs=whole
        ),
        out_shape=jax.ShapeDtypeStruct((rows, width), kind),
        compiler_params=params(),
        cost_estimate=LIGHT,
    )(place.reshape(1).astype(jnp.int32), *operands)


def round_body(count, in_ref, *out_refs):
    rows = in_ref.shape[0] // count
    for index in range(count):
        out_refs[index][...] = in_ref[index * rows : (index + 1) * rows].astype(LOW)


def round_low(value, count):
    rows, width = value.shape
    tile = min(width, 512)
    return pl.pallas_call(
        functools.partial(round_body, count),
        grid=(width // tile,),
        in_specs=[pl.BlockSpec((rows, tile), lambda i: (0, i))],
        out_specs=[pl.BlockSpec((rows // count, tile), lambda i: (0, i))] * count,
        out_shape=[jax.ShapeDtypeStruct((rows // count, width), LOW)] * count,
        compiler_params=params(),
        cost_estimate=LIGHT,
    )(value)


def norm_back_body(count, steps, place_ref, source_ref, arrived_ref, part_ref, gain_ref, *refs):
    bases, out_refs = refs[:count], refs[count:]
    base = bases[0][...]
    if count == 2:
        base = jnp.where(pl.program_id(0) < steps // 2, base, bases[1][...])
    source = source_ref[...].astype(FULL)
    back = arrived_ref[...].astype(FULL) + part_ref[...].astype(FULL)
    inverse = lax.rsqrt(jnp.mean(source * source, axis=-1, keepdims=True) + NORM_EPS)
    normal = source * inverse
    scaled = gain_ref[...] * back
    grad = base + inverse * (scaled - normal * jnp.mean(normal * scaled, axis=-1, keepdims=True))
    out_refs[0][...] = grad
    total = jnp.sum(back * normal, axis=0, keepdims=True)

    @pl.when(pl.program_id(0) == 0)
    def _():
        out_refs[1][...] = total

    @pl.when(pl.program_id(0) > 0)
    def _():
        out_refs[1][...] += total

    if len(out_refs) > 2:
        out_refs[2][...] = grad.astype(LOW)


def norm_back(place, source, arrived, part, gain, bases, base_first, low):
    rows, width = source.shape
    tile = min(rows, 64)
    steps = rows // tile
    row = pl.BlockSpec((tile, width), lambda i, p: (i, 0))
    whole = pl.BlockSpec((1, width), lambda i, p: (0, 0))
    shapes = [jax.ShapeDtypeStruct((rows, width), FULL), jax.ShapeDtypeStruct((1, width), FULL)]
    out_specs = [row, whole]
    if len(bases) == 1:
        base_specs = [pl.BlockSpec((tile, width), lambda i, p: (base_first // tile + i, 0))]
    else:
        base_specs = [
            pl.BlockSpec((tile, width), lambda i, p: (jnp.minimum(i, steps // 2 - 1), 0)),
            pl.BlockSpec((tile, width), lambda i, p: (jnp.maximum(i - steps // 2, 0), 0)),
        ]
    if low:
        shapes.append(jax.ShapeDtypeStruct((rows, width), LOW))
        out_specs.append(row)
    return pl.pallas_call(
        functools.partial(norm_back_body, len(bases), steps),
        grid_spec=pltpu.PrefetchScalarGridSpec(
            num_scalar_prefetch=1,
            grid=(steps,),
            in_specs=[
                row,
                row,
                pl.BlockSpec((tile, width), lambda i, p: (p[0] * steps + i, 0)),
                whole,
            ]
            + base_specs,
            out_specs=out_specs,
        ),
        out_shape=shapes,
        compiler_params=params(),
        cost_estimate=LIGHT,
    )(place.reshape(1).astype(jnp.int32), source, arrived, part, gain, *bases)


def mix_back_body(place_ref, low_ref, weight_ref, *out_refs):
    total = None
    shards, _, _, shard = weight_ref.shape
    for index in range(shards):
        left = low_ref[:, index * shard : (index + 1) * shard]
        product = lax.dot_general(left, weight_ref[index, 0], NT, preferred_element_type=FULL)
        total = product if total is None else total + product
    value = total.astype(LOW)
    for step, out in enumerate(out_refs):

        @pl.when(pl.program_id(0) == step)
        def _():
            out[...] = value


def mix_back(targets, low, weight):
    rows, width = low.shape
    shards, count, cols, shard = weight.shape
    spec = pl.BlockSpec((rows, cols), lambda i, p: (0, 0))
    return pl.pallas_call(
        mix_back_body,
        grid_spec=pltpu.PrefetchScalarGridSpec(
            num_scalar_prefetch=1,
            grid=(count,),
            in_specs=[
                pl.BlockSpec((rows, width), lambda i, p: (0, 0)),
                pl.BlockSpec((shards, 1, cols, shard), lambda i, p: (0, p[i], 0, 0)),
            ],
            out_specs=[spec] * count,
        ),
        out_shape=[jax.ShapeDtypeStruct((rows, cols), LOW)] * count,
        compiler_params=params(),
        cost_estimate=LIGHT,
    )(targets, low, weight)


def project_back_body(place_ref, back_ref, weight_ref, out_ref):
    total = None
    for part in range(3):
        product = lax.dot_general(back_ref[part], weight_ref[part], NT, preferred_element_type=FULL)
        total = product if total is None else total + product
    out_ref[...] = total.astype(LOW)


def project_back(place, back, weight, rows):
    _, width, cols = weight.shape
    tile = min(512, width)
    return pl.pallas_call(
        project_back_body,
        grid_spec=pltpu.PrefetchScalarGridSpec(
            num_scalar_prefetch=1,
            grid=(width // tile,),
            in_specs=[
                pl.BlockSpec((3, rows, cols), lambda i, p: (0, p[0], 0)),
                pl.BlockSpec((3, tile, cols), lambda i, p: (0, i, 0)),
            ],
            out_specs=pl.BlockSpec((rows, tile), lambda i, p: (0, i)),
        ),
        out_shape=jax.ShapeDtypeStruct((rows, width), LOW),
        compiler_params=params(),
        cost_estimate=LIGHT,
    )(place.reshape(1), back, weight)


def adam_step(weight, grad, first, second, factor, rate, decay):
    clipped = grad * factor
    first_new = BETA_ONE * first + (1.0 - BETA_ONE) * clipped
    second_new = BETA_TWO * second + (1.0 - BETA_TWO) * clipped * clipped
    first_hat = first_new / (1.0 - BETA_ONE**STEP)
    second_hat = second_new / (1.0 - BETA_TWO**STEP)
    weight_new = weight - rate * (first_hat / (jnp.sqrt(second_hat) + ADAM_EPS) + decay * weight)
    return (weight_new, weight_new.astype(LOW), first_new, second_new)


def adam_body(rates, factor_ref, *refs):
    count = len(rates)
    factor = factor_ref[0]
    for index, rate in enumerate(rates):
        weight, grad, first, second = refs[4 * index : 4 * index + 4]
        outs = refs[4 * count + 4 * index : 4 * count + 4 * index + 4]
        if len(weight.shape) == 3:
            cols = weight.shape[2]
            for part in range(weight.shape[0]):
                piece = grad[:, part * cols : (part + 1) * cols].astype(FULL)
                new = adam_step(weight[part], piece, first[part], second[part], factor, rate, DECAY_RATE)
                for out, value in zip(outs, new):
                    out[part] = value
        else:
            new = adam_step(weight[...], grad[...].astype(FULL), first[...], second[...], factor, rate, DECAY_RATE)
            for out, value in zip(outs, new):
                out[...] = value


def adam_all(factor, groups, rates):
    steps = 8
    for weight, _, _, _ in groups:
        steps = min(steps, weight.shape[-2] // 16)
    in_specs, out_specs, shapes, operands = [], [], [], []
    for weight, grad, first, second in groups:
        rows, cols = weight.shape[-2] // steps, weight.shape[-1]
        if weight.ndim == 3:
            spec = pl.BlockSpec((weight.shape[0], rows, cols), lambda i, f: (0, i, 0))
        else:
            spec = pl.BlockSpec((rows, cols), lambda i, f: (i, 0))
        grad_spec = pl.BlockSpec((rows, grad.shape[1]), lambda i, f: (i, 0))
        in_specs += [spec, grad_spec, spec, spec]
        out_specs += [spec] * 4
        operands += [weight, grad, first, second]
        for kind in (FULL, LOW, FULL, FULL):
            shapes.append(jax.ShapeDtypeStruct(weight.shape, kind))
    out = pl.pallas_call(
        functools.partial(adam_body, rates),
        grid_spec=pltpu.PrefetchScalarGridSpec(
            num_scalar_prefetch=1, grid=(steps,), in_specs=in_specs, out_specs=out_specs
        ),
        out_shape=shapes,
        compiler_params=params(),
        cost_estimate=LIGHT,
    )(factor.reshape(1), *operands)
    return [tuple(out[4 * index : 4 * index + 4]) for index in range(len(groups))]


def lay_body(spots, me_ref, *refs):
    count = len(spots)
    out_ref = refs[count]
    for piece, spot in zip(refs, spots):
        if isinstance(spot, tuple):
            rows = piece.shape[0]
            out_ref[me_ref[0] ^ spot[0], spot[1] * rows : (spot[1] + 1) * rows] = piece[...]
        else:
            out_ref[lax.rem(me_ref[0] + count - spot, count)] = piece[...]


def lay(me, pieces, spots):
    rows, width = pieces[0].shape
    if isinstance(spots[0], tuple):
        shape = (len(pieces) // 2, 2 * rows, width)
    else:
        shape = (len(pieces), rows, width)
    return pl.pallas_call(
        functools.partial(lay_body, spots),
        in_specs=[pl.BlockSpec(memory_space=pltpu.SMEM)] + [pl.BlockSpec(memory_space=pltpu.VMEM)] * len(pieces),
        out_specs=pl.BlockSpec(memory_space=pltpu.VMEM),
        out_shape=jax.ShapeDtypeStruct(shape, LOW),
        compiler_params=params(),
        cost_estimate=LIGHT,
    )(me.reshape(1).astype(jnp.int32), *pieces)


def lay_cores_body(core_ref, mine_ref, other_ref, out_ref):
    mine, other = mine_ref[...], other_ref[...]
    out_ref[0, 0] = jnp.where(core_ref[0] == 0, mine, other)[0]
    out_ref[0, 1] = jnp.where(core_ref[0] == 0, other, mine)[0]


def lay_cores(core, mine, other):
    chips, rows, width = mine.shape
    spec = pl.BlockSpec((1, rows, width), lambda i, c: (i, 0, 0))
    return pl.pallas_call(
        lay_cores_body,
        grid_spec=pltpu.PrefetchScalarGridSpec(
            num_scalar_prefetch=1,
            grid=(chips,),
            in_specs=[spec, spec],
            out_specs=pl.BlockSpec((1, 2, rows, width), lambda i, c: (i, 0, 0, 0)),
        ),
        out_shape=jax.ShapeDtypeStruct((chips, 2, rows, width), LOW),
        compiler_params=params(),
        cost_estimate=LIGHT,
    )(core, mine, other)


def squares(value):
    wide = value.astype(FULL)
    return jnp.sum(wide * wide)


def after(value, *others):
    if not others:
        return value
    return lax.optimization_barrier((value, *others))[0]


def per_device(
    chips,
    cores,
    bkts,
    block_in,
    cotangent,
    buckets,
    qkv_weight,
    qkv_first,
    qkv_second,
    out_weight,
    out_first,
    out_second,
    up_weight,
    up_first,
    up_second,
    down_weight,
    down_first,
    down_second,
    norm_gains,
    gains_first,
    gains_second,
):
    toks = chips * cores
    tok = ("chip", "core")
    group = lax.axis_index("bkt")
    core = lax.axis_index("core")
    chip = lax.axis_index("chip")
    core_id = core.reshape(1).astype(jnp.int32)
    rows, width = block_in.shape
    half = rows // 2
    length = rows * bkts
    ring = [(i, (i + 1) % bkts) for i in range(bkts)]

    last = []

    def at(value, *others):
        return after(value, *last, *others)

    def did(value):
        last[:] = [value]
        return value

    def wait(value):
        return did(after(value, *last))

    def pass_on(name, value, *others):
        with jax.named_scope(name):
            return lax.ppermute(at(value, *others), "bkt", ring)

    def owner(step):
        return lax.rem(group - step + bkts, bkts)

    places = jnp.stack([owner(step) for step in range(bkts)]).astype(jnp.int32)

    def rows_of(value, step):
        size = value.shape[0] // bkts
        return lax.dynamic_slice_in_dim(value, owner(step) * size, size, 0)

    def add(arrived, value, step):
        return did(ring_add(owner(step), at(arrived), value, LOW))

    def add_final(arrived, value):
        return did(ring_add(owner(0), at(arrived), value, FULL))

    def swap(name, values):
        with jax.named_scope(name + "_swap"):
            return [lax.ppermute(at(value), "core", [(0, 1), (1, 0)]) for value in values]

    def core_add(kept, arrived):
        return did(core_add_kernel(at(kept), arrived))

    def chip_sum(value):
        value = value.reshape(chips * value.shape[1], *value.shape[2:])
        return lax.psum_scatter(value, "chip", scatter_dimension=0, tiled=True)

    by_bits = chips & (chips - 1) == 0

    qkv_full = lax.all_gather(did(qkv_weight.astype(LOW)), tok, axis=1, tiled=True)
    x_held = [block_in, pass_on("x1", block_in)]
    (out_low,) = round_low(at(out_weight), 1)
    did(out_low)
    x_held[1] = wait(x_held[1])
    x_held.append(pass_on("x2", x_held[1]))
    out_held = [out_low, pass_on("out1", out_low)]
    (up_low,) = round_low(at(up_weight), 1)
    up_full = lax.all_gather(did(up_low), tok, axis=0, tiled=True)
    gain_width = norm_gains.shape[1]
    gain_line = jnp.zeros((toks, 2, gain_width), FULL)
    gain_line = lax.dynamic_update_slice(
        gain_line, norm_gains.astype(LOW).astype(FULL)[None], (lax.axis_index(tok), 0, 0)
    )
    if by_bits:
        for axis, size in (("core", cores), ("chip", chips)):
            for bit in range(size.bit_length() - 1):
                perm = [(i, i ^ (1 << bit)) for i in range(size)]
                with jax.named_scope("gains"):
                    gain_line = did(gain_line + lax.ppermute(at(gain_line), axis, perm))
    else:
        gain_line = did(lax.psum(at(gain_line), tok))
    gain_float = did(gain_line.transpose(1, 0, 2).reshape(2, width))
    cosine, sine = rotary_tables(length)
    for step in range(3, bkts):
        x_held[-1] = wait(x_held[-1])
        out_held[-1] = wait(out_held[-1])
        x_held.append(pass_on("x" + str(step), x_held[-1], cosine, sine))
        out_held.append(pass_on("out" + str(step - 1), out_held[-1]))

    carried = None
    for step in range(bkts - 1):
        carried = project(
            owner(step).reshape(1), at(x_held[step]), gain_float[0:1], qkv_full, cosine, sine, carried
        )
        did(carried[0])
    x_held[-1] = wait(x_held[-1])
    out_held[-1] = wait(out_held[-1])
    out_held.append(pass_on("out" + str(bkts - 1), out_held[-1]))
    normed_one, qkv, seq_in = project(
        owner(bkts - 1).reshape(1), at(x_held[-1]), gain_float[0:1], qkv_full, cosine, sine, carried
    )
    did(normed_one)
    out_held[-1] = wait(out_held[-1])
    out_depth, out_width = out_weight.shape
    out_line = did(lay(group, [at(out_held[0])] + out_held[1:], list(range(bkts))))
    out_full = lax.all_gather(after(out_line, up_full), tok, axis=0, tiled=False)
    (down_low,) = round_low(at(down_weight), 1)
    down_full = lax.all_gather(did(down_low), tok, axis=1, tiled=True)
    cols = qkv.shape[2]
    seq_in = seq_in.reshape(bkts, rows, width)

    slab, log_a = attend(0, bkts, at(qkv), cotangent)
    slabs = [[did(slab)], []]

    def next_slab(part):
        held = slabs[part]
        if len(held) > 1:
            held[-1] = wait(held[-1])
        held.append(pass_on("slab" + "ab"[part] + str(len(held)), held[-1]))

    next_slab(0)
    slab, log_b = attend(1, bkts, at(qkv), cotangent)
    slabs[1].append(did(slab))
    logs = [log_a, log_b]
    for step in range(2, bkts):
        next_slab(0)
    slabs[0][-1] = wait(slabs[0][-1])
    for step in range(1, bkts - 2):
        next_slab(1)

    live = (buckets >= group).astype(FULL)
    acc = did(mix_first(0, places, at(seq_in), slabs[0][:-1], out_full))
    normed_a, middle_a, mixed_a = mix_last(places, acc, gain_float[1:2], slabs[0], out_full)
    did(normed_a)
    next_slab(1)
    hidden_a, inner_a, low_a = hidden_units(places, live, at(normed_a), up_full, down_full, slabs[0])
    did(inner_a)
    next_slab(1)
    back_a = did(product(at(inner_a), up_full, True))
    sum_a = did(rows_of(back_a, 1))
    arrived_a = pass_on("sum_a1", sum_a)
    acc = did(mix_first(1, places, at(seq_in), slabs[1][:-1], out_full))
    prod_a = did(product(at(hidden_a), down_full, False))
    slabs[1][-1] = wait(slabs[1][-1])
    normed_b, middle_b, mixed_b = mix_last(places, at(acc), gain_float[1:2], slabs[1], out_full)
    did(normed_b)
    sum_a = add(arrived_a, back_a, 2)
    arrived_a = pass_on("sum_a2", sum_a)

    hidden_b, inner_b, low_b = hidden_units(places, live, at(normed_b), up_full, down_full, slabs[1])
    did(inner_b)
    sum_a = add(arrived_a, back_a, 3)
    arrived_a = pass_on("sum_a3", sum_a)
    back_b = did(product(at(inner_b), up_full, True))
    prod_b = did(product(at(hidden_b), down_full, False))
    arrived_a = wait(arrived_a)
    sum_b = did(rows_of(at(back_b), 1))
    arrived_b = pass_on("sum_b1", sum_b)

    first = jnp.zeros((), jnp.int32)
    targets = jnp.stack([lax.rem(group + step, bkts) for step in range(bkts)]).astype(jnp.int32)

    def middle_back(part, middle, arrived, back):
        grad, gain_sum, low = norm_back(
            owner(0), middle, at(arrived), back, gain_float[1:2], [cotangent], part * half, True
        )
        found = list(mix_back(targets, low, out_full))
        did(found[0])
        return grad, low, gain_sum, found

    def exchange(part, found):
        with jax.named_scope("exchange" + str(part)):
            for step in range(1, bkts):
                found[step] = lax.ppermute(
                    at(found[step]), "bkt", [(i, (i + step) % bkts) for i in range(bkts)]
                )

    grad_a, mid_low_a, gain_a, pieces_a = middle_back(0, middle_a, arrived_a, back_a)
    sum_b = add(arrived_b, back_b, 2)
    exchange(0, pieces_a)
    arrived_b = pass_on("sum_b2", sum_b)
    up_kept, up_sent = weight_grad(core_id, [normed_a, normed_b], [at(inner_a), inner_b], chips, 0)
    did(up_kept)
    pieces_a = pieces_a[:1] + [wait(piece) for piece in pieces_a[1:]]
    sum_b = add(arrived_b, back_b, 3)
    up_arrived = swap("up_grad", up_sent)
    arrived_b = pass_on("sum_b3", sum_b)
    down_kept, down_sent = weight_grad(core_id, [hidden_a, hidden_b], [at(low_a), low_b], chips, 1)
    did(down_kept)
    arrived_b = wait(arrived_b)
    up_core = core_add(up_kept, up_arrived)
    up_part = chip_sum(up_core)
    grad_b, mid_low_b, gain_b, pieces_b = middle_back(1, middle_b, arrived_b, back_b)
    exchange(1, pieces_b)
    out_kept, out_sent = weight_grad(
        core_id, [at(mixed_a), mixed_b], [mid_low_a, mid_low_b], chips, 1
    )
    did(out_kept)
    prods = [prod_a, prod_b]
    ffn = did(pair_add(owner(1), half, [at(prod_a), prod_b], None, None, LOW))
    pieces_b = pieces_b[:1] + [wait(piece) for piece in pieces_b[1:]]
    down_arrived = swap("down_grad", down_sent)
    out_arrived = swap("out_grad", out_sent)
    arrived_f = pass_on("ffn1", ffn)

    back_project = did(attend_back(places, at(qkv), pieces_a + pieces_b, logs, cosine, sine))
    total = did(project_back(owner(1), at(back_project), qkv_full, rows))
    arrived_f = wait(arrived_f)
    down_core = core_add(down_kept, down_arrived)
    down_part = chip_sum(down_core)
    direct = chips <= 4 and by_bits

    def out_plane(mask):
        with jax.named_scope("out_plane"):
            out_apart[mask] = lax.ppermute(
                at(out_apart[mask]), "chip", [(i, i ^ mask) for i in range(chips)]
            )

    if direct:
        out_apart = list(core_add_apart(chip, at(out_kept), out_arrived))
        did(out_apart[0])
        for mask in range(1, chips):
            if mask & (mask - 1) == 0:
                out_plane(mask)
    else:
        out_sum = chip_sum(core_add(out_kept, out_arrived))
    arrived = pass_on("back1", total)
    qkv_kept, qkv_sent = project_grad(core_id, normed_one, at(back_project), chips)
    did(qkv_kept)
    own = did(project_back(owner(2), at(back_project), qkv_full, rows))
    total = did(ring_add(first, at(arrived), own, LOW))
    if direct:
        for mask in range(1, chips):
            if mask & (mask - 1) == 0:
                out_apart[mask] = wait(out_apart[mask])
            else:
                out_plane(mask)
    qkv_arrived = swap("qkv_grad", qkv_sent)
    arrived = pass_on("back2", total)
    own = did(project_back(owner(3), at(back_project), qkv_full, rows))
    qkv_core = core_add(qkv_kept, qkv_arrived)
    qkv_part = chip_sum(qkv_core)
    last_own = did(project_back(owner(0), at(back_project), qkv_full, rows))
    total = did(ring_add(first, at(arrived), own, LOW))
    if direct:
        out_sum = add_many([at(out_apart[0])] + out_apart[1:])
    did(out_sum)
    arrived = pass_on("back3", total)
    arrived_out = pass_on("out_sum1", rows_of(out_sum, 1))
    for step in range(2, bkts):
        arrived_out = pass_on("out_sum" + str(step), add(arrived_out, out_sum, step))
    out_part = add_final(arrived_out, out_sum)
    out_squares = did(squares(at(out_part)))
    block_in_grad, gain_one = norm_back(
        first, block_in, at(arrived), last_own, gain_float[0:1], [grad_a, grad_b], 0, False
    )
    did(gain_one)
    ffn = did(pair_add(owner(2), half, prods, at(arrived_f), None, LOW))
    arrived_f = pass_on("ffn2", ffn)
    up_squares = did(squares(at(up_part)))
    down_squares = did(squares(at(down_part)))
    gain_grad_one = gain_one[0]
    gain_grad_two = (gain_a + gain_b)[0]

    weight_squares = did(up_squares + down_squares + out_squares + squares(at(qkv_part)))
    packed = jnp.concatenate(
        [gain_grad_one, gain_grad_two, jnp.broadcast_to(weight_squares, (HD,))]
    )
    for axis, size in (("core", cores), ("chip", chips), ("bkt", bkts)):
        if size & (size - 1):
            packed = lax.psum(packed, axis)
        else:
            step = 1
            while step < size:
                packed = packed + lax.ppermute(packed, axis, [(i, i ^ step) for i in range(size)])
                step *= 2
    did(packed)
    ffn = did(pair_add(owner(3), half, prods, at(arrived_f), None, LOW))
    arrived_f = pass_on("ffn3", ffn)
    gain_total = packed[: 2 * width].reshape(2, width)
    grad_norm = jnp.sqrt(packed[2 * width] + jnp.sum(gain_total * gain_total))
    factor = jnp.minimum(1.0, CLIP_NORM / grad_norm)
    gain_part = lax.dynamic_slice_in_dim(gain_total, lax.axis_index(tok) * gain_width, gain_width, 1)
    updated = adam_all(
        factor,
        [
            (qkv_weight, qkv_part, qkv_first, qkv_second),
            (out_weight, out_part, out_first, out_second),
            (up_weight, up_part, up_first, up_second),
            (down_weight, down_part, down_first, down_second),
        ],
        (D ** (-0.5), (H * HD // 16) ** (-0.5), D ** (-0.5), FF ** (-0.5)),
    )
    block_out = pair_add(
        owner(0), half, prods, after(arrived_f, updated[0][0]), [middle_a, middle_b], FULL
    )
    gain_out = adam_step(norm_gains, gain_part, gains_first, gains_second, factor, GAIN_RATE, 0.0)
    return (block_out, block_in_grad, grad_norm, *[value for new in updated for value in new], *gain_out)


def solution(mesh):
    toks, bkts = mesh.shape["tok"], mesh.shape["bkt"]
    cores = 2
    chips = toks // cores
    tok = ("chip", "core")
    rows = P(("chip", "core", "bkt"), None)
    qkv = P(None, tok, "bkt")
    tall = P("bkt", tok)
    wide = P(tok, "bkt")
    gains = P(None, tok)
    return jax.shard_map(
        functools.partial(per_device, chips, cores, bkts),
        mesh=Mesh(mesh.devices.reshape(chips, cores, bkts), ("chip", "core", "bkt")),
        in_specs=(rows, rows, P(tok), *[qkv] * 3, *[tall] * 3, *[wide] * 3, *[tall] * 3, *[gains] * 3),
        out_specs=(rows, rows, P(), *[qkv] * 4, *[tall] * 4, *[wide] * 4, *[tall] * 4, *[gains] * 4),
        check_vma=False,
    )
```

```python
import functools
import jax
import jax.numpy as jnp
from jax import lax
from jax.experimental import pallas as pl
from jax.experimental.pallas import tpu as pltpu
from jax.sharding import Mesh, PartitionSpec as P

D = 2048
H = 16
HD = 128
FF = 8192
STEP = 10

NORM_EPS = 1e-05
ADAM_EPS = 1e-08
CLIP_NORM = 1.0
BETA_ONE = 0.9
BETA_TWO = 0.95
DECAY_RATE = 0.1
GAIN_RATE = 0.3
ROPE_BASE = 10000.0

LOW = jnp.bfloat16
FULL = jnp.float32
SCALE = HD ** (-0.5)
VMEM_BYTES = 48 * 1024 * 1024
NN = (((1,), (0,)), ((), ()))
NT = (((1,), (1,)), ((), ()))
TN = (((0,), (0,)), ((), ()))


def rotary_tables(length):
    positions = jnp.arange(length).astype(FULL)[:, None]
    freq_index = jnp.arange(HD // 2).astype(FULL)
    angles = positions * (ROPE_BASE ** (-2.0 * freq_index / HD))[None, :]
    cosine = jnp.cos(angles)
    sine = jnp.sin(angles)
    return (jnp.concatenate([cosine, cosine], axis=-1), jnp.concatenate([-sine, sine], axis=-1))


LIGHT = pl.CostEstimate(flops=1, bytes_accessed=1, transcendentals=0)


def params(vmem=VMEM_BYTES):
    return pltpu.CompilerParams(vmem_limit_bytes=vmem)


def project_body(place_ref, x_ref, gain_ref, w_ref, cos_ref, sin_ref, *rest):
    normed_ref, out_ref, seq_ref = rest[-3:]
    part = pl.program_id(0)

    @pl.when(part == 0)
    def _():
        low = x_ref[...]
        seq_ref[...] = low
        values = low.astype(FULL)
        inverse = lax.rsqrt(jnp.mean(values * values, axis=-1, keepdims=True) + NORM_EPS)
        normed_ref[...] = (values * inverse * gain_ref[...]).astype(LOW)

    product = jnp.dot(normed_ref[...], w_ref[0], preferred_element_type=FULL)

    @pl.when(part < 2)
    def _():
        for head in range(product.shape[1] // HD):
            one = product[:, head * HD : (head + 1) * HD]
            turned = one * cos_ref[...] + pltpu.roll(one, HD // 2, 1) * sin_ref[...]
            out_ref[0, :, head * HD : (head + 1) * HD] = turned.astype(LOW)

    @pl.when(part == 2)
    def _():
        out_ref[0] = product.astype(LOW)


def project(place, x, gain, weight, cosine, sine, carried):
    rows, width = x.shape
    length = cosine.shape[0]
    cols = weight.shape[2]
    shapes = [
        jax.ShapeDtypeStruct((length, width), LOW),
        jax.ShapeDtypeStruct((3, length, cols), LOW),
        jax.ShapeDtypeStruct((length, width), LOW),
    ]
    in_specs = [
        pl.BlockSpec((rows, width), lambda c, p: (0, 0)),
        pl.BlockSpec((1, width), lambda c, p: (0, 0)),
        pl.BlockSpec((1, width, cols), lambda c, p: (c, 0, 0)),
        pl.BlockSpec((rows, HD), lambda c, p: (p[0], 0)),
        pl.BlockSpec((rows, HD), lambda c, p: (p[0], 0)),
    ]
    aliases = {}
    if carried is not None:
        in_specs += [pl.BlockSpec(memory_space=pl.ANY)] * 3
        aliases = {6: 0, 7: 1, 8: 2}
    return pl.pallas_call(
        project_body,
        grid_spec=pltpu.PrefetchScalarGridSpec(
            num_scalar_prefetch=1,
            grid=(3,),
            in_specs=in_specs,
            out_specs=[
                pl.BlockSpec((rows, width), lambda c, p: (p[0], 0)),
                pl.BlockSpec((1, rows, cols), lambda c, p: (c, p[0], 0)),
                pl.BlockSpec((rows, width), lambda c, p: (p[0], 0)),
            ],
        ),
        out_shape=shapes,
        input_output_aliases=aliases,
        compiler_params=params(),
        cost_estimate=LIGHT,
    )(place, x, gain, weight, cosine, sine, *(carried or ()))


def attend_body(half, blocks, count, q_ref, k_ref, v_ref, *rest):
    cotangents, (ring_ref, log_ref) = rest[:count], rest[count:]
    length = q_ref.shape[1]
    block = length // blocks
    rows = block // 2
    for index in range(count):
        first = length // 2 + index * rows
        ring_ref[first : first + rows] = cotangents[index][...].astype(LOW)
    for index in range(blocks):
        first = index * block + half * rows
        last = first + rows
        query = q_ref[0, first:last]
        scores = (
            lax.dot_general(query, k_ref[0, :last], NT, preferred_element_type=FULL) * SCALE
        )
        row = lax.broadcasted_iota(jnp.int32, scores.shape, 0) + first
        col = lax.broadcasted_iota(jnp.int32, scores.shape, 1)
        scores = jnp.where(row >= col, scores, -1e30)
        peak = jnp.max(scores, axis=-1, keepdims=True)
        expo = jnp.exp(scores - peak)
        total = jnp.sum(expo, axis=-1, keepdims=True)
        probs = (expo / total).astype(LOW)
        mixed = jnp.dot(probs, v_ref[0, :last], preferred_element_type=FULL)
        ring_ref[index * rows : (index + 1) * rows] = mixed.astype(LOW)
        log_ref[index * rows : (index + 1) * rows] = jnp.broadcast_to(
            peak + jnp.log(total), (rows, HD)
        )


def attend(half, blocks, qkv, cotangent):
    _, length, cols = qkv.shape
    heads = cols // HD
    rows, width = cotangent.shape
    count = width // cols

    def cotangent_spec(index):
        return pl.BlockSpec((rows // 2, HD), lambda h: (half, index * heads + h))

    return pl.pallas_call(
        functools.partial(attend_body, half, blocks, count),
        grid=(heads,),
        in_specs=[
            pl.BlockSpec((1, length, HD), lambda h: (0, 0, h)),
            pl.BlockSpec((1, length, HD), lambda h: (1, 0, h)),
            pl.BlockSpec((1, length, HD), lambda h: (2, 0, h)),
        ]
        + [cotangent_spec(index) for index in range(count)],
        out_specs=[
            pl.BlockSpec((length // 2 + count * rows // 2, HD), lambda h: (0, h)),
            pl.BlockSpec((length // 2, HD), lambda h: (0, h)),
        ],
        out_shape=[
            jax.ShapeDtypeStruct((length // 2 + count * rows // 2, cols), LOW),
            jax.ShapeDtypeStruct((length // 2, cols), FULL),
        ],
        compiler_params=params(),
        cost_estimate=LIGHT,
    )(qkv, qkv, qkv, *[cotangent] * count)


def attend_back_body(blocks, place_ref, q_ref, k_ref, v_ref, log_a_ref, log_b_ref, cos_ref, sin_ref, *rest):
    pieces = rest[: 2 * blocks]
    out_ref, key_acc, value_acc, back_ref = rest[2 * blocks :]
    length = q_ref.shape[1]
    block = length // blocks
    rows = block // 2
    for half in range(2):
        for step in range(blocks):
            first = pl.multiple_of(place_ref[step] * block + half * rows, rows)
            back_ref[pl.ds(first, rows), :] = pieces[half * blocks + step][...]

    def turn_back(one, cosine, sine):
        return one * cosine - pltpu.roll(one, HD // 2, 1) * sine

    for index in range(blocks):
        first, last = index * block, (index + 1) * block
        query = q_ref[0, first:last]
        back = back_ref[first:last]
        keys = k_ref[0, :last]
        log_total = jnp.concatenate(
            [
                log_a_ref[index * rows : (index + 1) * rows, :1],
                log_b_ref[index * rows : (index + 1) * rows, :1],
            ],
            axis=0,
        )
        scores = lax.dot_general(query, keys, NT, preferred_element_type=FULL) * SCALE
        row = lax.broadcasted_iota(jnp.int32, scores.shape, 0) + first
        col = lax.broadcasted_iota(jnp.int32, scores.shape, 1)
        probs = jnp.exp(jnp.where(row >= col, scores, -1e30) - log_total)
        back_probs = lax.dot_general(back, v_ref[0, :last], NT, preferred_element_type=FULL)
        centre = jnp.sum(probs * back_probs, axis=-1, keepdims=True)
        back_scores = (probs * (back_probs - centre)).astype(LOW)
        query_grad = jnp.dot(back_scores, keys, preferred_element_type=FULL) * SCALE
        out_ref[0, first:last] = turn_back(query_grad, cos_ref[first:last], sin_ref[first:last]).astype(LOW)
        key_part = lax.dot_general(back_scores, query, TN, preferred_element_type=FULL)
        value_part = lax.dot_general(probs.astype(LOW), back, TN, preferred_element_type=FULL)
        if index > 0:
            key_acc[:first] += key_part[:first]
            value_acc[:first] += value_part[:first]
        key_acc[first:last] = key_part[first:]
        value_acc[first:last] = value_part[first:]
    out_ref[1] = turn_back(key_acc[...] * SCALE, cos_ref[...], sin_ref[...]).astype(LOW)
    out_ref[2] = value_acc[...].astype(LOW)


def attend_back(places, qkv, pieces, logs, cosine, sine):
    _, length, cols = qkv.shape
    heads = cols // HD
    blocks = len(pieces) // 2
    column = lambda h, p: (0, h)
    return pl.pallas_call(
        functools.partial(attend_back_body, blocks),
        grid_spec=pltpu.PrefetchScalarGridSpec(
            num_scalar_prefetch=1,
            grid=(heads,),
            in_specs=[
                pl.BlockSpec((1, length, HD), lambda h, p: (0, 0, h)),
                pl.BlockSpec((1, length, HD), lambda h, p: (1, 0, h)),
                pl.BlockSpec((1, length, HD), lambda h, p: (2, 0, h)),
                pl.BlockSpec((length // 2, HD), column),
                pl.BlockSpec((length // 2, HD), column),
                pl.BlockSpec((length, HD), lambda h, p: (0, 0)),
                pl.BlockSpec((length, HD), lambda h, p: (0, 0)),
            ]
            + [pl.BlockSpec((length // blocks // 2, HD), column)] * (2 * blocks),
            out_specs=pl.BlockSpec((3, length, HD), lambda h, p: (0, 0, h)),
            scratch_shapes=[
                pltpu.VMEM((length, HD), FULL),
                pltpu.VMEM((length, HD), FULL),
                pltpu.VMEM((length, HD), LOW),
            ],
        ),
        out_shape=jax.ShapeDtypeStruct((3, length, cols), LOW),
        compiler_params=params(),
        cost_estimate=LIGHT,
    )(places, qkv, qkv, qkv, logs[0], logs[1], cosine, sine, *pieces)


def mix_first_body(count, place_ref, seq_ref, *rest):
    slabs, weights, acc_ref = rest[:count], rest[count : 2 * count], rest[2 * count]
    blocks, rows, width = seq_ref.shape
    shards, _, _, shard = weights[0].shape
    for index in range(shards):
        span = slice(index * shard, (index + 1) * shard)
        total = seq_ref[:, :, span].reshape(blocks * rows, shard).astype(FULL)
        for slab, weight in zip(slabs, weights):
            total = total + jnp.dot(slab[...], weight[index, 0], preferred_element_type=FULL)
        acc_ref[:, span] = total


def mix_first(part, places, seq_in, slabs, weight):
    blocks, block, width = seq_in.shape
    half = block // 2
    shards, _, cols, shard = weight.shape
    tile = max(1, 512 // shard)
    count = len(slabs)

    def weight_spec(step):
        return pl.BlockSpec((tile, 1, cols, shard), lambda i, p: (i, p[step], 0, 0))

    return pl.pallas_call(
        functools.partial(mix_first_body, count),
        grid_spec=pltpu.PrefetchScalarGridSpec(
            num_scalar_prefetch=1,
            grid=(shards // tile,),
            in_specs=[pl.BlockSpec((blocks, half, tile * shard), lambda i, p: (0, part, i))]
            + [pl.BlockSpec((blocks * half, cols), lambda i, p: (0, 0))] * count
            + [weight_spec(step) for step in range(count)],
            out_specs=pl.BlockSpec((blocks * half, tile * shard), lambda i, p: (0, i)),
        ),
        out_shape=jax.ShapeDtypeStruct((blocks * half, width), FULL),
        compiler_params=params(),
        cost_estimate=LIGHT,
    )(places, seq_in, *slabs, *[weight] * count)


def mix_last_body(count, place_ref, acc_ref, gain_ref, weight_ref, *rest):
    slabs = rest[:count]
    normed_ref, middle_ref, mixed_ref = rest[count:]
    cols = slabs[0].shape[1]
    slab = slabs[-1][...]
    parts = [
        jnp.dot(slab, weight_ref[index, 0], preferred_element_type=FULL)
        for index in range(weight_ref.shape[0])
    ]
    middle = acc_ref[...] + jnp.concatenate(parts, axis=1)
    inverse = lax.rsqrt(jnp.mean(middle * middle, axis=-1, keepdims=True) + NORM_EPS)
    normed_ref[...] = (middle * inverse * gain_ref[...]).astype(LOW)

    @pl.when(pl.program_id(0) == place_ref[0])
    def _():
        middle_ref[...] = middle
        for step in range(count):
            first = pl.multiple_of(place_ref[step] * cols, cols)
            mixed_ref[:, pl.ds(first, cols)] = slabs[step][...]


def mix_last(places, acc, gain, slabs, weight):
    length, width = acc.shape
    shards, count, cols, shard = weight.shape
    rows = length // count
    return pl.pallas_call(
        functools.partial(mix_last_body, count),
        grid_spec=pltpu.PrefetchScalarGridSpec(
            num_scalar_prefetch=1,
            grid=(count,),
            in_specs=[
                pl.BlockSpec((rows, width), lambda i, p: (i, 0)),
                pl.BlockSpec((1, width), lambda i, p: (0, 0)),
                pl.BlockSpec((shards, 1, cols, shard), lambda i, p: (0, p[count - 1], 0, 0)),
            ]
            + [pl.BlockSpec((rows, cols), lambda i, p: (i, 0))] * count,
            out_specs=[
                pl.BlockSpec((rows, width), lambda i, p: (i, 0)),
                pl.BlockSpec((rows, width), lambda i, p: (0, 0)),
                pl.BlockSpec((rows, count * cols), lambda i, p: (0, 0)),
            ],
        ),
        out_shape=[
            jax.ShapeDtypeStruct((length, width), LOW),
            jax.ShapeDtypeStruct((rows, width), FULL),
            jax.ShapeDtypeStruct((rows, count * cols), LOW),
        ],
        compiler_params=params(),
        cost_estimate=LIGHT,
    )(places, acc, gain, weight, *slabs)


def hidden_body(count, place_ref, live_ref, normed_ref, up_ref, down_ref, *rest):
    pieces = rest[:count]
    hidden_ref, inner_ref, back_ref = rest[count:]
    cols = pieces[0].shape[1]
    rows = pieces[0].shape[0] * cols // back_ref.shape[1]

    @pl.when(pl.program_id(0) == 0)
    def _():
        for step in range(count):
            first = pl.multiple_of(place_ref[step] * rows, rows)
            for index in range(pieces[0].shape[0] // rows):
                span = slice(index * rows, (index + 1) * rows)
                back_ref[pl.ds(first, rows), index * cols : (index + 1) * cols] = pieces[step][span]

    inner = jnp.dot(normed_ref[...], up_ref[...], preferred_element_type=FULL)
    inner = jnp.maximum(inner, 0.0) * live_ref[0]
    hidden_ref[...] = (inner * inner).astype(LOW)
    back = lax.dot_general(back_ref[...], down_ref[...], NT, preferred_element_type=FULL)
    inner_ref[...] = (back * 2.0 * inner).astype(LOW)


def hidden_units(places, live, normed, up, down, pieces):
    length, width = normed.shape
    units = up.shape[1]
    tile = min(512, units)
    count = len(pieces)
    cols = pieces[0].shape[1]
    below = pieces[0].shape[0] - length
    whole = lambda i, p, l: (0, 0)
    column = lambda i, p, l: (0, i)
    return pl.pallas_call(
        functools.partial(hidden_body, count),
        grid_spec=pltpu.PrefetchScalarGridSpec(
            num_scalar_prefetch=2,
            grid=(units // tile,),
            in_specs=[
                pl.BlockSpec((length, width), whole),
                pl.BlockSpec((width, tile), column),
                pl.BlockSpec((tile, width), lambda i, p, l: (i, 0)),
            ]
            + [pl.BlockSpec((below, cols), lambda i, p, l: (length // below, 0))] * count,
            out_specs=[
                pl.BlockSpec((length, tile), column),
                pl.BlockSpec((length, tile), column),
                pl.BlockSpec((length, width), whole),
            ],
        ),
        out_shape=[
            jax.ShapeDtypeStruct((length, units), LOW),
            jax.ShapeDtypeStruct((length, units), LOW),
            jax.ShapeDtypeStruct((length, width), LOW),
        ],
        compiler_params=params(),
        cost_estimate=LIGHT,
    )(places, live, normed, up, down, *pieces)


def product_body(dims, left_ref, right_ref, out_ref):
    out_ref[...] = lax.dot_general(
        left_ref[...], right_ref[...], dims, preferred_element_type=FULL
    ).astype(LOW)


def product(left, right, turned):
    length, depth = left.shape
    width = right.shape[0] if turned else right.shape[1]
    tile = min(512, width)
    if turned:
        spec = pl.BlockSpec((tile, depth), lambda i: (i, 0))
    else:
        spec = pl.BlockSpec((depth, tile), lambda i: (0, i))
    return pl.pallas_call(
        functools.partial(product_body, NT if turned else NN),
        grid=(width // tile,),
        in_specs=[pl.BlockSpec((length, depth), lambda i: (0, 0)), spec],
        out_specs=pl.BlockSpec((length, tile), lambda i: (0, i)),
        out_shape=jax.ShapeDtypeStruct((length, width), LOW),
        compiler_params=params(),
        cost_estimate=LIGHT,
    )(left, right)


def split_shards(core, total, axis, first, kept_ref, sent_refs):
    shard = kept_ref.shape[1 + axis]
    count = total.shape[axis] // (2 * shard)

    def cut(index):
        span = slice(index * shard, (index + 1) * shard)
        return total[span] if axis == 0 else total[:, span]

    for index in range(count):
        even, odd = cut(2 * index), cut(2 * index + 1)
        kept_ref[index] = jnp.where(core == 0, even, odd).astype(LOW)
        sent = jnp.where(core == 0, odd, even).astype(LOW)
        if axis == 1:
            sent_refs[index][...] = sent
        else:
            for chip in range(index, len(sent_refs), count):

                @pl.when(first + index == chip)
                def _():
                    sent_refs[chip][...] = sent


def grad_body(count, axis, core_ref, *refs):
    total = None
    for index in range(count):
        product = lax.dot_general(
            refs[index][...], refs[count + index][...], TN, preferred_element_type=FULL
        )
        total = product if total is None else total + product
    kept_ref, sent_refs = refs[2 * count], refs[2 * count + 1 :]
    first = pl.program_id(0) * kept_ref.shape[0] if axis == 0 else 0
    split_shards(core_ref[0], total, axis, first, kept_ref, sent_refs)


def weight_grad(core, lefts, rights, chips, axis):
    depth = lefts[0].shape[1]
    width = rights[0].shape[1]
    tile = min(512, depth)
    shards = 2 * chips
    if axis == 1:
        shape = (depth, width // shards)
        spec = pl.BlockSpec((chips, tile, width // shards), lambda i, c: (0, i, 0))
        sent = pl.BlockSpec((tile, width // shards), lambda i, c: (i, 0))
    else:
        shape = (depth // shards, width)
        spec = pl.BlockSpec((tile * chips // depth, depth // shards, width), lambda i, c: (i, 0, 0))
        sent = pl.BlockSpec(shape, lambda i, c: (0, 0))
    out = pl.pallas_call(
        functools.partial(grad_body, len(lefts), axis),
        grid_spec=pltpu.PrefetchScalarGridSpec(
            num_scalar_prefetch=1,
            grid=(depth // tile,),
            in_specs=[pl.BlockSpec((left.shape[0], tile), lambda i, c: (0, i)) for left in lefts]
            + [pl.BlockSpec(right.shape, lambda i, c: (0, 0)) for right in rights],
            out_specs=[spec] + [sent] * chips,
        ),
        out_shape=[jax.ShapeDtypeStruct((chips, *shape), LOW)] + [jax.ShapeDtypeStruct(shape, LOW)] * chips,
        compiler_params=params(),
        cost_estimate=LIGHT,
    )(core, *lefts, *rights)
    return out[0], out[1:]


def project_grad_body(core_ref, left_ref, right_ref, kept_ref, *sent_refs):
    products = [
        lax.dot_general(left_ref[...], right_ref[part], TN, preferred_element_type=FULL)
        for part in range(3)
    ]
    first = pl.program_id(0) * kept_ref.shape[0]
    split_shards(core_ref[0], jnp.concatenate(products, axis=1), 0, first, kept_ref, sent_refs)


def project_grad(core, left, right, chips):
    length, depth = left.shape
    cols = right.shape[2]
    tile = min(512, depth)
    shards = 2 * chips
    shape = (depth // shards, 3 * cols)
    out = pl.pallas_call(
        project_grad_body,
        grid_spec=pltpu.PrefetchScalarGridSpec(
            num_scalar_prefetch=1,
            grid=(depth // tile,),
            in_specs=[
                pl.BlockSpec((length, tile), lambda i, c: (0, i)),
                pl.BlockSpec(right.shape, lambda i, c: (0, 0, 0)),
            ],
            out_specs=[pl.BlockSpec((tile * chips // depth, *shape), lambda i, c: (i, 0, 0))]
            + [pl.BlockSpec(shape, lambda i, c: (0, 0))] * chips,
        ),
        out_shape=[jax.ShapeDtypeStruct((chips, *shape), LOW)] + [jax.ShapeDtypeStruct(shape, LOW)] * chips,
        compiler_params=params(),
        cost_estimate=LIGHT,
    )(core, left, right)
    return out[0], out[1:]


def core_add_body(kept_ref, *refs):
    for index, arrived in enumerate(refs[:-1]):
        refs[-1][index] = (kept_ref[index].astype(FULL) + arrived[...].astype(FULL)).astype(LOW)


def core_add_kernel(kept, arrived):
    chips, rows, width = kept.shape
    tile = min(rows, max(16, rows // 4))
    spec = pl.BlockSpec((chips, tile, width), lambda i: (0, i, 0))
    return pl.pallas_call(
        core_add_body,
        grid=(rows // tile,),
        in_specs=[spec] + [pl.BlockSpec((tile, width), lambda i: (i, 0))] * chips,
        out_specs=spec,
        out_shape=jax.ShapeDtypeStruct(kept.shape, LOW),
        compiler_params=params(),
        cost_estimate=LIGHT,
    )(kept, *arrived)


def core_add_apart_body(count, chip_ref, kept_ref, *refs):
    for index in range(count):
        total = (kept_ref[index].astype(FULL) + refs[index][...].astype(FULL)).astype(LOW)
        for mask in range(count):

            @pl.when((chip_ref[0] ^ index) == mask)
            def _():
                refs[count + mask][...] = total


def core_add_apart(chip, kept, arrived):
    chips, rows, width = kept.shape
    tile = min(rows, max(16, rows // 4))
    spec = pl.BlockSpec((tile, width), lambda i, c: (i, 0))
    return pl.pallas_call(
        functools.partial(core_add_apart_body, chips),
        grid_spec=pltpu.PrefetchScalarGridSpec(
            num_scalar_prefetch=1,
            grid=(rows // tile,),
            in_specs=[pl.BlockSpec((chips, tile, width), lambda i, c: (0, i, 0))] + [spec] * chips,
            out_specs=[spec] * chips,
        ),
        out_shape=[jax.ShapeDtypeStruct((rows, width), LOW)] * chips,
        compiler_params=params(),
        cost_estimate=LIGHT,
    )(chip.reshape(1).astype(jnp.int32), kept, *arrived)


def add_many_body(*refs):
    total = refs[0][...].astype(FULL)
    for ref in refs[1:-1]:
        total = total + ref[...].astype(FULL)
    refs[-1][...] = total.astype(LOW)


def add_many(values):
    rows, width = values[0].shape
    tile = max(16, rows // 4)
    spec = pl.BlockSpec((tile, width), lambda i: (i, 0))
    return pl.pallas_call(
        add_many_body,
        grid=(rows // tile,),
        in_specs=[spec] * len(values),
        out_specs=spec,
        out_shape=jax.ShapeDtypeStruct((rows, width), LOW),
        compiler_params=params(),
        cost_estimate=LIGHT,
    )(*values)


def ring_add_body(place_ref, arrived_ref, part_ref, out_ref):
    out_ref[...] = (arrived_ref[...].astype(FULL) + part_ref[...].astype(FULL)).astype(out_ref.dtype)


def ring_add(place, arrived, part, kind):
    rows, width = arrived.shape
    return pl.pallas_call(
        ring_add_body,
        grid_spec=pltpu.PrefetchScalarGridSpec(
            num_scalar_prefetch=1,
            grid=(1,),
            in_specs=[
                pl.BlockSpec((rows, width), lambda i, p: (0, 0)),
                pl.BlockSpec((rows, width), lambda i, p: (p[0], 0)),
            ],
            out_specs=pl.BlockSpec((rows, width), lambda i, p: (0, 0)),
        ),
        out_shape=jax.ShapeDtypeStruct((rows, width), kind),
        compiler_params=params(),
        cost_estimate=LIGHT,
    )(place.reshape(1).astype(jnp.int32), arrived, part)


def pair_add_body(count, place_ref, *refs):
    out_ref = refs[-1]
    rows = refs[0].shape[0]
    for half in range(2):
        span = slice(half * rows, (half + 1) * rows)
        total = refs[half][...].astype(FULL)
        if count > 2:
            total = total + refs[2][span].astype(FULL)
        if count > 3:
            total = total + refs[3 + half][...]
        out_ref[span] = total.astype(out_ref.dtype)


def pair_add(place, block_rows, parts, arrived, bases, kind):
    rows, width = 2 * block_rows, parts[0].shape[1]
    block = pl.BlockSpec((rows // 2, width), lambda i, p: (p[0], 0))
    whole = pl.BlockSpec((rows, width), lambda i, p: (0, 0))
    half = pl.BlockSpec((rows // 2, width), lambda i, p: (0, 0))
    operands, in_specs = list(parts), [block, block]
    if arrived is not None:
        operands.append(arrived)
        in_specs.append(whole)
    if bases is not None:
        operands += bases
        in_specs += [half, half]
    return pl.pallas_call(
        functools.partial(pair_add_body, len(operands)),
        grid_spec=pltpu.PrefetchScalarGridSpec(
            num_scalar_prefetch=1, grid=(1,), in_specs=in_specs, out_specs=whole
        ),
        out_shape=jax.ShapeDtypeStruct((rows, width), kind),
        compiler_params=params(),
        cost_estimate=LIGHT,
    )(place.reshape(1).astype(jnp.int32), *operands)


def round_body(count, in_ref, *out_refs):
    rows = in_ref.shape[0] // count
    for index in range(count):
        out_refs[index][...] = in_ref[index * rows : (index + 1) * rows].astype(LOW)


def round_low(value, count):
    rows, width = value.shape
    tile = min(width, 512)
    return pl.pallas_call(
        functools.partial(round_body, count),
        grid=(width // tile,),
        in_specs=[pl.BlockSpec((rows, tile), lambda i: (0, i))],
        out_specs=[pl.BlockSpec((rows // count, tile), lambda i: (0, i))] * count,
        out_shape=[jax.ShapeDtypeStruct((rows // count, width), LOW)] * count,
        compiler_params=params(),
        cost_estimate=LIGHT,
    )(value)


def norm_back_body(count, steps, place_ref, source_ref, arrived_ref, part_ref, gain_ref, *refs):
    bases, out_refs = refs[:count], refs[count:]
    base = bases[0][...]
    if count == 2:
        base = jnp.where(pl.program_id(0) < steps // 2, base, bases[1][...])
    source = source_ref[...].astype(FULL)
    back = arrived_ref[...].astype(FULL) + part_ref[...].astype(FULL)
    inverse = lax.rsqrt(jnp.mean(source * source, axis=-1, keepdims=True) + NORM_EPS)
    normal = source * inverse
    scaled = gain_ref[...] * back
    grad = base + inverse * (scaled - normal * jnp.mean(normal * scaled, axis=-1, keepdims=True))
    out_refs[0][...] = grad
    total = jnp.sum(back * normal, axis=0, keepdims=True)

    @pl.when(pl.program_id(0) == 0)
    def _():
        out_refs[1][...] = total

    @pl.when(pl.program_id(0) > 0)
    def _():
        out_refs[1][...] += total

    if len(out_refs) > 2:
        out_refs[2][...] = grad.astype(LOW)


def norm_back(place, source, arrived, part, gain, bases, base_first, low):
    rows, width = source.shape
    tile = min(rows, 64)
    steps = rows // tile
    row = pl.BlockSpec((tile, width), lambda i, p: (i, 0))
    whole = pl.BlockSpec((1, width), lambda i, p: (0, 0))
    shapes = [jax.ShapeDtypeStruct((rows, width), FULL), jax.ShapeDtypeStruct((1, width), FULL)]
    out_specs = [row, whole]
    if len(bases) == 1:
        base_specs = [pl.BlockSpec((tile, width), lambda i, p: (base_first // tile + i, 0))]
    else:
        base_specs = [
            pl.BlockSpec((tile, width), lambda i, p: (jnp.minimum(i, steps // 2 - 1), 0)),
            pl.BlockSpec((tile, width), lambda i, p: (jnp.maximum(i - steps // 2, 0), 0)),
        ]
    if low:
        shapes.append(jax.ShapeDtypeStruct((rows, width), LOW))
        out_specs.append(row)
    return pl.pallas_call(
        functools.partial(norm_back_body, len(bases), steps),
        grid_spec=pltpu.PrefetchScalarGridSpec(
            num_scalar_prefetch=1,
            grid=(steps,),
            in_specs=[
                row,
                row,
                pl.BlockSpec((tile, width), lambda i, p: (p[0] * steps + i, 0)),
                whole,
            ]
            + base_specs,
            out_specs=out_specs,
        ),
        out_shape=shapes,
        compiler_params=params(),
        cost_estimate=LIGHT,
    )(place.reshape(1).astype(jnp.int32), source, arrived, part, gain, *bases)


def mix_back_body(place_ref, low_ref, weight_ref, *out_refs):
    total = None
    shards, _, _, shard = weight_ref.shape
    for index in range(shards):
        left = low_ref[:, index * shard : (index + 1) * shard]
        product = lax.dot_general(left, weight_ref[index, 0], NT, preferred_element_type=FULL)
        total = product if total is None else total + product
    value = total.astype(LOW)
    for step, out in enumerate(out_refs):

        @pl.when(pl.program_id(0) == step)
        def _():
            out[...] = value


def mix_back(targets, low, weight):
    rows, width = low.shape
    shards, count, cols, shard = weight.shape
    spec = pl.BlockSpec((rows, cols), lambda i, p: (0, 0))
    return pl.pallas_call(
        mix_back_body,
        grid_spec=pltpu.PrefetchScalarGridSpec(
            num_scalar_prefetch=1,
            grid=(count,),
            in_specs=[
                pl.BlockSpec((rows, width), lambda i, p: (0, 0)),
                pl.BlockSpec((shards, 1, cols, shard), lambda i, p: (0, p[i], 0, 0)),
            ],
            out_specs=[spec] * count,
        ),
        out_shape=[jax.ShapeDtypeStruct((rows, cols), LOW)] * count,
        compiler_params=params(),
        cost_estimate=LIGHT,
    )(targets, low, weight)


def project_back_body(place_ref, back_ref, weight_ref, out_ref):
    total = None
    for part in range(3):
        product = lax.dot_general(back_ref[part], weight_ref[part], NT, preferred_element_type=FULL)
        total = product if total is None else total + product
    out_ref[...] = total.astype(LOW)


def project_back(place, back, weight, rows):
    _, width, cols = weight.shape
    tile = min(512, width)
    return pl.pallas_call(
        project_back_body,
        grid_spec=pltpu.PrefetchScalarGridSpec(
            num_scalar_prefetch=1,
            grid=(width // tile,),
            in_specs=[
                pl.BlockSpec((3, rows, cols), lambda i, p: (0, p[0], 0)),
                pl.BlockSpec((3, tile, cols), lambda i, p: (0, i, 0)),
            ],
            out_specs=pl.BlockSpec((rows, tile), lambda i, p: (0, i)),
        ),
        out_shape=jax.ShapeDtypeStruct((rows, width), LOW),
        compiler_params=params(),
        cost_estimate=LIGHT,
    )(place.reshape(1), back, weight)


def adam_step(weight, grad, first, second, factor, rate, decay):
    clipped = grad * factor
    first_new = BETA_ONE * first + (1.0 - BETA_ONE) * clipped
    second_new = BETA_TWO * second + (1.0 - BETA_TWO) * clipped * clipped
    first_hat = first_new / (1.0 - BETA_ONE**STEP)
    second_hat = second_new / (1.0 - BETA_TWO**STEP)
    weight_new = weight - rate * (first_hat / (jnp.sqrt(second_hat) + ADAM_EPS) + decay * weight)
    return (weight_new, weight_new.astype(LOW), first_new, second_new)


def adam_body(rates, factor_ref, *refs):
    count = len(rates)
    factor = factor_ref[0]
    for index, rate in enumerate(rates):
        weight, grad, first, second = refs[4 * index : 4 * index + 4]
        outs = refs[4 * count + 4 * index : 4 * count + 4 * index + 4]
        if len(weight.shape) == 3:
            cols = weight.shape[2]
            for part in range(weight.shape[0]):
                piece = grad[:, part * cols : (part + 1) * cols].astype(FULL)
                new = adam_step(weight[part], piece, first[part], second[part], factor, rate, DECAY_RATE)
                for out, value in zip(outs, new):
                    out[part] = value
        else:
            new = adam_step(weight[...], grad[...].astype(FULL), first[...], second[...], factor, rate, DECAY_RATE)
            for out, value in zip(outs, new):
                out[...] = value


def adam_all(factor, groups, rates):
    steps = 8
    for weight, _, _, _ in groups:
        steps = min(steps, weight.shape[-2] // 16)
    in_specs, out_specs, shapes, operands = [], [], [], []
    for weight, grad, first, second in groups:
        rows, cols = weight.shape[-2] // steps, weight.shape[-1]
        if weight.ndim == 3:
            spec = pl.BlockSpec((weight.shape[0], rows, cols), lambda i, f: (0, i, 0))
        else:
            spec = pl.BlockSpec((rows, cols), lambda i, f: (i, 0))
        grad_spec = pl.BlockSpec((rows, grad.shape[1]), lambda i, f: (i, 0))
        in_specs += [spec, grad_spec, spec, spec]
        out_specs += [spec] * 4
        operands += [weight, grad, first, second]
        for kind in (FULL, LOW, FULL, FULL):
            shapes.append(jax.ShapeDtypeStruct(weight.shape, kind))
    out = pl.pallas_call(
        functools.partial(adam_body, rates),
        grid_spec=pltpu.PrefetchScalarGridSpec(
            num_scalar_prefetch=1, grid=(steps,), in_specs=in_specs, out_specs=out_specs
        ),
        out_shape=shapes,
        compiler_params=params(60 * 1024 * 1024),
        cost_estimate=LIGHT,
    )(factor.reshape(1), *operands)
    return [tuple(out[4 * index : 4 * index + 4]) for index in range(len(groups))]


def lay_body(spots, me_ref, *refs):
    count = len(spots)
    out_ref = refs[count]
    for piece, spot in zip(refs, spots):
        if isinstance(spot, tuple):
            rows = piece.shape[0]
            out_ref[me_ref[0] ^ spot[0], spot[1] * rows : (spot[1] + 1) * rows] = piece[...]
        else:
            out_ref[lax.rem(me_ref[0] + count - spot, count)] = piece[...]


def lay(me, pieces, spots):
    rows, width = pieces[0].shape
    if isinstance(spots[0], tuple):
        shape = (len(pieces) // 2, 2 * rows, width)
    else:
        shape = (len(pieces), rows, width)
    return pl.pallas_call(
        functools.partial(lay_body, spots),
        in_specs=[pl.BlockSpec(memory_space=pltpu.SMEM)] + [pl.BlockSpec(memory_space=pltpu.VMEM)] * len(pieces),
        out_specs=pl.BlockSpec(memory_space=pltpu.VMEM),
        out_shape=jax.ShapeDtypeStruct(shape, LOW),
        compiler_params=params(),
        cost_estimate=LIGHT,
    )(me.reshape(1).astype(jnp.int32), *pieces)


def lay_cores_body(core_ref, mine_ref, other_ref, out_ref):
    mine, other = mine_ref[...], other_ref[...]
    out_ref[0, 0] = jnp.where(core_ref[0] == 0, mine, other)[0]
    out_ref[0, 1] = jnp.where(core_ref[0] == 0, other, mine)[0]


def lay_cores(core, mine, other):
    chips, rows, width = mine.shape
    spec = pl.BlockSpec((1, rows, width), lambda i, c: (i, 0, 0))
    return pl.pallas_call(
        lay_cores_body,
        grid_spec=pltpu.PrefetchScalarGridSpec(
            num_scalar_prefetch=1,
            grid=(chips,),
            in_specs=[spec, spec],
            out_specs=pl.BlockSpec((1, 2, rows, width), lambda i, c: (i, 0, 0, 0)),
        ),
        out_shape=jax.ShapeDtypeStruct((chips, 2, rows, width), LOW),
        compiler_params=params(),
        cost_estimate=LIGHT,
    )(core, mine, other)


def squares(value):
    wide = value.astype(FULL)
    return jnp.sum(wide * wide)


def after(value, *others):
    if not others:
        return value
    return lax.optimization_barrier((value, *others))[0]


def per_device(
    chips,
    cores,
    bkts,
    block_in,
    cotangent,
    buckets,
    qkv_weight,
    qkv_first,
    qkv_second,
    out_weight,
    out_first,
    out_second,
    up_weight,
    up_first,
    up_second,
    down_weight,
    down_first,
    down_second,
    norm_gains,
    gains_first,
    gains_second,
):
    toks = chips * cores
    tok = ("chip", "core")
    group = lax.axis_index("bkt")
    core = lax.axis_index("core")
    chip = lax.axis_index("chip")
    core_id = core.reshape(1).astype(jnp.int32)
    rows, width = block_in.shape
    half = rows // 2
    length = rows * bkts
    ring = [(i, (i + 1) % bkts) for i in range(bkts)]

    last = []

    def at(value, *others):
        return after(value, *last, *others)

    def did(value):
        last[:] = [value]
        return value

    def wait(value):
        return did(after(value, *last))

    def pass_on(name, value, *others):
        with jax.named_scope(name):
            return lax.ppermute(at(value, *others), "bkt", ring)

    def owner(step):
        return lax.rem(group - step + bkts, bkts)

    places = jnp.stack([owner(step) for step in range(bkts)]).astype(jnp.int32)

    def rows_of(value, step):
        size = value.shape[0] // bkts
        return lax.dynamic_slice_in_dim(value, owner(step) * size, size, 0)

    def add(arrived, value, step):
        return did(ring_add(owner(step), at(arrived), value, LOW))

    def add_final(arrived, value):
        return did(ring_add(owner(0), at(arrived), value, FULL))

    def swap(name, values):
        with jax.named_scope(name + "_swap"):
            return [lax.ppermute(at(value), "core", [(0, 1), (1, 0)]) for value in values]

    def core_add(kept, arrived):
        return did(core_add_kernel(at(kept), arrived))

    def chip_sum(value):
        value = value.reshape(chips * value.shape[1], *value.shape[2:])
        return lax.psum_scatter(value, "chip", scatter_dimension=0, tiled=True)

    by_bits = chips & (chips - 1) == 0

    qkv_full = lax.all_gather(did(qkv_weight.astype(LOW)), tok, axis=1, tiled=True)
    x_held = [block_in, pass_on("x1", block_in)]
    (out_low,) = round_low(at(out_weight), 1)
    did(out_low)
    x_held[1] = wait(x_held[1])
    x_held.append(pass_on("x2", x_held[1]))
    out_held = [out_low, pass_on("out1", out_low)]
    (up_low,) = round_low(at(up_weight), 1)
    up_full = lax.all_gather(did(up_low), tok, axis=0, tiled=True)
    gain_width = norm_gains.shape[1]
    gain_line = jnp.zeros((toks, 2, gain_width), FULL)
    gain_line = lax.dynamic_update_slice(
        gain_line, norm_gains.astype(LOW).astype(FULL)[None], (lax.axis_index(tok), 0, 0)
    )
    if by_bits:
        for axis, size in (("core", cores), ("chip", chips)):
            for bit in range(size.bit_length() - 1):
                perm = [(i, i ^ (1 << bit)) for i in range(size)]
                with jax.named_scope("gains"):
                    gain_line = did(gain_line + lax.ppermute(at(gain_line), axis, perm))
    else:
        gain_line = did(lax.psum(at(gain_line), tok))
    gain_float = gain_line.transpose(1, 0, 2).reshape(2, width)
    cosine, sine = rotary_tables(length)
    for step in range(3, bkts):
        x_held[-1] = wait(x_held[-1])
        out_held[-1] = wait(out_held[-1])
        x_held.append(pass_on("x" + str(step), x_held[-1], cosine, sine))
        out_held.append(pass_on("out" + str(step - 1), out_held[-1]))

    carried = None
    for step in range(bkts - 1):
        carried = project(
            owner(step).reshape(1), at(x_held[step]), gain_float[0:1], qkv_full, cosine, sine, carried
        )
        did(carried[0])
    x_held[-1] = wait(x_held[-1])
    out_held[-1] = wait(out_held[-1])
    out_held.append(pass_on("out" + str(bkts - 1), out_held[-1]))
    normed_one, qkv, seq_in = project(
        owner(bkts - 1).reshape(1), at(x_held[-1]), gain_float[0:1], qkv_full, cosine, sine, carried
    )
    did(normed_one)
    out_held[-1] = wait(out_held[-1])
    out_depth, out_width = out_weight.shape
    out_line = did(lay(group, [at(out_held[0])] + out_held[1:], list(range(bkts))))
    out_full = lax.all_gather(after(out_line, up_full), tok, axis=0, tiled=False)
    (down_low,) = round_low(at(down_weight), 1)
    down_full = lax.all_gather(did(down_low), tok, axis=1, tiled=True)
    cols = qkv.shape[2]
    seq_in = seq_in.reshape(bkts, rows, width)

    slab, log_a = attend(0, bkts, at(qkv), cotangent)
    slabs = [[did(slab)], []]

    def next_slab(part):
        held = slabs[part]
        if len(held) > 1:
            held[-1] = wait(held[-1])
        held.append(pass_on("slab" + "ab"[part] + str(len(held)), held[-1]))

    next_slab(0)
    slab, log_b = attend(1, bkts, at(qkv), cotangent)
    slabs[1].append(did(slab))
    logs = [log_a, log_b]
    for step in range(2, bkts):
        next_slab(0)
    slabs[0][-1] = wait(slabs[0][-1])
    for step in range(1, bkts - 2):
        next_slab(1)

    live = (buckets >= group).astype(FULL)
    acc = did(mix_first(0, places, at(seq_in), slabs[0][:-1], out_full))
    normed_a, middle_a, mixed_a = mix_last(places, acc, gain_float[1:2], slabs[0], out_full)
    did(normed_a)
    next_slab(1)
    hidden_a, inner_a, low_a = hidden_units(places, live, at(normed_a), up_full, down_full, slabs[0])
    did(inner_a)
    next_slab(1)
    back_a = did(product(at(inner_a), up_full, True))
    sum_a = did(rows_of(back_a, 1))
    arrived_a = pass_on("sum_a1", sum_a)
    acc = did(mix_first(1, places, at(seq_in), slabs[1][:-1], out_full))
    prod_a = did(product(at(hidden_a), down_full, False))
    slabs[1][-1] = wait(slabs[1][-1])
    normed_b, middle_b, mixed_b = mix_last(places, at(acc), gain_float[1:2], slabs[1], out_full)
    did(normed_b)
    sum_a = add(arrived_a, back_a, 2)
    arrived_a = pass_on("sum_a2", sum_a)

    hidden_b, inner_b, low_b = hidden_units(places, live, at(normed_b), up_full, down_full, slabs[1])
    did(inner_b)
    sum_a = add(arrived_a, back_a, 3)
    arrived_a = pass_on("sum_a3", sum_a)
    up_kept, up_sent = weight_grad(core_id, [normed_a, normed_b], [at(inner_a), inner_b], chips, 0)
    did(up_kept)
    back_b = did(product(at(inner_b), up_full, True))
    arrived_a = wait(arrived_a)
    sum_b = did(rows_of(at(back_b), 1))
    arrived_b = pass_on("sum_b1", sum_b)
    up_arrived = swap("up_grad", up_sent)

    first = jnp.zeros((), jnp.int32)
    targets = jnp.stack([lax.rem(group + step, bkts) for step in range(bkts)]).astype(jnp.int32)

    def middle_back(part, middle, arrived, back):
        grad, gain_sum, low = norm_back(
            owner(0), middle, at(arrived), back, gain_float[1:2], [cotangent], part * half, True
        )
        found = list(mix_back(targets, low, out_full))
        did(found[0])
        return grad, low, gain_sum, found

    def exchange(part, found):
        with jax.named_scope("exchange" + str(part)):
            for step in range(1, bkts):
                found[step] = lax.ppermute(
                    at(found[step]), "bkt", [(i, (i + step) % bkts) for i in range(bkts)]
                )

    grad_a, mid_low_a, gain_a, pieces_a = middle_back(0, middle_a, arrived_a, back_a)
    sum_b = add(arrived_b, back_b, 2)
    arrived_b = pass_on("sum_b2", sum_b)
    exchange(0, pieces_a)
    up_core = core_add(up_kept, up_arrived)
    up_part = chip_sum(up_core)
    down_kept, down_sent = weight_grad(core_id, [hidden_a, hidden_b], [at(low_a), low_b], chips, 1)
    did(down_kept)
    pieces_a = pieces_a[:1] + [wait(piece) for piece in pieces_a[1:]]
    sum_b = add(arrived_b, back_b, 3)
    arrived_b = pass_on("sum_b3", sum_b)
    down_arrived = swap("down_grad", down_sent)
    prod_b = did(product(at(hidden_b), down_full, False))
    grad_b, mid_low_b, gain_b, pieces_b = middle_back(1, middle_b, arrived_b, back_b)
    exchange(1, pieces_b)
    down_core = core_add(down_kept, down_arrived)
    down_part = chip_sum(down_core)
    out_kept, out_sent = weight_grad(
        core_id, [at(mixed_a), mixed_b], [mid_low_a, mid_low_b], chips, 1
    )
    did(out_kept)
    prods = [prod_a, prod_b]
    ffn = did(pair_add(owner(1), half, [at(prod_a), prod_b], None, None, LOW))
    pieces_b = pieces_b[:1] + [wait(piece) for piece in pieces_b[1:]]
    arrived_f = pass_on("ffn1", ffn)
    out_arrived = swap("out_grad", out_sent)

    back_project = did(attend_back(places, at(qkv), pieces_a + pieces_b, logs, cosine, sine))
    total = did(project_back(owner(1), at(back_project), qkv_full, rows))
    arrived_f = wait(arrived_f)
    up_squares = did(squares(at(up_part)))
    out_core = core_add(out_kept, out_arrived)
    out_sum = chip_sum(out_core)
    arrived = pass_on("back1", total)
    qkv_kept, qkv_sent = project_grad(core_id, normed_one, at(back_project), chips)
    did(qkv_kept)
    own = did(project_back(owner(2), at(back_project), qkv_full, rows))
    total = did(ring_add(first, at(arrived), own, LOW))
    down_squares = did(squares(at(down_part)))
    arrived = pass_on("back2", total)
    qkv_arrived = swap("qkv_grad", qkv_sent)
    own = did(project_back(owner(3), at(back_project), qkv_full, rows))
    qkv_core = core_add(qkv_kept, qkv_arrived)
    qkv_part = chip_sum(qkv_core)
    last_own = did(project_back(owner(0), at(back_project), qkv_full, rows))
    arrived_out = pass_on("out_sum1", rows_of(out_sum, 1))
    total = did(ring_add(first, at(arrived), own, LOW))
    out_part = add(arrived_out, out_sum, 2)
    arrived_out = pass_on("out_sum2", out_part)
    arrived = pass_on("back3", total, out_part)
    ffn = did(pair_add(owner(2), half, prods, at(arrived_f), None, LOW))
    for step in range(3, bkts):
        out_part = add(arrived_out, out_sum, step)
        arrived_out = pass_on("out_sum" + str(step), out_part)
    block_in_grad, gain_one = norm_back(
        first, block_in, at(arrived), last_own, gain_float[0:1], [grad_a, grad_b], 0, False
    )
    did(gain_one)
    out_part = add_final(arrived_out, out_sum)
    arrived_f = pass_on("ffn2", ffn)
    out_squares = did(squares(at(out_part)))
    gain_grad_one = gain_one[0]
    gain_grad_two = (gain_a + gain_b)[0]

    weight_squares = did(up_squares + down_squares + out_squares + squares(at(qkv_part)))
    packed = jnp.concatenate(
        [gain_grad_one, gain_grad_two, jnp.broadcast_to(weight_squares, (HD,))]
    )
    for axis, size in (("core", cores), ("chip", chips), ("bkt", bkts)):
        if size & (size - 1):
            packed = lax.psum(packed, axis)
        else:
            step = 1
            while step < size:
                packed = packed + lax.ppermute(packed, axis, [(i, i ^ step) for i in range(size)])
                if axis == "bkt" and step == 1:
                    ffn = pair_add(owner(3), half, prods, after(arrived_f, packed), None, LOW)
                step *= 2
    did(packed)
    arrived_f = pass_on("ffn3", ffn)
    gain_total = packed[: 2 * width].reshape(2, width)
    grad_norm = jnp.sqrt(packed[2 * width] + jnp.sum(gain_total * gain_total))
    factor = jnp.minimum(1.0, CLIP_NORM / grad_norm)
    gain_part = lax.dynamic_slice_in_dim(gain_total, lax.axis_index(tok) * gain_width, gain_width, 1)
    updated = adam_all(
        factor,
        [
            (qkv_weight, qkv_part, qkv_first, qkv_second),
            (out_weight, out_part, out_first, out_second),
            (up_weight, up_part, up_first, up_second),
            (down_weight, down_part, down_first, down_second),
        ],
        (D ** (-0.5), (H * HD // 16) ** (-0.5), D ** (-0.5), FF ** (-0.5)),
    )
    block_out = pair_add(
        owner(0), half, prods, after(arrived_f, updated[0][0]), [middle_a, middle_b], FULL
    )
    gain_out = adam_step(norm_gains, gain_part, gains_first, gains_second, factor, GAIN_RATE, 0.0)
    return (block_out, block_in_grad, grad_norm, *[value for new in updated for value in new], *gain_out)


def solution(mesh):
    toks, bkts = mesh.shape["tok"], mesh.shape["bkt"]
    cores = 2
    chips = toks // cores
    tok = ("chip", "core")
    rows = P(("chip", "core", "bkt"), None)
    qkv = P(None, tok, "bkt")
    tall = P("bkt", tok)
    wide = P(tok, "bkt")
    gains = P(None, tok)
    return jax.shard_map(
        functools.partial(per_device, chips, cores, bkts),
        mesh=Mesh(mesh.devices.reshape(chips, cores, bkts), ("chip", "core", "bkt")),
        in_specs=(rows, rows, P(tok), *[qkv] * 3, *[tall] * 3, *[wide] * 3, *[tall] * 3, *[gains] * 3),
        out_specs=(rows, rows, P(), *[qkv] * 4, *[tall] * 4, *[wide] * 4, *[tall] * 4, *[gains] * 4),
        check_vma=False,
    )
```

```python
import functools
import jax
import jax.numpy as jnp
from jax import lax
from jax.experimental import pallas as pl
from jax.experimental.pallas import tpu as pltpu
from jax.sharding import Mesh, PartitionSpec as P

D = 2048
H = 16
HD = 128
FF = 8192
STEP = 10

NORM_EPS = 1e-05
ADAM_EPS = 1e-08
CLIP_NORM = 1.0
BETA_ONE = 0.9
BETA_TWO = 0.95
DECAY_RATE = 0.1
GAIN_RATE = 0.3
ROPE_BASE = 10000.0

LOW = jnp.bfloat16
FULL = jnp.float32
SCALE = HD ** (-0.5)
VMEM_BYTES = 48 * 1024 * 1024
NN = (((1,), (0,)), ((), ()))
NT = (((1,), (1,)), ((), ()))
TN = (((0,), (0,)), ((), ()))


def rotary_tables(length):
    positions = jnp.arange(length).astype(FULL)[:, None]
    freq_index = jnp.arange(HD // 2).astype(FULL)
    angles = positions * (ROPE_BASE ** (-2.0 * freq_index / HD))[None, :]
    cosine = jnp.cos(angles)
    sine = jnp.sin(angles)
    return (jnp.concatenate([cosine, cosine], axis=-1), jnp.concatenate([-sine, sine], axis=-1))


LIGHT = pl.CostEstimate(flops=1, bytes_accessed=1, transcendentals=0)


def params(vmem=VMEM_BYTES):
    return pltpu.CompilerParams(vmem_limit_bytes=vmem)


def project_body(place_ref, x_ref, gain_ref, w_ref, cos_ref, sin_ref, *rest):
    normed_ref, out_ref, seq_ref = rest[-3:]
    part = pl.program_id(0)

    @pl.when(part == 0)
    def _():
        low = x_ref[...]
        seq_ref[...] = low
        values = low.astype(FULL)
        inverse = lax.rsqrt(jnp.mean(values * values, axis=-1, keepdims=True) + NORM_EPS)
        normed_ref[...] = (values * inverse * gain_ref[...]).astype(LOW)

    product = jnp.dot(normed_ref[...], w_ref[0], preferred_element_type=FULL)

    @pl.when(part < 2)
    def _():
        for head in range(product.shape[1] // HD):
            one = product[:, head * HD : (head + 1) * HD]
            turned = one * cos_ref[...] + pltpu.roll(one, HD // 2, 1) * sin_ref[...]
            out_ref[0, :, head * HD : (head + 1) * HD] = turned.astype(LOW)

    @pl.when(part == 2)
    def _():
        out_ref[0] = product.astype(LOW)


def project(place, x, gain, weight, cosine, sine, carried):
    rows, width = x.shape
    length = cosine.shape[0]
    cols = weight.shape[2]
    shapes = [
        jax.ShapeDtypeStruct((length, width), LOW),
        jax.ShapeDtypeStruct((3, length, cols), LOW),
        jax.ShapeDtypeStruct((length, width), LOW),
    ]
    in_specs = [
        pl.BlockSpec((rows, width), lambda c, p: (0, 0)),
        pl.BlockSpec((1, width), lambda c, p: (0, 0)),
        pl.BlockSpec((1, width, cols), lambda c, p: (c, 0, 0)),
        pl.BlockSpec((rows, HD), lambda c, p: (p[0], 0)),
        pl.BlockSpec((rows, HD), lambda c, p: (p[0], 0)),
    ]
    aliases = {}
    if carried is not None:
        in_specs += [pl.BlockSpec(memory_space=pl.ANY)] * 3
        aliases = {6: 0, 7: 1, 8: 2}
    return pl.pallas_call(
        project_body,
        grid_spec=pltpu.PrefetchScalarGridSpec(
            num_scalar_prefetch=1,
            grid=(3,),
            in_specs=in_specs,
            out_specs=[
                pl.BlockSpec((rows, width), lambda c, p: (p[0], 0)),
                pl.BlockSpec((1, rows, cols), lambda c, p: (c, p[0], 0)),
                pl.BlockSpec((rows, width), lambda c, p: (p[0], 0)),
            ],
        ),
        out_shape=shapes,
        input_output_aliases=aliases,
        compiler_params=params(),
        cost_estimate=LIGHT,
    )(place, x, gain, weight, cosine, sine, *(carried or ()))


def pack_body(in_ref, out_ref):
    out_ref[...] = in_ref[...].astype(LOW)


def pack_half(half, cotangent, cols):
    rows, width = cotangent.shape
    count = width // cols
    return pl.pallas_call(
        pack_body,
        grid=(count,),
        in_specs=[pl.BlockSpec((rows // 2, cols), lambda j: (half, j))],
        out_specs=pl.BlockSpec((rows // 2, cols), lambda j: (j, 0)),
        out_shape=jax.ShapeDtypeStruct((count * rows // 2, cols), LOW),
        compiler_params=params(),
        cost_estimate=LIGHT,
    )(cotangent)


def attend_body(half, blocks, q_ref, k_ref, v_ref, lower_ref, ring_ref, log_ref):
    length = q_ref.shape[1]
    block = length // blocks
    rows = block // 2
    ring_ref[length // 2 :] = lower_ref[...]
    for index in range(blocks):
        first = index * block + half * rows
        last = first + rows
        query = q_ref[0, first:last]
        scores = (
            lax.dot_general(query, k_ref[0, :last], NT, preferred_element_type=FULL) * SCALE
        )
        row = lax.broadcasted_iota(jnp.int32, scores.shape, 0) + first
        col = lax.broadcasted_iota(jnp.int32, scores.shape, 1)
        scores = jnp.where(row >= col, scores, -1e30)
        peak = jnp.max(scores, axis=-1, keepdims=True)
        expo = jnp.exp(scores - peak)
        total = jnp.sum(expo, axis=-1, keepdims=True)
        probs = (expo / total).astype(LOW)
        mixed = jnp.dot(probs, v_ref[0, :last], preferred_element_type=FULL)
        ring_ref[index * rows : (index + 1) * rows] = mixed.astype(LOW)
        log_ref[index * rows : (index + 1) * rows] = jnp.broadcast_to(
            peak + jnp.log(total), (rows, HD)
        )


def attend(half, blocks, qkv, lower):
    _, length, cols = qkv.shape
    heads = cols // HD
    below = lower.shape[0]
    return pl.pallas_call(
        functools.partial(attend_body, half, blocks),
        grid=(heads,),
        in_specs=[
            pl.BlockSpec((1, length, HD), lambda h: (0, 0, h)),
            pl.BlockSpec((1, length, HD), lambda h: (1, 0, h)),
            pl.BlockSpec((1, length, HD), lambda h: (2, 0, h)),
            pl.BlockSpec((below, HD), lambda h: (0, h)),
        ],
        out_specs=[
            pl.BlockSpec((length // 2 + below, HD), lambda h: (0, h)),
            pl.BlockSpec((length // 2, HD), lambda h: (0, h)),
        ],
        out_shape=[
            jax.ShapeDtypeStruct((length // 2 + below, cols), LOW),
            jax.ShapeDtypeStruct((length // 2, cols), FULL),
        ],
        compiler_params=params(),
        cost_estimate=LIGHT,
    )(qkv, qkv, qkv, lower)


def attend_back_body(blocks, place_ref, q_ref, k_ref, v_ref, log_a_ref, log_b_ref, cos_ref, sin_ref, *rest):
    pieces = rest[:blocks]
    out_ref, key_acc, value_acc, back_ref = rest[blocks:]
    length = q_ref.shape[1]
    block = length // blocks
    rows = block // 2
    for step in range(blocks):
        first = pl.multiple_of(place_ref[step] * block, block)
        back_ref[pl.ds(first, block), :] = pieces[step][...]

    def turn_back(one, cosine, sine):
        return one * cosine - pltpu.roll(one, HD // 2, 1) * sine

    for index in range(blocks):
        first, last = index * block, (index + 1) * block
        query = q_ref[0, first:last]
        back = back_ref[first:last]
        keys = k_ref[0, :last]
        log_total = jnp.concatenate(
            [
                log_a_ref[index * rows : (index + 1) * rows, :1],
                log_b_ref[index * rows : (index + 1) * rows, :1],
            ],
            axis=0,
        )
        scores = lax.dot_general(query, keys, NT, preferred_element_type=FULL) * SCALE
        row = lax.broadcasted_iota(jnp.int32, scores.shape, 0) + first
        col = lax.broadcasted_iota(jnp.int32, scores.shape, 1)
        probs = jnp.exp(jnp.where(row >= col, scores, -1e30) - log_total)
        back_probs = lax.dot_general(back, v_ref[0, :last], NT, preferred_element_type=FULL)
        centre = jnp.sum(probs * back_probs, axis=-1, keepdims=True)
        back_scores = (probs * (back_probs - centre)).astype(LOW)
        query_grad = jnp.dot(back_scores, keys, preferred_element_type=FULL) * SCALE
        out_ref[0, first:last] = turn_back(query_grad, cos_ref[first:last], sin_ref[first:last]).astype(LOW)
        key_part = lax.dot_general(back_scores, query, TN, preferred_element_type=FULL)
        value_part = lax.dot_general(probs.astype(LOW), back, TN, preferred_element_type=FULL)
        if index > 0:
            key_acc[:first] += key_part[:first]
            value_acc[:first] += value_part[:first]
        key_acc[first:last] = key_part[first:]
        value_acc[first:last] = value_part[first:]
    out_ref[1] = turn_back(key_acc[...] * SCALE, cos_ref[...], sin_ref[...]).astype(LOW)
    out_ref[2] = value_acc[...].astype(LOW)


def attend_back(places, qkv, pieces, logs, cosine, sine):
    _, length, cols = qkv.shape
    heads = cols // HD
    blocks = len(pieces)
    column = lambda h, p: (0, h)
    return pl.pallas_call(
        functools.partial(attend_back_body, blocks),
        grid_spec=pltpu.PrefetchScalarGridSpec(
            num_scalar_prefetch=1,
            grid=(heads,),
            in_specs=[
                pl.BlockSpec((1, length, HD), lambda h, p: (0, 0, h)),
                pl.BlockSpec((1, length, HD), lambda h, p: (1, 0, h)),
                pl.BlockSpec((1, length, HD), lambda h, p: (2, 0, h)),
                pl.BlockSpec((length // 2, HD), column),
                pl.BlockSpec((length // 2, HD), column),
                pl.BlockSpec((length, HD), lambda h, p: (0, 0)),
                pl.BlockSpec((length, HD), lambda h, p: (0, 0)),
            ]
            + [pl.BlockSpec((length // blocks, HD), column)] * blocks,
            out_specs=pl.BlockSpec((3, length, HD), lambda h, p: (0, 0, h)),
            scratch_shapes=[
                pltpu.VMEM((length, HD), FULL),
                pltpu.VMEM((length, HD), FULL),
                pltpu.VMEM((length, HD), LOW),
            ],
        ),
        out_shape=jax.ShapeDtypeStruct((3, length, cols), LOW),
        compiler_params=params(),
        cost_estimate=LIGHT,
    )(places, qkv, qkv, qkv, logs[0], logs[1], cosine, sine, *pieces)


def mix_first_body(count, place_ref, seq_ref, *rest):
    slabs, weights, acc_ref = rest[:count], rest[count : 2 * count], rest[2 * count]
    blocks, rows, width = seq_ref.shape
    shards, _, _, shard = weights[0].shape
    for index in range(shards):
        span = slice(index * shard, (index + 1) * shard)
        total = seq_ref[:, :, span].reshape(blocks * rows, shard).astype(FULL)
        for slab, weight in zip(slabs, weights):
            total = total + jnp.dot(slab[...], weight[index, 0], preferred_element_type=FULL)
        acc_ref[:, span] = total


def mix_first(part, places, seq_in, slabs, weight):
    blocks, block, width = seq_in.shape
    half = block // 2
    shards, _, cols, shard = weight.shape
    tile = max(1, 512 // shard)
    count = len(slabs)

    def weight_spec(step):
        return pl.BlockSpec((tile, 1, cols, shard), lambda i, p: (i, p[step], 0, 0))

    return pl.pallas_call(
        functools.partial(mix_first_body, count),
        grid_spec=pltpu.PrefetchScalarGridSpec(
            num_scalar_prefetch=1,
            grid=(shards // tile,),
            in_specs=[pl.BlockSpec((blocks, half, tile * shard), lambda i, p: (0, part, i))]
            + [pl.BlockSpec((blocks * half, cols), lambda i, p: (0, 0))] * count
            + [weight_spec(step) for step in range(count)],
            out_specs=pl.BlockSpec((blocks * half, tile * shard), lambda i, p: (0, i)),
        ),
        out_shape=jax.ShapeDtypeStruct((blocks * half, width), FULL),
        compiler_params=params(),
        cost_estimate=LIGHT,
    )(places, seq_in, *slabs, *[weight] * count)


def mix_last_body(count, place_ref, acc_ref, gain_ref, weight_ref, *rest):
    slabs = rest[:count]
    normed_ref, middle_ref, mixed_ref = rest[count:]
    cols = slabs[0].shape[1]
    slab = slabs[-1][...]
    parts = [
        jnp.dot(slab, weight_ref[index, 0], preferred_element_type=FULL)
        for index in range(weight_ref.shape[0])
    ]
    middle = acc_ref[...] + jnp.concatenate(parts, axis=1)
    inverse = lax.rsqrt(jnp.mean(middle * middle, axis=-1, keepdims=True) + NORM_EPS)
    normed_ref[...] = (middle * inverse * gain_ref[...]).astype(LOW)

    @pl.when(pl.program_id(0) == place_ref[0])
    def _():
        middle_ref[...] = middle
        for step in range(count):
            first = pl.multiple_of(place_ref[step] * cols, cols)
            mixed_ref[:, pl.ds(first, cols)] = slabs[step][...]


def mix_last(places, acc, gain, slabs, weight):
    length, width = acc.shape
    shards, count, cols, shard = weight.shape
    rows = length // count
    return pl.pallas_call(
        functools.partial(mix_last_body, count),
        grid_spec=pltpu.PrefetchScalarGridSpec(
            num_scalar_prefetch=1,
            grid=(count,),
            in_specs=[
                pl.BlockSpec((rows, width), lambda i, p: (i, 0)),
                pl.BlockSpec((1, width), lambda i, p: (0, 0)),
                pl.BlockSpec((shards, 1, cols, shard), lambda i, p: (0, p[count - 1], 0, 0)),
            ]
            + [pl.BlockSpec((rows, cols), lambda i, p: (i, 0))] * count,
            out_specs=[
                pl.BlockSpec((rows, width), lambda i, p: (i, 0)),
                pl.BlockSpec((rows, width), lambda i, p: (0, 0)),
                pl.BlockSpec((rows, count * cols), lambda i, p: (0, 0)),
            ],
        ),
        out_shape=[
            jax.ShapeDtypeStruct((length, width), LOW),
            jax.ShapeDtypeStruct((rows, width), FULL),
            jax.ShapeDtypeStruct((rows, count * cols), LOW),
        ],
        compiler_params=params(),
        cost_estimate=LIGHT,
    )(places, acc, gain, weight, *slabs)


def hidden_body(count, place_ref, live_ref, normed_ref, up_ref, down_ref, *rest):
    pieces = rest[:count]
    hidden_ref, inner_ref, back_ref = rest[count:]
    cols = pieces[0].shape[1]
    rows = pieces[0].shape[0] * cols // back_ref.shape[1]

    @pl.when(pl.program_id(0) == 0)
    def _():
        for step in range(count):
            first = pl.multiple_of(place_ref[step] * rows, rows)
            for index in range(pieces[0].shape[0] // rows):
                span = slice(index * rows, (index + 1) * rows)
                back_ref[pl.ds(first, rows), index * cols : (index + 1) * cols] = pieces[step][span]

    inner = jnp.dot(normed_ref[...], up_ref[...], preferred_element_type=FULL)
    inner = jnp.maximum(inner, 0.0) * live_ref[0]
    hidden_ref[...] = (inner * inner).astype(LOW)
    back = lax.dot_general(back_ref[...], down_ref[...], NT, preferred_element_type=FULL)
    inner_ref[...] = (back * 2.0 * inner).astype(LOW)


def hidden_units(places, live, normed, up, down, pieces):
    length, width = normed.shape
    units = up.shape[1]
    tile = min(512, units)
    count = len(pieces)
    rows = length // count
    cols = pieces[0][0].shape[1]
    below = rows * width // cols
    whole = lambda i, p, l: (0, 0)

    def piece_spec(index):
        return pl.BlockSpec((below, cols), lambda i, p, l: (index, 0))

    column = lambda i, p, l: (0, i)
    return pl.pallas_call(
        functools.partial(hidden_body, count),
        grid_spec=pltpu.PrefetchScalarGridSpec(
            num_scalar_prefetch=2,
            grid=(units // tile,),
            in_specs=[
                pl.BlockSpec((length, width), whole),
                pl.BlockSpec((width, tile), column),
                pl.BlockSpec((tile, width), lambda i, p, l: (i, 0)),
            ]
            + [piece_spec(index) for _, index in pieces],
            out_specs=[
                pl.BlockSpec((length, tile), column),
                pl.BlockSpec((length, tile), column),
                pl.BlockSpec((length, width), whole),
            ],
        ),
        out_shape=[
            jax.ShapeDtypeStruct((length, units), LOW),
            jax.ShapeDtypeStruct((length, units), LOW),
            jax.ShapeDtypeStruct((length, width), LOW),
        ],
        compiler_params=params(56 * 1024 * 1024),
        cost_estimate=LIGHT,
    )(places, live, normed, up, down, *[piece for piece, _ in pieces])


def product_body(dims, left_ref, right_ref, out_ref):
    out_ref[...] = lax.dot_general(
        left_ref[...], right_ref[...], dims, preferred_element_type=FULL
    ).astype(LOW)


def product(left, right, turned):
    length, depth = left.shape
    width = right.shape[0] if turned else right.shape[1]
    tile = min(512, width)
    if turned:
        spec = pl.BlockSpec((tile, depth), lambda i: (i, 0))
    else:
        spec = pl.BlockSpec((depth, tile), lambda i: (0, i))
    return pl.pallas_call(
        functools.partial(product_body, NT if turned else NN),
        grid=(width // tile,),
        in_specs=[pl.BlockSpec((length, depth), lambda i: (0, 0)), spec],
        out_specs=pl.BlockSpec((length, tile), lambda i: (0, i)),
        out_shape=jax.ShapeDtypeStruct((length, width), LOW),
        compiler_params=params(),
        cost_estimate=LIGHT,
    )(left, right)


def split_shards(core, total, axis, first, kept_ref, sent_refs):
    shard = kept_ref.shape[1 + axis]
    count = total.shape[axis] // (2 * shard)

    def cut(index):
        span = slice(index * shard, (index + 1) * shard)
        return total[span] if axis == 0 else total[:, span]

    for index in range(count):
        even, odd = cut(2 * index), cut(2 * index + 1)
        kept_ref[index] = jnp.where(core == 0, even, odd).astype(LOW)
        sent = jnp.where(core == 0, odd, even).astype(LOW)
        if axis == 1:
            sent_refs[index][...] = sent
        else:
            for chip in range(index, len(sent_refs), count):

                @pl.when(first + index == chip)
                def _():
                    sent_refs[chip][...] = sent


def grad_body(count, axis, core_ref, *refs):
    total = None
    for index in range(count):
        product = lax.dot_general(
            refs[index][...], refs[count + index][...], TN, preferred_element_type=FULL
        )
        total = product if total is None else total + product
    kept_ref, sent_refs = refs[2 * count], refs[2 * count + 1 :]
    first = pl.program_id(0) * kept_ref.shape[0] if axis == 0 else 0
    split_shards(core_ref[0], total, axis, first, kept_ref, sent_refs)


def weight_grad(core, lefts, rights, chips, axis):
    depth = lefts[0].shape[1]
    width = rights[0].shape[1]
    tile = min(512, depth)
    shards = 2 * chips
    if axis == 1:
        shape = (depth, width // shards)
        spec = pl.BlockSpec((chips, tile, width // shards), lambda i, c: (0, i, 0))
        sent = pl.BlockSpec((tile, width // shards), lambda i, c: (i, 0))
    else:
        shape = (depth // shards, width)
        spec = pl.BlockSpec((tile * chips // depth, depth // shards, width), lambda i, c: (i, 0, 0))
        sent = pl.BlockSpec(shape, lambda i, c: (0, 0))
    out = pl.pallas_call(
        functools.partial(grad_body, len(lefts), axis),
        grid_spec=pltpu.PrefetchScalarGridSpec(
            num_scalar_prefetch=1,
            grid=(depth // tile,),
            in_specs=[pl.BlockSpec((left.shape[0], tile), lambda i, c: (0, i)) for left in lefts]
            + [pl.BlockSpec(right.shape, lambda i, c: (0, 0)) for right in rights],
            out_specs=[spec] + [sent] * chips,
        ),
        out_shape=[jax.ShapeDtypeStruct((chips, *shape), LOW)] + [jax.ShapeDtypeStruct(shape, LOW)] * chips,
        compiler_params=params(),
        cost_estimate=LIGHT,
    )(core, *lefts, *rights)
    return out[0], out[1:]


def project_grad_body(core_ref, left_ref, right_ref, kept_ref, *sent_refs):
    products = [
        lax.dot_general(left_ref[...], right_ref[part], TN, preferred_element_type=FULL)
        for part in range(3)
    ]
    first = pl.program_id(0) * kept_ref.shape[0]
    split_shards(core_ref[0], jnp.concatenate(products, axis=1), 0, first, kept_ref, sent_refs)


def project_grad(core, left, right, chips):
    length, depth = left.shape
    cols = right.shape[2]
    tile = min(512, depth)
    shards = 2 * chips
    shape = (depth // shards, 3 * cols)
    out = pl.pallas_call(
        project_grad_body,
        grid_spec=pltpu.PrefetchScalarGridSpec(
            num_scalar_prefetch=1,
            grid=(depth // tile,),
            in_specs=[
                pl.BlockSpec((length, tile), lambda i, c: (0, i)),
                pl.BlockSpec(right.shape, lambda i, c: (0, 0, 0)),
            ],
            out_specs=[pl.BlockSpec((tile * chips // depth, *shape), lambda i, c: (i, 0, 0))]
            + [pl.BlockSpec(shape, lambda i, c: (0, 0))] * chips,
        ),
        out_shape=[jax.ShapeDtypeStruct((chips, *shape), LOW)] + [jax.ShapeDtypeStruct(shape, LOW)] * chips,
        compiler_params=params(),
        cost_estimate=LIGHT,
    )(core, left, right)
    return out[0], out[1:]


def core_add_body(kept_ref, *refs):
    for index, arrived in enumerate(refs[:-1]):
        refs[-1][index] = (kept_ref[index].astype(FULL) + arrived[...].astype(FULL)).astype(LOW)


def core_add_kernel(kept, arrived):
    chips, rows, width = kept.shape
    tile = min(rows, max(16, rows // 4))
    spec = pl.BlockSpec((chips, tile, width), lambda i: (0, i, 0))
    return pl.pallas_call(
        core_add_body,
        grid=(rows // tile,),
        in_specs=[spec] + [pl.BlockSpec((tile, width), lambda i: (i, 0))] * chips,
        out_specs=spec,
        out_shape=jax.ShapeDtypeStruct(kept.shape, LOW),
        compiler_params=params(),
        cost_estimate=LIGHT,
    )(kept, *arrived)


def core_add_apart_body(count, chip_ref, kept_ref, *refs):
    for index in range(count):
        total = (kept_ref[index].astype(FULL) + refs[index][...].astype(FULL)).astype(LOW)
        for mask in range(count):

            @pl.when((chip_ref[0] ^ index) == mask)
            def _():
                refs[count + mask][...] = total


def core_add_apart(chip, kept, arrived):
    chips, rows, width = kept.shape
    tile = min(rows, max(16, rows // 4))
    spec = pl.BlockSpec((tile, width), lambda i, c: (i, 0))
    return pl.pallas_call(
        functools.partial(core_add_apart_body, chips),
        grid_spec=pltpu.PrefetchScalarGridSpec(
            num_scalar_prefetch=1,
            grid=(rows // tile,),
            in_specs=[pl.BlockSpec((chips, tile, width), lambda i, c: (0, i, 0))] + [spec] * chips,
            out_specs=[spec] * chips,
        ),
        out_shape=[jax.ShapeDtypeStruct((rows, width), LOW)] * chips,
        compiler_params=params(),
        cost_estimate=LIGHT,
    )(chip.reshape(1).astype(jnp.int32), kept, *arrived)


def add_many_body(*refs):
    total = refs[0][...].astype(FULL)
    for ref in refs[1:-1]:
        total = total + ref[...].astype(FULL)
    refs[-1][...] = total.astype(LOW)


def add_many(values):
    rows, width = values[0].shape
    tile = max(16, rows // 4)
    spec = pl.BlockSpec((tile, width), lambda i: (i, 0))
    return pl.pallas_call(
        add_many_body,
        grid=(rows // tile,),
        in_specs=[spec] * len(values),
        out_specs=spec,
        out_shape=jax.ShapeDtypeStruct((rows, width), LOW),
        compiler_params=params(),
        cost_estimate=LIGHT,
    )(*values)


def ring_add_body(place_ref, arrived_ref, part_ref, out_ref):
    out_ref[...] = (arrived_ref[...].astype(FULL) + part_ref[...].astype(FULL)).astype(out_ref.dtype)


def ring_add(place, arrived, part, kind):
    rows, width = arrived.shape
    return pl.pallas_call(
        ring_add_body,
        grid_spec=pltpu.PrefetchScalarGridSpec(
            num_scalar_prefetch=1,
            grid=(1,),
            in_specs=[
                pl.BlockSpec((rows, width), lambda i, p: (0, 0)),
                pl.BlockSpec((rows, width), lambda i, p: (p[0], 0)),
            ],
            out_specs=pl.BlockSpec((rows, width), lambda i, p: (0, 0)),
        ),
        out_shape=jax.ShapeDtypeStruct((rows, width), kind),
        compiler_params=params(),
        cost_estimate=LIGHT,
    )(place.reshape(1).astype(jnp.int32), arrived, part)


def pair_add_body(count, place_ref, *refs):
    out_ref = refs[-1]
    rows = refs[0].shape[0]
    for half in range(2):
        span = slice(half * rows, (half + 1) * rows)
        total = refs[half][...].astype(FULL)
        if count > 2:
            total = total + refs[2][span].astype(FULL)
        if count > 3:
            total = total + refs[3 + half][...]
        out_ref[span] = total.astype(out_ref.dtype)


def pair_add(place, block_rows, parts, arrived, bases, kind):
    rows, width = 2 * block_rows, parts[0].shape[1]
    block = pl.BlockSpec((rows // 2, width), lambda i, p: (p[0], 0))
    whole = pl.BlockSpec((rows, width), lambda i, p: (0, 0))
    half = pl.BlockSpec((rows // 2, width), lambda i, p: (0, 0))
    operands, in_specs = list(parts), [block, block]
    if arrived is not None:
        operands.append(arrived)
        in_specs.append(whole)
    if bases is not None:
        operands += bases
        in_specs += [half, half]
    return pl.pallas_call(
        functools.partial(pair_add_body, len(operands)),
        grid_spec=pltpu.PrefetchScalarGridSpec(
            num_scalar_prefetch=1, grid=(1,), in_specs=in_specs, out_specs=whole
        ),
        out_shape=jax.ShapeDtypeStruct((rows, width), kind),
        compiler_params=params(),
        cost_estimate=LIGHT,
    )(place.reshape(1).astype(jnp.int32), *operands)


def round_body(count, in_ref, *out_refs):
    rows = in_ref.shape[0] // count
    for index in range(count):
        out_refs[index][...] = in_ref[index * rows : (index + 1) * rows].astype(LOW)


def round_low(value, count):
    rows, width = value.shape
    tile = min(width, 512)
    return pl.pallas_call(
        functools.partial(round_body, count),
        grid=(width // tile,),
        in_specs=[pl.BlockSpec((rows, tile), lambda i: (0, i))],
        out_specs=[pl.BlockSpec((rows // count, tile), lambda i: (0, i))] * count,
        out_shape=[jax.ShapeDtypeStruct((rows // count, width), LOW)] * count,
        compiler_params=params(),
        cost_estimate=LIGHT,
    )(value)


def norm_back_body(count, steps, place_ref, source_ref, arrived_ref, part_ref, gain_ref, *refs):
    bases, out_refs = refs[:count], refs[count:]
    base = bases[0][...]
    if count == 2:
        base = jnp.where(pl.program_id(0) < steps // 2, base, bases[1][...])
    source = source_ref[...].astype(FULL)
    back = arrived_ref[...].astype(FULL) + part_ref[...].astype(FULL)
    inverse = lax.rsqrt(jnp.mean(source * source, axis=-1, keepdims=True) + NORM_EPS)
    normal = source * inverse
    scaled = gain_ref[...] * back
    grad = base + inverse * (scaled - normal * jnp.mean(normal * scaled, axis=-1, keepdims=True))
    out_refs[0][...] = grad
    total = jnp.sum(back * normal, axis=0, keepdims=True)

    @pl.when(pl.program_id(0) == 0)
    def _():
        out_refs[1][...] = total

    @pl.when(pl.program_id(0) > 0)
    def _():
        out_refs[1][...] += total

    if len(out_refs) > 2:
        out_refs[2][...] = grad.astype(LOW)


def norm_back(place, source, arrived, part, gain, bases, base_first, low):
    rows, width = source.shape
    tile = min(rows, 64)
    steps = rows // tile
    row = pl.BlockSpec((tile, width), lambda i, p: (i, 0))
    whole = pl.BlockSpec((1, width), lambda i, p: (0, 0))
    shapes = [jax.ShapeDtypeStruct((rows, width), FULL), jax.ShapeDtypeStruct((1, width), FULL)]
    out_specs = [row, whole]
    if len(bases) == 1:
        base_specs = [pl.BlockSpec((tile, width), lambda i, p: (base_first // tile + i, 0))]
    else:
        base_specs = [
            pl.BlockSpec((tile, width), lambda i, p: (jnp.minimum(i, steps // 2 - 1), 0)),
            pl.BlockSpec((tile, width), lambda i, p: (jnp.maximum(i - steps // 2, 0), 0)),
        ]
    if low:
        shapes.append(jax.ShapeDtypeStruct((rows, width), LOW))
        out_specs.append(row)
    return pl.pallas_call(
        functools.partial(norm_back_body, len(bases), steps),
        grid_spec=pltpu.PrefetchScalarGridSpec(
            num_scalar_prefetch=1,
            grid=(steps,),
            in_specs=[
                row,
                row,
                pl.BlockSpec((tile, width), lambda i, p: (p[0] * steps + i, 0)),
                whole,
            ]
            + base_specs,
            out_specs=out_specs,
        ),
        out_shape=shapes,
        compiler_params=params(),
        cost_estimate=LIGHT,
    )(place.reshape(1).astype(jnp.int32), source, arrived, part, gain, *bases)


def mix_back_body(count, place_ref, *refs):
    lows, weight_ref, out_refs = refs[:count], refs[count], refs[count + 1 :]
    total = None
    shards, _, _, shard = weight_ref.shape
    for index in range(shards):
        span = slice(index * shard, (index + 1) * shard)
        left = jnp.concatenate([low[:, span] for low in lows], axis=0)
        product = lax.dot_general(left, weight_ref[index, 0], NT, preferred_element_type=FULL)
        total = product if total is None else total + product
    value = total.astype(LOW)
    for step, out in enumerate(out_refs):

        @pl.when(pl.program_id(0) == step)
        def _():
            out[...] = value


def mix_back(targets, lows, weight):
    rows, width = lows[0].shape
    shards, count, cols, shard = weight.shape
    total = rows * len(lows)
    spec = pl.BlockSpec((total, cols), lambda i, p: (0, 0))
    return pl.pallas_call(
        functools.partial(mix_back_body, len(lows)),
        grid_spec=pltpu.PrefetchScalarGridSpec(
            num_scalar_prefetch=1,
            grid=(count,),
            in_specs=[pl.BlockSpec((rows, width), lambda i, p: (0, 0))] * len(lows)
            + [pl.BlockSpec((shards, 1, cols, shard), lambda i, p: (0, p[i], 0, 0))],
            out_specs=[spec] * count,
        ),
        out_shape=[jax.ShapeDtypeStruct((total, cols), LOW)] * count,
        compiler_params=params(),
        cost_estimate=LIGHT,
    )(targets, *lows, weight)


def project_back_body(place_ref, back_ref, weight_ref, out_ref):
    total = None
    for part in range(3):
        product = lax.dot_general(back_ref[part], weight_ref[part], NT, preferred_element_type=FULL)
        total = product if total is None else total + product
    out_ref[...] = total.astype(LOW)


def project_back(place, back, weight, rows):
    _, width, cols = weight.shape
    tile = min(512, width)
    return pl.pallas_call(
        project_back_body,
        grid_spec=pltpu.PrefetchScalarGridSpec(
            num_scalar_prefetch=1,
            grid=(width // tile,),
            in_specs=[
                pl.BlockSpec((3, rows, cols), lambda i, p: (0, p[0], 0)),
                pl.BlockSpec((3, tile, cols), lambda i, p: (0, i, 0)),
            ],
            out_specs=pl.BlockSpec((rows, tile), lambda i, p: (0, i)),
        ),
        out_shape=jax.ShapeDtypeStruct((rows, width), LOW),
        compiler_params=params(),
        cost_estimate=LIGHT,
    )(place.reshape(1), back, weight)


def adam_step(weight, grad, first, second, factor, rate, decay):
    clipped = grad * factor
    first_new = BETA_ONE * first + (1.0 - BETA_ONE) * clipped
    second_new = BETA_TWO * second + (1.0 - BETA_TWO) * clipped * clipped
    first_hat = first_new / (1.0 - BETA_ONE**STEP)
    second_hat = second_new / (1.0 - BETA_TWO**STEP)
    weight_new = weight - rate * (first_hat / (jnp.sqrt(second_hat) + ADAM_EPS) + decay * weight)
    return (weight_new, weight_new.astype(LOW), first_new, second_new)


def adam_body(rates, factor_ref, *refs):
    count = len(rates)
    factor = factor_ref[0]
    for index, rate in enumerate(rates):
        weight, grad, first, second = refs[4 * index : 4 * index + 4]
        outs = refs[4 * count + 4 * index : 4 * count + 4 * index + 4]
        if len(weight.shape) == 3:
            cols = weight.shape[2]
            for part in range(weight.shape[0]):
                piece = grad[:, part * cols : (part + 1) * cols].astype(FULL)
                new = adam_step(weight[part], piece, first[part], second[part], factor, rate, DECAY_RATE)
                for out, value in zip(outs, new):
                    out[part] = value
        else:
            new = adam_step(weight[...], grad[...].astype(FULL), first[...], second[...], factor, rate, DECAY_RATE)
            for out, value in zip(outs, new):
                out[...] = value


def adam_all(factor, groups, rates):
    steps = 8
    for weight, _, _, _ in groups:
        steps = min(steps, weight.shape[-2] // 16)
    in_specs, out_specs, shapes, operands = [], [], [], []
    for weight, grad, first, second in groups:
        rows, cols = weight.shape[-2] // steps, weight.shape[-1]
        if weight.ndim == 3:
            spec = pl.BlockSpec((weight.shape[0], rows, cols), lambda i, f: (0, i, 0))
        else:
            spec = pl.BlockSpec((rows, cols), lambda i, f: (i, 0))
        grad_spec = pl.BlockSpec((rows, grad.shape[1]), lambda i, f: (i, 0))
        in_specs += [spec, grad_spec, spec, spec]
        out_specs += [spec] * 4
        operands += [weight, grad, first, second]
        for kind in (FULL, LOW, FULL, FULL):
            shapes.append(jax.ShapeDtypeStruct(weight.shape, kind))
    out = pl.pallas_call(
        functools.partial(adam_body, rates),
        grid_spec=pltpu.PrefetchScalarGridSpec(
            num_scalar_prefetch=1, grid=(steps,), in_specs=in_specs, out_specs=out_specs
        ),
        out_shape=shapes,
        compiler_params=params(60 * 1024 * 1024),
        cost_estimate=LIGHT,
    )(factor.reshape(1), *operands)
    return [tuple(out[4 * index : 4 * index + 4]) for index in range(len(groups))]


def lay_body(spots, me_ref, *refs):
    count = len(spots)
    out_ref = refs[count]
    for piece, spot in zip(refs, spots):
        if isinstance(spot, tuple):
            rows = piece.shape[0]
            out_ref[me_ref[0] ^ spot[0], spot[1] * rows : (spot[1] + 1) * rows] = piece[...]
        else:
            out_ref[lax.rem(me_ref[0] + count - spot, count)] = piece[...]


def lay(me, pieces, spots):
    rows, width = pieces[0].shape
    if isinstance(spots[0], tuple):
        shape = (len(pieces) // 2, 2 * rows, width)
    else:
        shape = (len(pieces), rows, width)
    return pl.pallas_call(
        functools.partial(lay_body, spots),
        in_specs=[pl.BlockSpec(memory_space=pltpu.SMEM)] + [pl.BlockSpec(memory_space=pltpu.VMEM)] * len(pieces),
        out_specs=pl.BlockSpec(memory_space=pltpu.VMEM),
        out_shape=jax.ShapeDtypeStruct(shape, LOW),
        compiler_params=params(),
        cost_estimate=LIGHT,
    )(me.reshape(1).astype(jnp.int32), *pieces)


def lay_cores_body(core_ref, mine_ref, other_ref, out_ref):
    mine, other = mine_ref[...], other_ref[...]
    out_ref[0, 0] = jnp.where(core_ref[0] == 0, mine, other)[0]
    out_ref[0, 1] = jnp.where(core_ref[0] == 0, other, mine)[0]


def lay_cores(core, mine, other):
    chips, rows, width = mine.shape
    spec = pl.BlockSpec((1, rows, width), lambda i, c: (i, 0, 0))
    return pl.pallas_call(
        lay_cores_body,
        grid_spec=pltpu.PrefetchScalarGridSpec(
            num_scalar_prefetch=1,
            grid=(chips,),
            in_specs=[spec, spec],
            out_specs=pl.BlockSpec((1, 2, rows, width), lambda i, c: (i, 0, 0, 0)),
        ),
        out_shape=jax.ShapeDtypeStruct((chips, 2, rows, width), LOW),
        compiler_params=params(),
        cost_estimate=LIGHT,
    )(core, mine, other)


def squares(value):
    wide = value.astype(FULL)
    return jnp.sum(wide * wide)


def after(value, *others):
    if not others:
        return value
    return lax.optimization_barrier((value, *others))[0]


def per_device(
    chips,
    cores,
    bkts,
    block_in,
    cotangent,
    buckets,
    qkv_weight,
    qkv_first,
    qkv_second,
    out_weight,
    out_first,
    out_second,
    up_weight,
    up_first,
    up_second,
    down_weight,
    down_first,
    down_second,
    norm_gains,
    gains_first,
    gains_second,
):
    toks = chips * cores
    tok = ("chip", "core")
    group = lax.axis_index("bkt")
    core = lax.axis_index("core")
    chip = lax.axis_index("chip")
    core_id = core.reshape(1).astype(jnp.int32)
    rows, width = block_in.shape
    half = rows // 2
    length = rows * bkts
    ring = [(i, (i + 1) % bkts) for i in range(bkts)]

    last = []

    def at(value, *others):
        return after(value, *last, *others)

    def did(value):
        last[:] = [value]
        return value

    def wait(value):
        return did(after(value, *last))

    def pass_on(name, value, *others):
        with jax.named_scope(name):
            return lax.ppermute(at(value, *others), "bkt", ring)

    def owner(step):
        return lax.rem(group - step + bkts, bkts)

    places = jnp.stack([owner(step) for step in range(bkts)]).astype(jnp.int32)

    def rows_of(value, step):
        size = value.shape[0] // bkts
        return lax.dynamic_slice_in_dim(value, owner(step) * size, size, 0)

    def add(arrived, value, step):
        return did(ring_add(owner(step), at(arrived), value, LOW))

    def add_final(arrived, value):
        return did(ring_add(owner(0), at(arrived), value, FULL))

    def swap(name, values):
        with jax.named_scope(name + "_swap"):
            return [lax.ppermute(at(value), "core", [(0, 1), (1, 0)]) for value in values]

    def core_add(kept, arrived):
        return did(core_add_kernel(at(kept), arrived))

    def chip_sum(value):
        value = value.reshape(chips * value.shape[1], *value.shape[2:])
        return lax.psum_scatter(value, "chip", scatter_dimension=0, tiled=True)

    by_bits = chips & (chips - 1) == 0

    qkv_full = lax.all_gather(did(qkv_weight.astype(LOW)), tok, axis=1, tiled=True)
    x_held = [block_in, pass_on("x1", block_in)]
    (out_low,) = round_low(at(out_weight), 1)
    did(out_low)
    cols = qkv_weight.shape[2]
    lower_a = did(pack_half(0, at(cotangent), cols))
    lower_b = [did(pack_half(1, at(cotangent), cols))]
    x_held[1] = wait(x_held[1])
    x_held.append(pass_on("x2", x_held[1]))
    out_held = [out_low, pass_on("out1", out_low)]
    (up_low,) = round_low(at(up_weight), 1)
    up_full = lax.all_gather(did(up_low), tok, axis=0, tiled=True)
    gain_width = norm_gains.shape[1]
    gain_line = jnp.zeros((toks, 2, gain_width), FULL)
    gain_line = lax.dynamic_update_slice(
        gain_line, norm_gains.astype(LOW).astype(FULL)[None], (lax.axis_index(tok), 0, 0)
    )
    if by_bits:
        for axis, size in (("core", cores), ("chip", chips)):
            for bit in range(size.bit_length() - 1):
                perm = [(i, i ^ (1 << bit)) for i in range(size)]
                with jax.named_scope("gains"):
                    gain_line = did(gain_line + lax.ppermute(at(gain_line), axis, perm))
    else:
        gain_line = did(lax.psum(at(gain_line), tok))
    gain_float = gain_line.transpose(1, 0, 2).reshape(2, width)
    cosine, sine = rotary_tables(length)
    for step in range(3, bkts):
        x_held[-1] = wait(x_held[-1])
        out_held[-1] = wait(out_held[-1])
        x_held.append(pass_on("x" + str(step), x_held[-1], cosine, sine))
        out_held.append(pass_on("out" + str(step - 1), out_held[-1]))

    carried = None
    for step in range(bkts - 1):
        carried = project(
            owner(step).reshape(1), at(x_held[step]), gain_float[0:1], qkv_full, cosine, sine, carried
        )
        did(carried[0])
    x_held[-1] = wait(x_held[-1])
    out_held[-1] = wait(out_held[-1])
    out_held.append(pass_on("out" + str(bkts - 1), out_held[-1]))
    normed_one, qkv, seq_in = project(
        owner(bkts - 1).reshape(1), at(x_held[-1]), gain_float[0:1], qkv_full, cosine, sine, carried
    )
    did(normed_one)
    out_held[-1] = wait(out_held[-1])
    out_depth, out_width = out_weight.shape
    lower_b.append(pass_on("cotangent_b1", lower_b[0]))
    out_line = did(lay(group, [at(out_held[0])] + out_held[1:], list(range(bkts))))
    out_full = lax.all_gather(after(out_line, up_full), tok, axis=0, tiled=False)
    (down_low,) = round_low(at(down_weight), 1)
    down_full = lax.all_gather(did(down_low), tok, axis=1, tiled=True)
    seq_in = seq_in.reshape(bkts, rows, width)

    upper = length // 2
    slab, log_a = attend(0, bkts, at(qkv), lower_a)
    slabs = [[did(slab)], []]

    def next_slab(part):
        held = slabs[part]
        if len(held) > 1:
            held[-1] = wait(held[-1])
        value = held[-1]
        if part == 1 and len(held) == bkts - 1:
            value = value[:upper]
        held.append(pass_on("slab" + "ab"[part] + str(len(held)), value))

    lower_b[1] = wait(lower_b[1])
    next_slab(0)
    slab, log_b = attend(1, bkts, at(qkv), lower_b[1])
    slabs[1].append(did(slab))
    logs = [log_a, log_b]
    for step in range(2, bkts):
        next_slab(0)
    slabs[0][-1] = wait(slabs[0][-1])
    for step in range(1, bkts - 2):
        next_slab(1)

    live = (buckets >= group).astype(FULL)
    acc = did(mix_first(0, places, at(seq_in), slabs[0][:-1], out_full))
    normed_a, middle_a, mixed_a = mix_last(places, acc, gain_float[1:2], slabs[0], out_full)
    did(normed_a)
    next_slab(1)
    hidden_a, inner_a, low_a = hidden_units(
        places, live, at(normed_a), up_full, down_full, [(slab, 1) for slab in slabs[0]]
    )
    did(inner_a)
    next_slab(1)
    back_a = did(product(at(inner_a), up_full, True))
    sum_a = did(rows_of(back_a, 1))
    arrived_a = pass_on("sum_a1", sum_a)
    acc = did(mix_first(1, places, at(seq_in), slabs[1][:-1], out_full))
    slabs[1][-1] = wait(slabs[1][-1])
    normed_b, middle_b, mixed_b = mix_last(places, at(acc), gain_float[1:2], slabs[1], out_full)
    did(normed_b)
    sum_a = add(arrived_a, back_a, 2)
    arrived_a = pass_on("sum_a2", sum_a)

    hidden_b, inner_b, low_b = hidden_units(
        places,
        live,
        at(normed_b),
        up_full,
        down_full,
        [(lower_b[0], 0), (lower_b[1], 0)] + [(slab, 1) for slab in slabs[1][1:-1]],
    )
    did(inner_b)
    sum_a = add(arrived_a, back_a, 3)
    arrived_a = pass_on("sum_a3", sum_a)
    back_b = did(product(at(inner_b), up_full, True))
    sum_b = did(rows_of(at(back_b), 1))
    arrived_b = pass_on("sum_b1", sum_b)
    up_kept, up_sent = weight_grad(core_id, [normed_a, normed_b], [at(inner_a), inner_b], chips, 0)
    did(up_kept)

    first = jnp.zeros((), jnp.int32)
    targets = jnp.stack([lax.rem(group + step, bkts) for step in range(bkts)]).astype(jnp.int32)

    def middle_back(part, middle, arrived, back):
        grad, gain_sum, low = norm_back(
            owner(0), middle, at(arrived), back, gain_float[1:2], [cotangent], part * half, True
        )
        did(low)
        return grad, low, gain_sum

    def exchange(found):
        with jax.named_scope("exchange"):
            for step in range(1, bkts):
                found[step] = lax.ppermute(
                    at(found[step]), "bkt", [(i, (i + step) % bkts) for i in range(bkts)]
                )

    arrived_a = wait(arrived_a)
    sum_b = add(arrived_b, back_b, 2)
    arrived_b = pass_on("sum_b2", sum_b)
    up_arrived = swap("up_grad", up_sent)
    grad_a, mid_low_a, gain_a = middle_back(0, middle_a, arrived_a, back_a)
    prod_b = did(product(at(hidden_b), down_full, False))
    sum_b = add(arrived_b, back_b, 3)
    up_core = core_add(up_kept, up_arrived)
    up_part = chip_sum(up_core)
    arrived_b = pass_on("sum_b3", sum_b)
    down_kept, down_sent = weight_grad(core_id, [hidden_a, hidden_b], [at(low_a), low_b], chips, 1)
    did(down_kept)
    grad_b, mid_low_b, gain_b = middle_back(1, middle_b, arrived_b, back_b)
    down_arrived = swap("down_grad", down_sent)
    pieces = list(mix_back(targets, [mid_low_a, at(mid_low_b)], out_full))
    did(pieces[0])
    down_core = core_add(down_kept, down_arrived)
    down_part = chip_sum(down_core)
    exchange(pieces)
    out_kept, out_sent = weight_grad(
        core_id, [at(mixed_a), mixed_b], [mid_low_a, mid_low_b], chips, 1
    )
    did(out_kept)
    prod_a = did(product(at(hidden_a), down_full, False))
    prods = [prod_a, prod_b]
    ffn = did(pair_add(owner(1), half, [at(prod_a), prod_b], None, None, LOW))
    pieces = pieces[:1] + [wait(piece) for piece in pieces[1:]]
    arrived_f = pass_on("ffn1", ffn)
    out_arrived = swap("out_grad", out_sent)

    back_project = did(attend_back(places, at(qkv), pieces, logs, cosine, sine))
    total = did(project_back(owner(1), at(back_project), qkv_full, rows))
    arrived_f = wait(arrived_f)
    out_core = core_add(out_kept, out_arrived)
    out_sum = chip_sum(out_core)
    arrived = pass_on("back1", total)
    up_squares = did(squares(at(up_part)))
    qkv_kept, qkv_sent = project_grad(core_id, normed_one, at(back_project), chips)
    did(qkv_kept)
    own = did(project_back(owner(2), at(back_project), qkv_full, rows))
    total = did(ring_add(first, at(arrived), own, LOW))
    arrived = pass_on("back2", total)
    qkv_arrived = swap("qkv_grad", qkv_sent)
    own = did(project_back(owner(3), at(back_project), qkv_full, rows))
    last_own = did(project_back(owner(0), at(back_project), qkv_full, rows))
    down_squares = did(squares(at(down_part)))
    total = did(ring_add(first, at(arrived), own, LOW))
    qkv_core = core_add(qkv_kept, qkv_arrived)
    qkv_part = chip_sum(qkv_core)
    arrived = pass_on("back3", total)
    arrived_out = pass_on("out_sum1", rows_of(out_sum, 1))
    ffn = did(pair_add(owner(2), half, prods, at(arrived_f), None, LOW))
    block_in_grad, gain_one = norm_back(
        first, block_in, at(arrived), last_own, gain_float[0:1], [grad_a, grad_b], 0, False
    )
    did(gain_one)
    for step in range(2, bkts):
        out_part = add(arrived_out, out_sum, step)
        arrived_out = pass_on("out_sum" + str(step), out_part)
    out_part = add_final(arrived_out, out_sum)
    arrived_f = pass_on("ffn2", ffn)
    out_squares = did(squares(at(out_part)))
    gain_grad_one = gain_one[0]
    gain_grad_two = (gain_a + gain_b)[0]

    weight_squares = did(up_squares + down_squares + out_squares + squares(at(qkv_part)))
    packed = jnp.concatenate(
        [gain_grad_one, gain_grad_two, jnp.broadcast_to(weight_squares, (HD,))]
    )
    for axis, size in (("core", cores), ("chip", chips), ("bkt", bkts)):
        if size & (size - 1):
            packed = lax.psum(packed, axis)
        else:
            step = 1
            while step < size:
                packed = packed + lax.ppermute(packed, axis, [(i, i ^ step) for i in range(size)])
                if axis == "bkt" and step == 1:
                    ffn = pair_add(owner(3), half, prods, after(arrived_f, packed), None, LOW)
                step *= 2
    did(packed)
    arrived_f = pass_on("ffn3", ffn)
    gain_total = packed[: 2 * width].reshape(2, width)
    grad_norm = jnp.sqrt(packed[2 * width] + jnp.sum(gain_total * gain_total))
    factor = jnp.minimum(1.0, CLIP_NORM / grad_norm)
    gain_part = lax.dynamic_slice_in_dim(gain_total, lax.axis_index(tok) * gain_width, gain_width, 1)
    updated = adam_all(
        factor,
        [
            (qkv_weight, qkv_part, qkv_first, qkv_second),
            (out_weight, out_part, out_first, out_second),
            (up_weight, up_part, up_first, up_second),
            (down_weight, down_part, down_first, down_second),
        ],
        (D ** (-0.5), (H * HD // 16) ** (-0.5), D ** (-0.5), FF ** (-0.5)),
    )
    block_out = pair_add(
        owner(0), half, prods, after(arrived_f, updated[0][0]), [middle_a, middle_b], FULL
    )
    gain_out = adam_step(norm_gains, gain_part, gains_first, gains_second, factor, GAIN_RATE, 0.0)
    return (block_out, block_in_grad, grad_norm, *[value for new in updated for value in new], *gain_out)


def solution(mesh):
    toks, bkts = mesh.shape["tok"], mesh.shape["bkt"]
    cores = 2
    chips = toks // cores
    tok = ("chip", "core")
    rows = P(("chip", "core", "bkt"), None)
    qkv = P(None, tok, "bkt")
    tall = P("bkt", tok)
    wide = P(tok, "bkt")
    gains = P(None, tok)
    return jax.shard_map(
        functools.partial(per_device, chips, cores, bkts),
        mesh=Mesh(mesh.devices.reshape(chips, cores, bkts), ("chip", "core", "bkt")),
        in_specs=(rows, rows, P(tok), *[qkv] * 3, *[tall] * 3, *[wide] * 3, *[tall] * 3, *[gains] * 3),
        out_specs=(rows, rows, P(), *[qkv] * 4, *[tall] * 4, *[wide] * 4, *[tall] * 4, *[gains] * 4),
        check_vma=False,
    )
```

```python
import functools
import jax
import jax.numpy as jnp
from jax import lax
from jax.experimental import pallas as pl
from jax.experimental.pallas import tpu as pltpu
from jax.sharding import Mesh, PartitionSpec as P

D = 2048
H = 16
HD = 128
FF = 8192
STEP = 10

NORM_EPS = 1e-05
ADAM_EPS = 1e-08
CLIP_NORM = 1.0
BETA_ONE = 0.9
BETA_TWO = 0.95
DECAY_RATE = 0.1
GAIN_RATE = 0.3
ROPE_BASE = 10000.0

LOW = jnp.bfloat16
FULL = jnp.float32
SCALE = HD ** (-0.5)
VMEM_BYTES = 48 * 1024 * 1024
NN = (((1,), (0,)), ((), ()))
NT = (((1,), (1,)), ((), ()))
TN = (((0,), (0,)), ((), ()))


def rotary_tables(length):
    positions = jnp.arange(length).astype(FULL)[:, None]
    freq_index = jnp.arange(HD // 2).astype(FULL)
    angles = positions * (ROPE_BASE ** (-2.0 * freq_index / HD))[None, :]
    cosine = jnp.cos(angles)
    sine = jnp.sin(angles)
    return (jnp.concatenate([cosine, cosine], axis=-1), jnp.concatenate([-sine, sine], axis=-1))


LIGHT = pl.CostEstimate(flops=1, bytes_accessed=1, transcendentals=0)


def params(vmem=VMEM_BYTES):
    return pltpu.CompilerParams(vmem_limit_bytes=vmem)


def project_body(place_ref, x_ref, gain_ref, w_ref, cos_ref, sin_ref, *rest):
    normed_ref, out_ref, seq_ref = rest[-3:]
    part = pl.program_id(0)

    @pl.when(part == 0)
    def _():
        low = x_ref[...]
        seq_ref[...] = low
        values = low.astype(FULL)
        inverse = lax.rsqrt(jnp.mean(values * values, axis=-1, keepdims=True) + NORM_EPS)
        normed_ref[...] = (values * inverse * gain_ref[...]).astype(LOW)

    product = jnp.dot(normed_ref[...], w_ref[0], preferred_element_type=FULL)

    @pl.when(part < 2)
    def _():
        for head in range(product.shape[1] // HD):
            one = product[:, head * HD : (head + 1) * HD]
            turned = one * cos_ref[...] + pltpu.roll(one, HD // 2, 1) * sin_ref[...]
            out_ref[0, :, head * HD : (head + 1) * HD] = turned.astype(LOW)

    @pl.when(part == 2)
    def _():
        out_ref[0] = product.astype(LOW)


def project(place, x, gain, weight, cosine, sine, carried):
    rows, width = x.shape
    length = cosine.shape[0]
    cols = weight.shape[2]
    shapes = [
        jax.ShapeDtypeStruct((length, width), LOW),
        jax.ShapeDtypeStruct((3, length, cols), LOW),
        jax.ShapeDtypeStruct((length, width), LOW),
    ]
    in_specs = [
        pl.BlockSpec((rows, width), lambda c, p: (0, 0)),
        pl.BlockSpec((1, width), lambda c, p: (0, 0)),
        pl.BlockSpec((1, width, cols), lambda c, p: (c, 0, 0)),
        pl.BlockSpec((rows, HD), lambda c, p: (p[0], 0)),
        pl.BlockSpec((rows, HD), lambda c, p: (p[0], 0)),
    ]
    aliases = {}
    if carried is not None:
        in_specs += [pl.BlockSpec(memory_space=pl.ANY)] * 3
        aliases = {6: 0, 7: 1, 8: 2}
    return pl.pallas_call(
        project_body,
        grid_spec=pltpu.PrefetchScalarGridSpec(
            num_scalar_prefetch=1,
            grid=(3,),
            in_specs=in_specs,
            out_specs=[
                pl.BlockSpec((rows, width), lambda c, p: (p[0], 0)),
                pl.BlockSpec((1, rows, cols), lambda c, p: (c, p[0], 0)),
                pl.BlockSpec((rows, width), lambda c, p: (p[0], 0)),
            ],
        ),
        out_shape=shapes,
        input_output_aliases=aliases,
        compiler_params=params(),
        cost_estimate=LIGHT,
    )(place, x, gain, weight, cosine, sine, *(carried or ()))


def pack_body(in_ref, out_ref):
    out_ref[...] = in_ref[...].astype(LOW)


def pack_half(half, cotangent, cols):
    rows, width = cotangent.shape
    count = width // cols
    return pl.pallas_call(
        pack_body,
        grid=(count,),
        in_specs=[pl.BlockSpec((rows // 2, cols), lambda j: (half, j))],
        out_specs=pl.BlockSpec((rows // 2, cols), lambda j: (j, 0)),
        out_shape=jax.ShapeDtypeStruct((count * rows // 2, cols), LOW),
        compiler_params=params(),
        cost_estimate=LIGHT,
    )(cotangent)


def attend_body(half, blocks, q_ref, k_ref, v_ref, lower_ref, ring_ref, log_ref):
    length = q_ref.shape[1]
    block = length // blocks
    rows = block // 2
    ring_ref[length // 2 :] = lower_ref[...]
    for index in range(blocks):
        first = index * block + half * rows
        last = first + rows
        query = q_ref[0, first:last]
        scores = (
            lax.dot_general(query, k_ref[0, :last], NT, preferred_element_type=FULL) * SCALE
        )
        row = lax.broadcasted_iota(jnp.int32, scores.shape, 0) + first
        col = lax.broadcasted_iota(jnp.int32, scores.shape, 1)
        scores = jnp.where(row >= col, scores, -1e30)
        peak = jnp.max(scores, axis=-1, keepdims=True)
        expo = jnp.exp(scores - peak)
        total = jnp.sum(expo, axis=-1, keepdims=True)
        probs = (expo / total).astype(LOW)
        mixed = jnp.dot(probs, v_ref[0, :last], preferred_element_type=FULL)
        ring_ref[index * rows : (index + 1) * rows] = mixed.astype(LOW)
        log_ref[index * rows : (index + 1) * rows] = jnp.broadcast_to(
            peak + jnp.log(total), (rows, HD)
        )


def attend(half, blocks, qkv, lower):
    _, length, cols = qkv.shape
    heads = cols // HD
    below = lower.shape[0]
    return pl.pallas_call(
        functools.partial(attend_body, half, blocks),
        grid=(heads,),
        in_specs=[
            pl.BlockSpec((1, length, HD), lambda h: (0, 0, h)),
            pl.BlockSpec((1, length, HD), lambda h: (1, 0, h)),
            pl.BlockSpec((1, length, HD), lambda h: (2, 0, h)),
            pl.BlockSpec((below, HD), lambda h: (0, h)),
        ],
        out_specs=[
            pl.BlockSpec((length // 2 + below, HD), lambda h: (0, h)),
            pl.BlockSpec((length // 2, HD), lambda h: (0, h)),
        ],
        out_shape=[
            jax.ShapeDtypeStruct((length // 2 + below, cols), LOW),
            jax.ShapeDtypeStruct((length // 2, cols), FULL),
        ],
        compiler_params=params(),
        cost_estimate=LIGHT,
    )(qkv, qkv, qkv, lower)


def attend_back_body(blocks, place_ref, q_ref, k_ref, v_ref, log_a_ref, log_b_ref, cos_ref, sin_ref, *rest):
    pieces = rest[:blocks]
    out_ref, key_acc, value_acc, back_ref = rest[blocks:]
    length = q_ref.shape[1]
    block = length // blocks
    rows = block // 2
    for step in range(blocks):
        first = pl.multiple_of(place_ref[step] * block, block)
        back_ref[pl.ds(first, block), :] = pieces[step][...]

    def turn_back(one, cosine, sine):
        return one * cosine - pltpu.roll(one, HD // 2, 1) * sine

    for index in range(blocks):
        first, last = index * block, (index + 1) * block
        query = q_ref[0, first:last]
        back = back_ref[first:last]
        keys = k_ref[0, :last]
        log_total = jnp.concatenate(
            [
                log_a_ref[index * rows : (index + 1) * rows, :1],
                log_b_ref[index * rows : (index + 1) * rows, :1],
            ],
            axis=0,
        )
        scores = lax.dot_general(query, keys, NT, preferred_element_type=FULL) * SCALE
        row = lax.broadcasted_iota(jnp.int32, scores.shape, 0) + first
        col = lax.broadcasted_iota(jnp.int32, scores.shape, 1)
        probs = jnp.exp(jnp.where(row >= col, scores, -1e30) - log_total)
        back_probs = lax.dot_general(back, v_ref[0, :last], NT, preferred_element_type=FULL)
        centre = jnp.sum(probs * back_probs, axis=-1, keepdims=True)
        back_scores = (probs * (back_probs - centre)).astype(LOW)
        query_grad = jnp.dot(back_scores, keys, preferred_element_type=FULL) * SCALE
        out_ref[0, first:last] = turn_back(query_grad, cos_ref[first:last], sin_ref[first:last]).astype(LOW)
        key_part = lax.dot_general(back_scores, query, TN, preferred_element_type=FULL)
        value_part = lax.dot_general(probs.astype(LOW), back, TN, preferred_element_type=FULL)
        if index > 0:
            key_acc[:first] += key_part[:first]
            value_acc[:first] += value_part[:first]
        key_acc[first:last] = key_part[first:]
        value_acc[first:last] = value_part[first:]
    out_ref[1] = turn_back(key_acc[...] * SCALE, cos_ref[...], sin_ref[...]).astype(LOW)
    out_ref[2] = value_acc[...].astype(LOW)


def attend_back(places, qkv, pieces, logs, cosine, sine):
    _, length, cols = qkv.shape
    heads = cols // HD
    blocks = len(pieces)
    column = lambda h, p: (0, h)
    return pl.pallas_call(
        functools.partial(attend_back_body, blocks),
        grid_spec=pltpu.PrefetchScalarGridSpec(
            num_scalar_prefetch=1,
            grid=(heads,),
            in_specs=[
                pl.BlockSpec((1, length, HD), lambda h, p: (0, 0, h)),
                pl.BlockSpec((1, length, HD), lambda h, p: (1, 0, h)),
                pl.BlockSpec((1, length, HD), lambda h, p: (2, 0, h)),
                pl.BlockSpec((length // 2, HD), column),
                pl.BlockSpec((length // 2, HD), column),
                pl.BlockSpec((length, HD), lambda h, p: (0, 0)),
                pl.BlockSpec((length, HD), lambda h, p: (0, 0)),
            ]
            + [pl.BlockSpec((length // blocks, HD), column)] * blocks,
            out_specs=pl.BlockSpec((3, length, HD), lambda h, p: (0, 0, h)),
            scratch_shapes=[
                pltpu.VMEM((length, HD), FULL),
                pltpu.VMEM((length, HD), FULL),
                pltpu.VMEM((length, HD), LOW),
            ],
        ),
        out_shape=jax.ShapeDtypeStruct((3, length, cols), LOW),
        compiler_params=params(),
        cost_estimate=LIGHT,
    )(places, qkv, qkv, qkv, logs[0], logs[1], cosine, sine, *pieces)


def mix_first_body(count, place_ref, seq_ref, *rest):
    slabs, weights, acc_ref = rest[:count], rest[count : 2 * count], rest[2 * count]
    blocks, rows, width = seq_ref.shape
    shards, _, _, shard = weights[0].shape
    for index in range(shards):
        span = slice(index * shard, (index + 1) * shard)
        total = seq_ref[:, :, span].reshape(blocks * rows, shard).astype(FULL)
        for slab, weight in zip(slabs, weights):
            total = total + jnp.dot(slab[...], weight[index, 0], preferred_element_type=FULL)
        acc_ref[:, span] = total


def mix_first(part, places, seq_in, slabs, weight):
    blocks, block, width = seq_in.shape
    half = block // 2
    shards, _, cols, shard = weight.shape
    tile = max(1, 512 // shard)
    count = len(slabs)

    def weight_spec(step):
        return pl.BlockSpec((tile, 1, cols, shard), lambda i, p: (i, p[step], 0, 0))

    return pl.pallas_call(
        functools.partial(mix_first_body, count),
        grid_spec=pltpu.PrefetchScalarGridSpec(
            num_scalar_prefetch=1,
            grid=(shards // tile,),
            in_specs=[pl.BlockSpec((blocks, half, tile * shard), lambda i, p: (0, part, i))]
            + [pl.BlockSpec((blocks * half, cols), lambda i, p: (0, 0))] * count
            + [weight_spec(step) for step in range(count)],
            out_specs=pl.BlockSpec((blocks * half, tile * shard), lambda i, p: (0, i)),
        ),
        out_shape=jax.ShapeDtypeStruct((blocks * half, width), FULL),
        compiler_params=params(),
        cost_estimate=LIGHT,
    )(places, seq_in, *slabs, *[weight] * count)


def mix_last_body(count, place_ref, acc_ref, gain_ref, weight_ref, *rest):
    slabs = rest[:count]
    normed_ref, middle_ref, mixed_ref = rest[count:]
    cols = slabs[0].shape[1]
    slab = slabs[-1][...]
    parts = [
        jnp.dot(slab, weight_ref[index, 0], preferred_element_type=FULL)
        for index in range(weight_ref.shape[0])
    ]
    middle = acc_ref[...] + jnp.concatenate(parts, axis=1)
    inverse = lax.rsqrt(jnp.mean(middle * middle, axis=-1, keepdims=True) + NORM_EPS)
    normed_ref[...] = (middle * inverse * gain_ref[...]).astype(LOW)

    @pl.when(pl.program_id(0) == place_ref[0])
    def _():
        middle_ref[...] = middle
        for step in range(count):
            first = pl.multiple_of(place_ref[step] * cols, cols)
            mixed_ref[:, pl.ds(first, cols)] = slabs[step][...]


def mix_last(places, acc, gain, slabs, weight):
    length, width = acc.shape
    shards, count, cols, shard = weight.shape
    rows = length // count
    return pl.pallas_call(
        functools.partial(mix_last_body, count),
        grid_spec=pltpu.PrefetchScalarGridSpec(
            num_scalar_prefetch=1,
            grid=(count,),
            in_specs=[
                pl.BlockSpec((rows, width), lambda i, p: (i, 0)),
                pl.BlockSpec((1, width), lambda i, p: (0, 0)),
                pl.BlockSpec((shards, 1, cols, shard), lambda i, p: (0, p[count - 1], 0, 0)),
            ]
            + [pl.BlockSpec((rows, cols), lambda i, p: (i, 0))] * count,
            out_specs=[
                pl.BlockSpec((rows, width), lambda i, p: (i, 0)),
                pl.BlockSpec((rows, width), lambda i, p: (0, 0)),
                pl.BlockSpec((rows, count * cols), lambda i, p: (0, 0)),
            ],
        ),
        out_shape=[
            jax.ShapeDtypeStruct((length, width), LOW),
            jax.ShapeDtypeStruct((rows, width), FULL),
            jax.ShapeDtypeStruct((rows, count * cols), LOW),
        ],
        compiler_params=params(),
        cost_estimate=LIGHT,
    )(places, acc, gain, weight, *slabs)


def hidden_body(count, place_ref, live_ref, normed_ref, up_ref, down_ref, *rest):
    pieces = rest[:count]
    hidden_ref, inner_ref, back_ref = rest[count:]
    cols = pieces[0].shape[1]
    rows = pieces[0].shape[0] * cols // back_ref.shape[1]

    @pl.when(pl.program_id(0) == 0)
    def _():
        for step in range(count):
            first = pl.multiple_of(place_ref[step] * rows, rows)
            for index in range(pieces[0].shape[0] // rows):
                span = slice(index * rows, (index + 1) * rows)
                back_ref[pl.ds(first, rows), index * cols : (index + 1) * cols] = pieces[step][span]

    inner = jnp.dot(normed_ref[...], up_ref[...], preferred_element_type=FULL)
    inner = jnp.maximum(inner, 0.0) * live_ref[0]
    hidden_ref[...] = (inner * inner).astype(LOW)
    back = lax.dot_general(back_ref[...], down_ref[...], NT, preferred_element_type=FULL)
    inner_ref[...] = (back * 2.0 * inner).astype(LOW)


def hidden_units(places, live, normed, up, down, pieces):
    length, width = normed.shape
    units = up.shape[1]
    tile = min(512, units)
    count = len(pieces)
    rows = length // count
    cols = pieces[0][0].shape[1]
    below = rows * width // cols
    whole = lambda i, p, l: (0, 0)

    def piece_spec(index):
        return pl.BlockSpec((below, cols), lambda i, p, l: (index, 0))

    column = lambda i, p, l: (0, i)
    return pl.pallas_call(
        functools.partial(hidden_body, count),
        grid_spec=pltpu.PrefetchScalarGridSpec(
            num_scalar_prefetch=2,
            grid=(units // tile,),
            in_specs=[
                pl.BlockSpec((length, width), whole),
                pl.BlockSpec((width, tile), column),
                pl.BlockSpec((tile, width), lambda i, p, l: (i, 0)),
            ]
            + [piece_spec(index) for _, index in pieces],
            out_specs=[
                pl.BlockSpec((length, tile), column),
                pl.BlockSpec((length, tile), column),
                pl.BlockSpec((length, width), whole),
            ],
        ),
        out_shape=[
            jax.ShapeDtypeStruct((length, units), LOW),
            jax.ShapeDtypeStruct((length, units), LOW),
            jax.ShapeDtypeStruct((length, width), LOW),
        ],
        compiler_params=params(56 * 1024 * 1024),
        cost_estimate=LIGHT,
    )(places, live, normed, up, down, *[piece for piece, _ in pieces])


def product_body(dims, left_ref, right_ref, out_ref):
    out_ref[...] = lax.dot_general(
        left_ref[...], right_ref[...], dims, preferred_element_type=FULL
    ).astype(LOW)


def product(left, right, turned):
    length, depth = left.shape
    width = right.shape[0] if turned else right.shape[1]
    tile = min(512, width)
    if turned:
        spec = pl.BlockSpec((tile, depth), lambda i: (i, 0))
    else:
        spec = pl.BlockSpec((depth, tile), lambda i: (0, i))
    return pl.pallas_call(
        functools.partial(product_body, NT if turned else NN),
        grid=(width // tile,),
        in_specs=[pl.BlockSpec((length, depth), lambda i: (0, 0)), spec],
        out_specs=pl.BlockSpec((length, tile), lambda i: (0, i)),
        out_shape=jax.ShapeDtypeStruct((length, width), LOW),
        compiler_params=params(),
        cost_estimate=LIGHT,
    )(left, right)


def split_shards(core, total, axis, first, kept_ref, sent_refs):
    shard = kept_ref.shape[1 + axis]
    count = total.shape[axis] // (2 * shard)

    def cut(index):
        span = slice(index * shard, (index + 1) * shard)
        return total[span] if axis == 0 else total[:, span]

    for index in range(count):
        even, odd = cut(2 * index), cut(2 * index + 1)
        kept_ref[index] = jnp.where(core == 0, even, odd).astype(LOW)
        sent = jnp.where(core == 0, odd, even).astype(LOW)
        if axis == 1:
            sent_refs[index][...] = sent
        else:
            for chip in range(index, len(sent_refs), count):

                @pl.when(first + index == chip)
                def _():
                    sent_refs[chip][...] = sent


def grad_body(count, axis, core_ref, *refs):
    total = None
    for index in range(count):
        product = lax.dot_general(
            refs[index][...], refs[count + index][...], TN, preferred_element_type=FULL
        )
        total = product if total is None else total + product
    kept_ref, sent_refs = refs[2 * count], refs[2 * count + 1 :]
    first = pl.program_id(0) * kept_ref.shape[0] if axis == 0 else 0
    split_shards(core_ref[0], total, axis, first, kept_ref, sent_refs)


def weight_grad(core, lefts, rights, chips, axis):
    depth = lefts[0].shape[1]
    width = rights[0].shape[1]
    tile = min(512, depth)
    shards = 2 * chips
    if axis == 1:
        shape = (depth, width // shards)
        spec = pl.BlockSpec((chips, tile, width // shards), lambda i, c: (0, i, 0))
        sent = pl.BlockSpec((tile, width // shards), lambda i, c: (i, 0))
    else:
        shape = (depth // shards, width)
        spec = pl.BlockSpec((tile * chips // depth, depth // shards, width), lambda i, c: (i, 0, 0))
        sent = pl.BlockSpec(shape, lambda i, c: (0, 0))
    out = pl.pallas_call(
        functools.partial(grad_body, len(lefts), axis),
        grid_spec=pltpu.PrefetchScalarGridSpec(
            num_scalar_prefetch=1,
            grid=(depth // tile,),
            in_specs=[pl.BlockSpec((left.shape[0], tile), lambda i, c: (0, i)) for left in lefts]
            + [pl.BlockSpec(right.shape, lambda i, c: (0, 0)) for right in rights],
            out_specs=[spec] + [sent] * chips,
        ),
        out_shape=[jax.ShapeDtypeStruct((chips, *shape), LOW)] + [jax.ShapeDtypeStruct(shape, LOW)] * chips,
        compiler_params=params(),
        cost_estimate=LIGHT,
    )(core, *lefts, *rights)
    return out[0], out[1:]


def project_grad_body(core_ref, left_ref, right_ref, kept_ref, *sent_refs):
    products = [
        lax.dot_general(left_ref[...], right_ref[part], TN, preferred_element_type=FULL)
        for part in range(3)
    ]
    first = pl.program_id(0) * kept_ref.shape[0]
    split_shards(core_ref[0], jnp.concatenate(products, axis=1), 0, first, kept_ref, sent_refs)


def project_grad(core, left, right, chips):
    length, depth = left.shape
    cols = right.shape[2]
    tile = min(512, depth)
    shards = 2 * chips
    shape = (depth // shards, 3 * cols)
    out = pl.pallas_call(
        project_grad_body,
        grid_spec=pltpu.PrefetchScalarGridSpec(
            num_scalar_prefetch=1,
            grid=(depth // tile,),
            in_specs=[
                pl.BlockSpec((length, tile), lambda i, c: (0, i)),
                pl.BlockSpec(right.shape, lambda i, c: (0, 0, 0)),
            ],
            out_specs=[pl.BlockSpec((tile * chips // depth, *shape), lambda i, c: (i, 0, 0))]
            + [pl.BlockSpec(shape, lambda i, c: (0, 0))] * chips,
        ),
        out_shape=[jax.ShapeDtypeStruct((chips, *shape), LOW)] + [jax.ShapeDtypeStruct(shape, LOW)] * chips,
        compiler_params=params(),
        cost_estimate=LIGHT,
    )(core, left, right)
    return out[0], out[1:]


def core_add_body(kept_ref, *refs):
    for index, arrived in enumerate(refs[:-1]):
        refs[-1][index] = (kept_ref[index].astype(FULL) + arrived[...].astype(FULL)).astype(LOW)


def core_add_kernel(kept, arrived):
    chips, rows, width = kept.shape
    tile = min(rows, max(16, rows // 4))
    spec = pl.BlockSpec((chips, tile, width), lambda i: (0, i, 0))
    return pl.pallas_call(
        core_add_body,
        grid=(rows // tile,),
        in_specs=[spec] + [pl.BlockSpec((tile, width), lambda i: (i, 0))] * chips,
        out_specs=spec,
        out_shape=jax.ShapeDtypeStruct(kept.shape, LOW),
        compiler_params=params(),
        cost_estimate=LIGHT,
    )(kept, *arrived)


def core_add_apart_body(count, chip_ref, kept_ref, *refs):
    for index in range(count):
        total = (kept_ref[index].astype(FULL) + refs[index][...].astype(FULL)).astype(LOW)
        for mask in range(count):

            @pl.when((chip_ref[0] ^ index) == mask)
            def _():
                refs[count + mask][...] = total


def core_add_apart(chip, kept, arrived):
    chips, rows, width = kept.shape
    tile = min(rows, max(16, rows // 4))
    spec = pl.BlockSpec((tile, width), lambda i, c: (i, 0))
    return pl.pallas_call(
        functools.partial(core_add_apart_body, chips),
        grid_spec=pltpu.PrefetchScalarGridSpec(
            num_scalar_prefetch=1,
            grid=(rows // tile,),
            in_specs=[pl.BlockSpec((chips, tile, width), lambda i, c: (0, i, 0))] + [spec] * chips,
            out_specs=[spec] * chips,
        ),
        out_shape=[jax.ShapeDtypeStruct((rows, width), LOW)] * chips,
        compiler_params=params(),
        cost_estimate=LIGHT,
    )(chip.reshape(1).astype(jnp.int32), kept, *arrived)


def add_many_body(*refs):
    total = refs[0][...].astype(FULL)
    for ref in refs[1:-1]:
        total = total + ref[...].astype(FULL)
    refs[-1][...] = total.astype(LOW)


def add_many(values):
    rows, width = values[0].shape
    tile = max(16, rows // 4)
    spec = pl.BlockSpec((tile, width), lambda i: (i, 0))
    return pl.pallas_call(
        add_many_body,
        grid=(rows // tile,),
        in_specs=[spec] * len(values),
        out_specs=spec,
        out_shape=jax.ShapeDtypeStruct((rows, width), LOW),
        compiler_params=params(),
        cost_estimate=LIGHT,
    )(*values)


def ring_add_body(place_ref, arrived_ref, part_ref, out_ref):
    out_ref[...] = (arrived_ref[...].astype(FULL) + part_ref[...].astype(FULL)).astype(out_ref.dtype)


def ring_add(place, arrived, part, kind):
    rows, width = arrived.shape
    return pl.pallas_call(
        ring_add_body,
        grid_spec=pltpu.PrefetchScalarGridSpec(
            num_scalar_prefetch=1,
            grid=(1,),
            in_specs=[
                pl.BlockSpec((rows, width), lambda i, p: (0, 0)),
                pl.BlockSpec((rows, width), lambda i, p: (p[0], 0)),
            ],
            out_specs=pl.BlockSpec((rows, width), lambda i, p: (0, 0)),
        ),
        out_shape=jax.ShapeDtypeStruct((rows, width), kind),
        compiler_params=params(),
        cost_estimate=LIGHT,
    )(place.reshape(1).astype(jnp.int32), arrived, part)


def pair_add_body(count, place_ref, *refs):
    out_ref = refs[-1]
    rows = refs[0].shape[0]
    for half in range(2):
        span = slice(half * rows, (half + 1) * rows)
        total = refs[half][...].astype(FULL)
        if count > 2:
            total = total + refs[2][span].astype(FULL)
        if count > 3:
            total = total + refs[3 + half][...]
        out_ref[span] = total.astype(out_ref.dtype)


def pair_add(place, block_rows, parts, arrived, bases, kind):
    rows, width = 2 * block_rows, parts[0].shape[1]
    tile = min(512, width)
    block = pl.BlockSpec((rows // 2, tile), lambda i, p: (p[0], i))
    whole = pl.BlockSpec((rows, tile), lambda i, p: (0, i))
    half = pl.BlockSpec((rows // 2, tile), lambda i, p: (0, i))
    operands, in_specs = list(parts), [block, block]
    if arrived is not None:
        operands.append(arrived)
        in_specs.append(whole)
    if bases is not None:
        operands += bases
        in_specs += [half, half]
    return pl.pallas_call(
        functools.partial(pair_add_body, len(operands)),
        grid_spec=pltpu.PrefetchScalarGridSpec(
            num_scalar_prefetch=1, grid=(width // tile,), in_specs=in_specs, out_specs=whole
        ),
        out_shape=jax.ShapeDtypeStruct((rows, width), kind),
        compiler_params=params(),
        cost_estimate=LIGHT,
    )(place.reshape(1).astype(jnp.int32), *operands)


def round_body(count, in_ref, *out_refs):
    rows = in_ref.shape[0] // count
    for index in range(count):
        out_refs[index][...] = in_ref[index * rows : (index + 1) * rows].astype(LOW)


def round_low(value, count):
    rows, width = value.shape
    tile = min(width, 512)
    return pl.pallas_call(
        functools.partial(round_body, count),
        grid=(width // tile,),
        in_specs=[pl.BlockSpec((rows, tile), lambda i: (0, i))],
        out_specs=[pl.BlockSpec((rows // count, tile), lambda i: (0, i))] * count,
        out_shape=[jax.ShapeDtypeStruct((rows // count, width), LOW)] * count,
        compiler_params=params(),
        cost_estimate=LIGHT,
    )(value)


def norm_back_body(count, steps, place_ref, source_ref, arrived_ref, part_ref, gain_ref, *refs):
    bases, out_refs = refs[:count], refs[count:]
    base = bases[0][...]
    if count == 2:
        base = jnp.where(pl.program_id(0) < steps // 2, base, bases[1][...])
    source = source_ref[...].astype(FULL)
    back = arrived_ref[...].astype(FULL) + part_ref[...].astype(FULL)
    inverse = lax.rsqrt(jnp.mean(source * source, axis=-1, keepdims=True) + NORM_EPS)
    normal = source * inverse
    scaled = gain_ref[...] * back
    grad = base + inverse * (scaled - normal * jnp.mean(normal * scaled, axis=-1, keepdims=True))
    out_refs[0][...] = grad
    total = jnp.sum(back * normal, axis=0, keepdims=True)

    @pl.when(pl.program_id(0) == 0)
    def _():
        out_refs[1][...] = total

    @pl.when(pl.program_id(0) > 0)
    def _():
        out_refs[1][...] += total

    if len(out_refs) > 2:
        out_refs[2][...] = grad.astype(LOW)


def norm_back(place, source, arrived, part, gain, bases, base_first, low):
    rows, width = source.shape
    tile = min(rows, 64)
    steps = rows // tile
    row = pl.BlockSpec((tile, width), lambda i, p: (i, 0))
    whole = pl.BlockSpec((1, width), lambda i, p: (0, 0))
    shapes = [jax.ShapeDtypeStruct((rows, width), FULL), jax.ShapeDtypeStruct((1, width), FULL)]
    out_specs = [row, whole]
    if len(bases) == 1:
        base_specs = [pl.BlockSpec((tile, width), lambda i, p: (base_first // tile + i, 0))]
    else:
        base_specs = [
            pl.BlockSpec((tile, width), lambda i, p: (jnp.minimum(i, steps // 2 - 1), 0)),
            pl.BlockSpec((tile, width), lambda i, p: (jnp.maximum(i - steps // 2, 0), 0)),
        ]
    if low:
        shapes.append(jax.ShapeDtypeStruct((rows, width), LOW))
        out_specs.append(row)
    return pl.pallas_call(
        functools.partial(norm_back_body, len(bases), steps),
        grid_spec=pltpu.PrefetchScalarGridSpec(
            num_scalar_prefetch=1,
            grid=(steps,),
            in_specs=[
                row,
                row,
                pl.BlockSpec((tile, width), lambda i, p: (p[0] * steps + i, 0)),
                whole,
            ]
            + base_specs,
            out_specs=out_specs,
        ),
        out_shape=shapes,
        compiler_params=params(),
        cost_estimate=LIGHT,
    )(place.reshape(1).astype(jnp.int32), source, arrived, part, gain, *bases)


def mix_back_body(count, place_ref, *refs):
    lows, weight_ref, out_refs = refs[:count], refs[count], refs[count + 1 :]
    total = None
    shards, _, _, shard = weight_ref.shape
    for index in range(shards):
        span = slice(index * shard, (index + 1) * shard)
        left = jnp.concatenate([low[:, span] for low in lows], axis=0)
        product = lax.dot_general(left, weight_ref[index, 0], NT, preferred_element_type=FULL)
        total = product if total is None else total + product
    value = total.astype(LOW)
    for step, out in enumerate(out_refs):

        @pl.when(pl.program_id(0) == step)
        def _():
            out[...] = value


def mix_back(targets, lows, weight):
    rows, width = lows[0].shape
    shards, count, cols, shard = weight.shape
    total = rows * len(lows)
    spec = pl.BlockSpec((total, cols), lambda i, p: (0, 0))
    return pl.pallas_call(
        functools.partial(mix_back_body, len(lows)),
        grid_spec=pltpu.PrefetchScalarGridSpec(
            num_scalar_prefetch=1,
            grid=(count,),
            in_specs=[pl.BlockSpec((rows, width), lambda i, p: (0, 0))] * len(lows)
            + [pl.BlockSpec((shards, 1, cols, shard), lambda i, p: (0, p[i], 0, 0))],
            out_specs=[spec] * count,
        ),
        out_shape=[jax.ShapeDtypeStruct((total, cols), LOW)] * count,
        compiler_params=params(),
        cost_estimate=LIGHT,
    )(targets, *lows, weight)


def project_back_body(place_ref, back_ref, weight_ref, out_ref):
    total = None
    for part in range(3):
        product = lax.dot_general(back_ref[part], weight_ref[part], NT, preferred_element_type=FULL)
        total = product if total is None else total + product
    out_ref[...] = total.astype(LOW)


def project_back(place, back, weight, rows):
    _, width, cols = weight.shape
    tile = min(512, width)
    return pl.pallas_call(
        project_back_body,
        grid_spec=pltpu.PrefetchScalarGridSpec(
            num_scalar_prefetch=1,
            grid=(width // tile,),
            in_specs=[
                pl.BlockSpec((3, rows, cols), lambda i, p: (0, p[0], 0)),
                pl.BlockSpec((3, tile, cols), lambda i, p: (0, i, 0)),
            ],
            out_specs=pl.BlockSpec((rows, tile), lambda i, p: (0, i)),
        ),
        out_shape=jax.ShapeDtypeStruct((rows, width), LOW),
        compiler_params=params(),
        cost_estimate=LIGHT,
    )(place.reshape(1), back, weight)


def adam_step(weight, grad, first, second, factor, rate, decay):
    clipped = grad * factor
    first_new = BETA_ONE * first + (1.0 - BETA_ONE) * clipped
    second_new = BETA_TWO * second + (1.0 - BETA_TWO) * clipped * clipped
    first_hat = first_new / (1.0 - BETA_ONE**STEP)
    second_hat = second_new / (1.0 - BETA_TWO**STEP)
    weight_new = weight - rate * (first_hat / (jnp.sqrt(second_hat) + ADAM_EPS) + decay * weight)
    return (weight_new, weight_new.astype(LOW), first_new, second_new)


def adam_body(rates, factor_ref, *refs):
    count = len(rates)
    factor = factor_ref[0]
    for index, rate in enumerate(rates):
        weight, grad, first, second = refs[4 * index : 4 * index + 4]
        outs = refs[4 * count + 4 * index : 4 * count + 4 * index + 4]
        if len(weight.shape) == 3:
            cols = weight.shape[2]
            for part in range(weight.shape[0]):
                piece = grad[:, part * cols : (part + 1) * cols].astype(FULL)
                new = adam_step(weight[part], piece, first[part], second[part], factor, rate, DECAY_RATE)
                for out, value in zip(outs, new):
                    out[part] = value
        else:
            new = adam_step(weight[...], grad[...].astype(FULL), first[...], second[...], factor, rate, DECAY_RATE)
            for out, value in zip(outs, new):
                out[...] = value


def adam_all(factor, groups, rates):
    steps = 8
    for weight, _, _, _ in groups:
        steps = min(steps, weight.shape[-2] // 16)
    in_specs, out_specs, shapes, operands = [], [], [], []
    for weight, grad, first, second in groups:
        rows, cols = weight.shape[-2] // steps, weight.shape[-1]
        if weight.ndim == 3:
            spec = pl.BlockSpec((weight.shape[0], rows, cols), lambda i, f: (0, i, 0))
        else:
            spec = pl.BlockSpec((rows, cols), lambda i, f: (i, 0))
        grad_spec = pl.BlockSpec((rows, grad.shape[1]), lambda i, f: (i, 0))
        in_specs += [spec, grad_spec, spec, spec]
        out_specs += [spec] * 4
        operands += [weight, grad, first, second]
        for kind in (FULL, LOW, FULL, FULL):
            shapes.append(jax.ShapeDtypeStruct(weight.shape, kind))
    out = pl.pallas_call(
        functools.partial(adam_body, rates),
        grid_spec=pltpu.PrefetchScalarGridSpec(
            num_scalar_prefetch=1, grid=(steps,), in_specs=in_specs, out_specs=out_specs
        ),
        out_shape=shapes,
        compiler_params=params(60 * 1024 * 1024),
        cost_estimate=LIGHT,
    )(factor.reshape(1), *operands)
    return [tuple(out[4 * index : 4 * index + 4]) for index in range(len(groups))]


def lay_body(spots, me_ref, *refs):
    count = len(spots)
    out_ref = refs[count]
    for piece, spot in zip(refs, spots):
        if isinstance(spot, tuple):
            rows = piece.shape[0]
            out_ref[me_ref[0] ^ spot[0], spot[1] * rows : (spot[1] + 1) * rows] = piece[...]
        else:
            out_ref[lax.rem(me_ref[0] + count - spot, count)] = piece[...]


def lay(me, pieces, spots):
    rows, width = pieces[0].shape
    if isinstance(spots[0], tuple):
        shape = (len(pieces) // 2, 2 * rows, width)
    else:
        shape = (len(pieces), rows, width)
    return pl.pallas_call(
        functools.partial(lay_body, spots),
        in_specs=[pl.BlockSpec(memory_space=pltpu.SMEM)] + [pl.BlockSpec(memory_space=pltpu.VMEM)] * len(pieces),
        out_specs=pl.BlockSpec(memory_space=pltpu.VMEM),
        out_shape=jax.ShapeDtypeStruct(shape, LOW),
        compiler_params=params(),
        cost_estimate=LIGHT,
    )(me.reshape(1).astype(jnp.int32), *pieces)


def lay_cores_body(core_ref, mine_ref, other_ref, out_ref):
    mine, other = mine_ref[...], other_ref[...]
    out_ref[0, 0] = jnp.where(core_ref[0] == 0, mine, other)[0]
    out_ref[0, 1] = jnp.where(core_ref[0] == 0, other, mine)[0]


def lay_cores(core, mine, other):
    chips, rows, width = mine.shape
    spec = pl.BlockSpec((1, rows, width), lambda i, c: (i, 0, 0))
    return pl.pallas_call(
        lay_cores_body,
        grid_spec=pltpu.PrefetchScalarGridSpec(
            num_scalar_prefetch=1,
            grid=(chips,),
            in_specs=[spec, spec],
            out_specs=pl.BlockSpec((1, 2, rows, width), lambda i, c: (i, 0, 0, 0)),
        ),
        out_shape=jax.ShapeDtypeStruct((chips, 2, rows, width), LOW),
        compiler_params=params(),
        cost_estimate=LIGHT,
    )(core, mine, other)


def squares(value):
    wide = value.astype(FULL)
    return jnp.sum(wide * wide)


def after(value, *others):
    if not others:
        return value
    return lax.optimization_barrier((value, *others))[0]


def per_device(
    chips,
    cores,
    bkts,
    block_in,
    cotangent,
    buckets,
    qkv_weight,
    qkv_first,
    qkv_second,
    out_weight,
    out_first,
    out_second,
    up_weight,
    up_first,
    up_second,
    down_weight,
    down_first,
    down_second,
    norm_gains,
    gains_first,
    gains_second,
):
    toks = chips * cores
    tok = ("chip", "core")
    group = lax.axis_index("bkt")
    core = lax.axis_index("core")
    chip = lax.axis_index("chip")
    core_id = core.reshape(1).astype(jnp.int32)
    rows, width = block_in.shape
    half = rows // 2
    length = rows * bkts
    ring = [(i, (i + 1) % bkts) for i in range(bkts)]

    last = []

    def at(value, *others):
        return after(value, *last, *others)

    def did(value):
        last[:] = [value]
        return value

    def wait(value):
        return did(after(value, *last))

    def pass_on(name, value, *others):
        with jax.named_scope(name):
            return lax.ppermute(at(value, *others), "bkt", ring)

    def owner(step):
        return lax.rem(group - step + bkts, bkts)

    places = jnp.stack([owner(step) for step in range(bkts)]).astype(jnp.int32)

    def rows_of(value, step):
        size = value.shape[0] // bkts
        return lax.dynamic_slice_in_dim(value, owner(step) * size, size, 0)

    def add(arrived, value, step):
        return did(ring_add(owner(step), at(arrived), value, LOW))

    def add_final(arrived, value):
        return did(ring_add(owner(0), at(arrived), value, FULL))

    def swap(name, values):
        with jax.named_scope(name + "_swap"):
            return [lax.ppermute(at(value), "core", [(0, 1), (1, 0)]) for value in values]

    def core_add(kept, arrived):
        return did(core_add_kernel(at(kept), arrived))

    def chip_sum(value):
        value = value.reshape(chips * value.shape[1], *value.shape[2:])
        return lax.psum_scatter(value, "chip", scatter_dimension=0, tiled=True)

    by_bits = chips & (chips - 1) == 0

    qkv_full = lax.all_gather(did(qkv_weight.astype(LOW)), tok, axis=1, tiled=True)
    x_held = [block_in, pass_on("x1", block_in)]
    (out_low,) = round_low(at(out_weight), 1)
    did(out_low)
    cols = qkv_weight.shape[2]
    lower_a = did(pack_half(0, at(cotangent), cols))
    lower_b = [did(pack_half(1, at(cotangent), cols))]
    x_held[1] = wait(x_held[1])
    x_held.append(pass_on("x2", x_held[1]))
    out_held = [out_low, pass_on("out1", out_low)]
    (up_low,) = round_low(at(up_weight), 1)
    up_full = lax.all_gather(did(up_low), tok, axis=0, tiled=True)
    gain_width = norm_gains.shape[1]
    gain_line = jnp.zeros((toks, 2, gain_width), FULL)
    gain_line = lax.dynamic_update_slice(
        gain_line, norm_gains.astype(LOW).astype(FULL)[None], (lax.axis_index(tok), 0, 0)
    )
    if by_bits:
        for axis, size in (("core", cores), ("chip", chips)):
            for bit in range(size.bit_length() - 1):
                perm = [(i, i ^ (1 << bit)) for i in range(size)]
                with jax.named_scope("gains"):
                    gain_line = did(gain_line + lax.ppermute(at(gain_line), axis, perm))
    else:
        gain_line = did(lax.psum(at(gain_line), tok))
    gain_float = gain_line.transpose(1, 0, 2).reshape(2, width)
    cosine, sine = rotary_tables(length)
    for step in range(3, bkts):
        x_held[-1] = wait(x_held[-1])
        out_held[-1] = wait(out_held[-1])
        x_held.append(pass_on("x" + str(step), x_held[-1], cosine, sine))
        out_held.append(pass_on("out" + str(step - 1), out_held[-1]))

    carried = None
    for step in range(bkts - 1):
        carried = project(
            owner(step).reshape(1), at(x_held[step]), gain_float[0:1], qkv_full, cosine, sine, carried
        )
        did(carried[0])
    x_held[-1] = wait(x_held[-1])
    out_held[-1] = wait(out_held[-1])
    out_held.append(pass_on("out" + str(bkts - 1), out_held[-1]))
    normed_one, qkv, seq_in = project(
        owner(bkts - 1).reshape(1), at(x_held[-1]), gain_float[0:1], qkv_full, cosine, sine, carried
    )
    did(normed_one)
    out_held[-1] = wait(out_held[-1])
    out_depth, out_width = out_weight.shape
    lower_b.append(pass_on("cotangent_b1", lower_b[0]))
    out_line = did(lay(group, [at(out_held[0])] + out_held[1:], list(range(bkts))))
    out_full = lax.all_gather(after(out_line, up_full), tok, axis=0, tiled=False)
    (down_low,) = round_low(at(down_weight), 1)
    down_full = lax.all_gather(did(down_low), tok, axis=1, tiled=True)
    seq_in = seq_in.reshape(bkts, rows, width)

    upper = length // 2
    slab, log_a = attend(0, bkts, at(qkv), lower_a)
    slabs = [[did(slab)], []]

    def next_slab(part):
        held = slabs[part]
        if len(held) > 1:
            held[-1] = wait(held[-1])
        value = held[-1]
        if part == 1 and len(held) == bkts - 1:
            value = value[:upper]
        held.append(pass_on("slab" + "ab"[part] + str(len(held)), value))

    lower_b[1] = wait(lower_b[1])
    next_slab(0)
    slab, log_b = attend(1, bkts, at(qkv), lower_b[1])
    slabs[1].append(did(slab))
    logs = [log_a, log_b]
    for step in range(2, bkts):
        next_slab(0)
    slabs[0][-1] = wait(slabs[0][-1])
    for step in range(1, bkts - 2):
        next_slab(1)

    live = (buckets >= group).astype(FULL)
    acc = did(mix_first(0, places, at(seq_in), slabs[0][:-1], out_full))
    normed_a, middle_a, mixed_a = mix_last(places, acc, gain_float[1:2], slabs[0], out_full)
    did(normed_a)
    next_slab(1)
    hidden_a, inner_a, low_a = hidden_units(
        places, live, at(normed_a), up_full, down_full, [(slab, 1) for slab in slabs[0]]
    )
    did(inner_a)
    next_slab(1)
    back_a = did(product(at(inner_a), up_full, True))
    sum_a = did(rows_of(back_a, 1))
    arrived_a = pass_on("sum_a1", sum_a)
    acc = did(mix_first(1, places, at(seq_in), slabs[1][:-1], out_full))
    slabs[1][-1] = wait(slabs[1][-1])
    normed_b, middle_b, mixed_b = mix_last(places, at(acc), gain_float[1:2], slabs[1], out_full)
    did(normed_b)
    sum_a = add(arrived_a, back_a, 2)
    arrived_a = pass_on("sum_a2", sum_a)

    hidden_b, inner_b, low_b = hidden_units(
        places,
        live,
        at(normed_b),
        up_full,
        down_full,
        [(lower_b[0], 0), (lower_b[1], 0)] + [(slab, 1) for slab in slabs[1][1:-1]],
    )
    did(inner_b)
    sum_a = add(arrived_a, back_a, 3)
    arrived_a = pass_on("sum_a3", sum_a)
    back_b = did(product(at(inner_b), up_full, True))
    sum_b = did(rows_of(at(back_b), 1))
    arrived_b = pass_on("sum_b1", sum_b)
    up_kept, up_sent = weight_grad(core_id, [normed_a, normed_b], [at(inner_a), inner_b], chips, 0)
    did(up_kept)

    first = jnp.zeros((), jnp.int32)
    targets = jnp.stack([lax.rem(group + step, bkts) for step in range(bkts)]).astype(jnp.int32)

    def middle_back(part, middle, arrived, back):
        grad, gain_sum, low = norm_back(
            owner(0), middle, at(arrived), back, gain_float[1:2], [cotangent], part * half, True
        )
        did(low)
        return grad, low, gain_sum

    def exchange(found):
        with jax.named_scope("exchange"):
            for step in range(1, bkts):
                found[step] = lax.ppermute(
                    at(found[step]), "bkt", [(i, (i + step) % bkts) for i in range(bkts)]
                )

    arrived_a = wait(arrived_a)
    sum_b = add(arrived_b, back_b, 2)
    arrived_b = pass_on("sum_b2", sum_b)
    up_arrived = swap("up_grad", up_sent)
    grad_a, mid_low_a, gain_a = middle_back(0, middle_a, arrived_a, back_a)
    prod_b = did(product(at(hidden_b), down_full, False))
    sum_b = add(arrived_b, back_b, 3)
    up_core = core_add(up_kept, up_arrived)
    up_part = chip_sum(up_core)
    arrived_b = pass_on("sum_b3", sum_b)
    down_kept, down_sent = weight_grad(core_id, [hidden_a, hidden_b], [at(low_a), low_b], chips, 1)
    did(down_kept)
    grad_b, mid_low_b, gain_b = middle_back(1, middle_b, arrived_b, back_b)
    down_arrived = swap("down_grad", down_sent)
    pieces = list(mix_back(targets, [mid_low_a, at(mid_low_b)], out_full))
    did(pieces[0])
    down_core = core_add(down_kept, down_arrived)
    down_part = chip_sum(down_core)
    exchange(pieces)
    out_kept, out_sent = weight_grad(
        core_id, [at(mixed_a), mixed_b], [mid_low_a, mid_low_b], chips, 1
    )
    did(out_kept)
    prod_a = did(product(at(hidden_a), down_full, False))
    prods = [prod_a, prod_b]
    ffn = did(pair_add(owner(1), half, [at(prod_a), prod_b], None, None, LOW))
    pieces = pieces[:1] + [wait(piece) for piece in pieces[1:]]
    arrived_f = pass_on("ffn1", ffn)
    out_arrived = swap("out_grad", out_sent)

    back_project = did(attend_back(places, at(qkv), pieces, logs, cosine, sine))
    total = did(project_back(owner(1), at(back_project), qkv_full, rows))
    arrived_f = wait(arrived_f)
    out_core = core_add(out_kept, out_arrived)
    out_sum = chip_sum(out_core)
    arrived = pass_on("back1", total)
    up_squares = did(squares(at(up_part)))
    qkv_kept, qkv_sent = project_grad(core_id, normed_one, at(back_project), chips)
    did(qkv_kept)
    own = did(project_back(owner(2), at(back_project), qkv_full, rows))
    total = did(ring_add(first, at(arrived), own, LOW))
    arrived = pass_on("back2", total)
    qkv_arrived = swap("qkv_grad", qkv_sent)
    own = did(project_back(owner(3), at(back_project), qkv_full, rows))
    last_own = did(project_back(owner(0), at(back_project), qkv_full, rows))
    down_squares = did(squares(at(down_part)))
    total = did(ring_add(first, at(arrived), own, LOW))
    qkv_core = core_add(qkv_kept, qkv_arrived)
    qkv_part = chip_sum(qkv_core)
    arrived = pass_on("back3", total)
    arrived_out = pass_on("out_sum1", rows_of(out_sum, 1))
    ffn = did(pair_add(owner(2), half, prods, at(arrived_f), None, LOW))
    block_in_grad, gain_one = norm_back(
        first, block_in, at(arrived), last_own, gain_float[0:1], [grad_a, grad_b], 0, False
    )
    did(gain_one)
    for step in range(2, bkts):
        out_part = add(arrived_out, out_sum, step)
        arrived_out = pass_on("out_sum" + str(step), out_part)
    out_part = add_final(arrived_out, out_sum)
    arrived_f = pass_on("ffn2", ffn)
    out_squares = did(squares(at(out_part)))
    gain_grad_one = gain_one[0]
    gain_grad_two = (gain_a + gain_b)[0]

    weight_squares = did(up_squares + down_squares + out_squares + squares(at(qkv_part)))
    packed = jnp.concatenate(
        [gain_grad_one, gain_grad_two, jnp.broadcast_to(weight_squares, (HD,))]
    )
    for axis, size in (("core", cores), ("chip", chips), ("bkt", bkts)):
        if size & (size - 1):
            packed = lax.psum(packed, axis)
        else:
            step = 1
            while step < size:
                packed = packed + lax.ppermute(packed, axis, [(i, i ^ step) for i in range(size)])
                if axis == "bkt" and step == 1:
                    ffn = pair_add(owner(3), half, prods, after(arrived_f, packed), None, LOW)
                step *= 2
    did(packed)
    arrived_f = pass_on("ffn3", ffn)
    gain_total = packed[: 2 * width].reshape(2, width)
    grad_norm = jnp.sqrt(packed[2 * width] + jnp.sum(gain_total * gain_total))
    factor = jnp.minimum(1.0, CLIP_NORM / grad_norm)
    gain_part = lax.dynamic_slice_in_dim(gain_total, lax.axis_index(tok) * gain_width, gain_width, 1)
    updated = adam_all(
        factor,
        [
            (qkv_weight, qkv_part, qkv_first, qkv_second),
            (out_weight, out_part, out_first, out_second),
            (up_weight, up_part, up_first, up_second),
            (down_weight, down_part, down_first, down_second),
        ],
        (D ** (-0.5), (H * HD // 16) ** (-0.5), D ** (-0.5), FF ** (-0.5)),
    )
    block_out = pair_add(
        owner(0), half, prods, after(arrived_f, updated[0][0]), [middle_a, middle_b], FULL
    )
    gain_out = adam_step(norm_gains, gain_part, gains_first, gains_second, factor, GAIN_RATE, 0.0)
    return (block_out, block_in_grad, grad_norm, *[value for new in updated for value in new], *gain_out)


def solution(mesh):
    toks, bkts = mesh.shape["tok"], mesh.shape["bkt"]
    cores = 2
    chips = toks // cores
    tok = ("chip", "core")
    rows = P(("chip", "core", "bkt"), None)
    qkv = P(None, tok, "bkt")
    tall = P("bkt", tok)
    wide = P(tok, "bkt")
    gains = P(None, tok)
    return jax.shard_map(
        functools.partial(per_device, chips, cores, bkts),
        mesh=Mesh(mesh.devices.reshape(chips, cores, bkts), ("chip", "core", "bkt")),
        in_specs=(rows, rows, P(tok), *[qkv] * 3, *[tall] * 3, *[wide] * 3, *[tall] * 3, *[gains] * 3),
        out_specs=(rows, rows, P(), *[qkv] * 4, *[tall] * 4, *[wide] * 4, *[tall] * 4, *[gains] * 4),
        check_vma=False,
    )
```
